256 devices in a mesh: fsdp: 64 (over x, y_lo, z), rep: 4 (over y_hi, core).
Axes of the slice: x: 4, y: 4 (y_hi: 2, y_lo: 2; y = y_hi * 2 + y_lo), z: 8, core: 2. Of those that a mesh axis runs over, the one named last changes fastest.
Arguments:
- master: float32 [64, 256, 2880], P(None, 'rep', 'fsdp'), may hold values from -0.125 to 0.125
- placement: int32 [64], replicated, may hold values from 0 to 63, each once
- resident_gate_up: bfloat16 [64, 2880, 512], P('fsdp'), may hold values from -0.109375 to 0.109375
- resident_down: bfloat16 [64, 256, 2880], P('fsdp'), may hold values from -0.125 to 0.125
- hidden: bfloat16 [4, 256, 2880], P('rep'), may hold values from -6 to 6
- routes: int32 [4, 256, 4], P('rep'), may hold values from 0 to 7, all different within a row; in each aligned block of 4 rows (0 to 3, 4 to 7, ..., all dimensions but the last counted through in order) at most 3 rows name the same one
- norm_gain: bfloat16 [2880], replicated, may hold values from 0.099609375 to 1.8984375
- router: bfloat16 [2880, 8], P('rep'), may hold values from -0.21875 to 0.21875
Outputs:
- refreshed: bfloat16 [64, 256, 2880], P('fsdp')
- decoded: bfloat16 [4, 256, 2880], P('rep', 'fsdp')
The draws below stay inside these ranges and needn't reach their ends.
Inputs may be any that keep to these rules, and one draw needn't show every extreme that they name: `placement`: each slot has exactly one owner. `routes`: the 4 experts of a token differ; in each aligned block of 4 tokens of a replica group no expert is chosen by more than 3 tokens, and in some block one expert is chosen by exactly 3.
All inputs are finite; a program needn't handle non-finite values.
Results may differ from the reference program's by a relative error of at most 0.0056.
Values may be sent and summed in bfloat16 or wider, within the bound.
No kernel may reach another device: no remote copies, remote signals or barrier semaphores. Data moves between devices by JAX's collectives and lax.ppermute only.
A program may use at most 64 MiB of HBM per device.

```python
import math
import jax
import jax.numpy as jnp
import numpy as np
from jax import lax

D = 2880
FF = 2048
EXPERTS = 8
TOPK = 4
BLOCK = 32
TOK_REP = 256
HID_DEV = 256
T_OWN = 4
CAP = 3
N_FSDP = 64
N_REP = 4


def level_of(own_key, extent, pieces, smallest, largest):
    gain, own = 1.0, jax.random.fold_in(own_key, 6)
    for axis_at, blocks in pieces:
        draws = jnp.exp(jax.random.uniform(jax.random.fold_in(own, axis_at), (blocks,), jnp.float32, smallest / len(pieces), largest / len(pieces)))
        gain = gain * jnp.repeat(draws, extent[axis_at] // blocks).reshape([-1 if axis == axis_at else 1 for axis in range(len(extent))])
    return gain


def deal_out(own_key, own, number, rows, number_of, top, limit, lean):
    ranking = jax.random.permutation(own_key, number_of)
    packed, usual = shares(number_of, rows * top, limit, lean, True), shares(number_of, rows * top, limit, lean, False)
    places = jnp.arange(number_of)

    def named(lengths, turn):
        used = int((lengths > 0).sum())
        fixed = max(1, used // 4)
        shifted = fixed + (places - fixed + turn * (used - fixed)) % max(1, number_of - fixed)
        return jnp.zeros((number_of,), jnp.int32).at[ranking[jnp.where(places < fixed, places, shifted)]].set(jnp.asarray(lengths, jnp.int32))

    lengths = jnp.where(number % 4 == 0, named(packed, number // 4), named(usual, number - number // 4 - 1))
    mixed = jax.random.permutation(jax.random.fold_in(own, 3), number_of)
    giver, taker = mixed[0:number_of // 2 * 2:2], mixed[1:number_of // 2 * 2:2]
    margin = jnp.minimum(lengths[giver] - 1, limit - lengths[taker]) // 2
    margin = jnp.where((giver == ranking[0]) | (taker == ranking[0]) | (lengths[taker] == 0), 0, jnp.maximum(margin, 0))
    shifted = jax.random.randint(jax.random.fold_in(own, 4), (number_of // 2,), 0, 1 << 20) % (margin + 1)
    lengths = lengths.at[giver].add(-shifted).at[taker].add(shifted)
    labels = jnp.searchsorted(jnp.cumsum(lengths), jnp.arange(rows * top), side="right").astype(jnp.int32)
    grid = labels.reshape(top, rows).T
    grid = grid[jax.random.permutation(jax.random.fold_in(own, 1), rows)]
    turn = jax.random.randint(jax.random.fold_in(own, 2), (rows, 1), 0, top)
    return jnp.take_along_axis(grid, (jnp.arange(top)[None, :] + turn) % top, axis=1)


def shares(number_of, total, limit, slope, full):
    portions = [(1 << 20) // math.isqrt(standing ** slope) + 1 for standing in range(1, number_of + 1)]
    largest = limit if full else min(limit, max(-(-total // number_of), total * portions[0] // sum(portions)))
    least = 1 if total - largest >= number_of - 1 else 0
    holding, surplus = [largest] + [least] * (number_of - 1), total - largest - least * (number_of - 1)
    while surplus > 0:
        candidates = [i for i in range(1, number_of) if holding[i] < largest] or [i for i in range(1, number_of) if holding[i] < limit]
        pool, left = sum([portions[i] for i in candidates]), surplus
        for i in candidates:
            more = min(limit - holding[i], max(1, left * portions[i] // pool), surplus)
            holding[i] = holding[i] + more
            surplus = surplus - more
    return np.array(holding)


def scatter_about(key, dims, spread, bound, shards=(), held_as=jnp.bfloat16):
    result = jax.random.normal(key, dims, jnp.float32) * spread
    if len(shards) > 0:
        result = level_of(key, dims, shards, -0.22, 0.18) * result
    return jnp.clip(result, min=-bound, max=bound).astype(held_as)


def setup_inputs(seed: int = 0) -> dict:
    streams_of = jax.random.split(jax.random.key(seed), 9)
    master = scatter_about(streams_of[0], (N_FSDP, HID_DEV, D), FF ** -0.5, 0.125, ((1, 4), (2, 64)), jnp.float32)
    placement = jax.random.permutation(streams_of[1], N_FSDP).astype(jnp.int32)
    resident_gate_up = scatter_about(streams_of[2], (N_FSDP, D, 2 * HID_DEV), D ** -0.5, 0.109375, ((0, 64),))
    resident_down = scatter_about(streams_of[3], (N_FSDP, HID_DEV, D), FF ** -0.5, 0.125, ((0, 64),))
    hidden = scatter_about(streams_of[4], (N_REP, TOK_REP, D), 1.0, 6.0, ((0, 4),))
    routes_keys = jax.random.split(jax.random.fold_in(streams_of[5], 1), N_REP * TOK_REP // T_OWN)
    routes_turns = jax.random.permutation(jax.random.fold_in(streams_of[5], 3), N_REP * TOK_REP // T_OWN)
    routes = jax.vmap(lambda own, number: deal_out(jax.random.fold_in(streams_of[5], 2), own, number, T_OWN, EXPERTS, TOPK, CAP, 1))(routes_keys, routes_turns).reshape((N_REP, TOK_REP, TOPK))
    norm_gain = jnp.clip(1.0 + 0.18 * jax.random.normal(streams_of[6], (D,), jnp.float32), 0.099609375, 1.8984375).astype(jnp.bfloat16)
    router = scatter_about(streams_of[7], (D, EXPERTS), (D // 4) ** -0.5, 0.21875, ((0, 4),))
    return {"master": master, "placement": placement, "resident_gate_up": resident_gate_up, "resident_down": resident_down, "hidden": hidden, "routes": routes, "norm_gain": norm_gain, "router": router}


lowest_power = -40
highest_power = 8

def owner_slots(placement):
    count = placement.shape[0]
    iota_owner = jnp.arange(count, dtype=jnp.int32)
    matches = placement[:, None] == iota_owner[None, :]
    return lax.optimization_barrier(jnp.sum(jnp.where(matches, iota_owner[:, None], 0), axis=0)).astype(jnp.int32)

def power_scales(amax):
    scale = jnp.full(amax.shape, 2.0 ** lowest_power, amax.dtype)
    inverse = jnp.full(amax.shape, 2.0 ** (-lowest_power), amax.dtype)
    for power in range(lowest_power, highest_power):
        above = amax > 6.0 * 2.0 ** power
        scale = jnp.where(above, scale * 2.0, scale)
        inverse = jnp.where(above, inverse * 0.5, inverse)
    return (scale, inverse)

def nearest_level(values):
    size = jnp.abs(values)
    level = jnp.where(size >= 0.25, 0.5, 0.0) + jnp.where(size >= 0.75, 0.5, 0.0) + jnp.where(size >= 1.25, 0.5, 0.0) + jnp.where(size >= 1.75, 0.5, 0.0) + jnp.where(size >= 2.5, 1.0, 0.0) + jnp.where(size >= 3.5, 1.0, 0.0) + jnp.where(size >= 5.0, 2.0, 0.0)
    return jnp.where(values < 0, -level, level)

def encode_decode(master):
    slots, slot_rows, columns = master.shape
    grouped = master.reshape(slots, slot_rows // BLOCK, BLOCK, columns)
    amax = lax.optimization_barrier(jnp.max(jnp.abs(grouped), axis=2))
    scale, inverse = power_scales(amax)
    block_scale = scale.astype(jnp.bfloat16)
    code_values = nearest_level(grouped * inverse[:, :, None, :]).astype(jnp.bfloat16)
    widened = code_values.astype(jnp.float32) * block_scale.astype(jnp.float32)[:, :, None, :]
    return widened.astype(jnp.bfloat16).reshape(slots, slot_rows, columns)

def reference(master, placement, resident_gate_up, resident_down, hidden, routes, norm_gain, router):
    owners = owner_slots(placement)
    refreshed = encode_decode(master)[owners]
    split_count = N_FSDP // EXPERTS
    hid_units = resident_down.shape[1]
    width = hidden.shape[2]

    def one_group(pair):
        tokens, chosen = pair
        widened = tokens.astype(jnp.float32)
        normed = (widened * lax.rsqrt(lax.optimization_barrier(jnp.mean(widened * widened, axis=-1, keepdims=True)) + 1e-05) * norm_gain.astype(jnp.float32)).astype(jnp.bfloat16)
        logits = jnp.dot(normed, router, preferred_element_type=jnp.float32)
        picked = jnp.take_along_axis(logits, chosen, axis=1)
        powered = jnp.exp(picked)
        probs = powered / lax.optimization_barrier(jnp.sum(powered, axis=1, keepdims=True))

        def add_owner(total, owner_index):
            expert = owners[owner_index] // split_count
            token_weight = lax.optimization_barrier(jnp.sum(probs * (chosen == expert).astype(jnp.float32), axis=1))
            projected = jnp.dot(normed, resident_gate_up[owner_index], preferred_element_type=jnp.float32)
            gate_part = projected[:, :hid_units]
            up_part = projected[:, hid_units:]
            activated = (token_weight[:, None] * gate_part * jax.nn.sigmoid(1.702 * gate_part) * (up_part + 1.0)).astype(jnp.bfloat16)
            return (total + jnp.dot(activated, resident_down[owner_index], preferred_element_type=jnp.float32), None)
        start_total = jnp.zeros((tokens.shape[0], width), jnp.float32)
        mixed, _ = lax.scan(add_owner, start_total, jnp.arange(N_FSDP, dtype=jnp.int32))
        return (widened + mixed).astype(jnp.bfloat16)
    decoded = lax.map(one_group, (hidden, routes))
    return (refreshed, decoded)
```

```python
import functools

import jax
import jax.numpy as jnp
from jax import lax
from jax.experimental import pallas as pl
from jax.experimental.pallas import tpu as pltpu
from jax.sharding import Mesh
from jax.sharding import PartitionSpec as P

D = 2880
SLOTS = 64
COLS = 45
HALF = 24
ROWS = 64
TOK = 256
HID = 256
CAP = 3
PLANE = 8
DEPTH = 8
PACKED = TOK // 4 * CAP

VMEM = pltpu.VMEM
SMEM = pltpu.SMEM
BF = jnp.bfloat16
F32 = jnp.float32

FSDP = ("x", "yl", "z")
REP = ("yh", "c")


def params(mib):
    return pltpu.CompilerParams(vmem_limit_bytes=mib * 2**20)


def nt(a, b):
    return lax.dot_general(a, b, (((1,), (1,)), ((), ())), preferred_element_type=F32)


def tn(a, b):
    return lax.dot_general(a, b, (((0,), (0,)), ((), ())), preferred_element_type=F32)


def nn(a, b):
    return lax.dot_general(a, b, (((1,), (0,)), ((), ())), preferred_element_type=F32)


def iota(shape, dim):
    return lax.broadcasted_iota(jnp.int32, shape, dim)


def invert(place_ref, slot_ref):
    def step(s, _):
        slot_ref[place_ref[s]] = s
        return 0

    lax.fori_loop(0, SLOTS, step, 0, unroll=8)


def encode_kernel(place_ref, master_ref, out_ref, slot_ref, held_ref):
    invert(place_ref, slot_ref)
    spread = (iota((128, 128), 0) == (iota((128, 128), 1) // 32) * 32 + 31).astype(F32).astype(BF)

    def encode(j, _):
        low = master_ref[j]
        high = master_ref[jnp.minimum(j + HALF, COLS - 1)]
        values = jnp.concatenate([low, high], axis=1)
        size = jnp.abs(values)
        top = size
        for shift in (1, 2, 4, 8, 16):
            top = jnp.maximum(top, pltpu.roll(top, shift, 1))
        top = jnp.maximum(top, 6.0 * 2.0**-40)
        lead = top * (2.0**23 + 1.0)
        lead = jnp.abs(lead - lead * (1.0 - 2.0**-24))
        scale = jnp.where(top > lead * 1.5, lead * 0.5, lead * 0.25)
        s = nn(scale.astype(BF), spread)
        out = jnp.where(size >= s * 0.25, s * 0.5, 0.0)
        out = jnp.where(size >= s * 0.75, s, out)
        out = jnp.where(size >= s * 1.25, s * 1.5, out)
        out = jnp.where(size >= s * 1.75, s * 2.0, out)
        out = jnp.where(size >= s * 2.5, s * 3.0, out)
        out = jnp.where(size >= s * 3.5, s * 4.0, out)
        out = jnp.where(size >= s * 5.0, s * 6.0, out)
        held_ref[pl.ds(pl.multiple_of(j * SLOTS, SLOTS), SLOTS), :] = jnp.where(values < 0, -out, out)
        return 0

    lax.fori_loop(0, HALF, encode, 0, unroll=2)

    def deal(o, _):
        out_ref[o] = held_ref[pl.ds(slot_ref[o], HALF, stride=SLOTS), :].astype(BF)
        return 0

    lax.fori_loop(0, SLOTS, deal, 0, unroll=8)


def encode(placement, master):
    return pl.pallas_call(
        encode_kernel,
        name="encode",
        out_shape=jax.ShapeDtypeStruct((SLOTS, HALF, 128), BF),
        in_specs=[pl.BlockSpec(memory_space=SMEM), pl.BlockSpec(memory_space=VMEM)],
        out_specs=pl.BlockSpec(memory_space=VMEM),
        scratch_shapes=[pltpu.SMEM((SLOTS,), jnp.int32), pltpu.VMEM((HALF * SLOTS, 128), F32)],
        compiler_params=params(24),
        cost_estimate=pl.CostEstimate(flops=10**9, bytes_accessed=4 * 10**6, transcendentals=0),
    )(placement, master)


GROUP = 16


def assemble_kernel(got_ref, out_ref, held_ref):
    low = iota((HALF, 128), 1) < ROWS
    for i in range(GROUP):
        for h in range(2):
            first = got_ref[2 * h, i].astype(F32)
            second = got_ref[2 * h + 1, i].astype(F32)
            upper = jnp.where(low, first, pltpu.roll(second, ROWS, 1))
            lower = jnp.where(low, pltpu.roll(first, ROWS, 1), second)
            lanes = slice(128 * h, 128 * h + 128)
            held_ref[COLS * i : COLS * i + HALF, lanes] = upper
            held_ref[COLS * i + HALF : COLS * (i + 1), lanes] = lower[: COLS - HALF]
    out_ref[...] = held_ref[...].astype(BF)


def assemble(got):
    rows = GROUP * COLS
    return pl.pallas_call(
        assemble_kernel,
        name="assemble",
        grid=(SLOTS // GROUP,),
        out_shape=jax.ShapeDtypeStruct((D, 4 * ROWS), BF),
        in_specs=[pl.BlockSpec((4, GROUP, HALF, 128), lambda g: (0, g, 0, 0))],
        out_specs=pl.BlockSpec((rows, 4 * ROWS), lambda g: (g, 0)),
        scratch_shapes=[pltpu.VMEM((rows, 4 * ROWS), F32)],
        compiler_params=params(24),
        cost_estimate=pl.CostEstimate(flops=10**9, bytes_accessed=4 * 10**6, transcendentals=0),
    )(got)


def expert_kernel(
    place_ref,
    hidden_ref,
    routes_ref,
    gain_ref,
    router_ref,
    gate_up_ref,
    down_ref,
    out_ref,
    rows_ref,
    merge_ref,
    slot_ref,
    normed_ref,
):
    invert(place_ref, slot_ref)
    plane = lax.axis_index("x") * 2 + lax.axis_index("yl")
    depth = lax.axis_index("z")
    owner = plane * DEPTH + depth
    mine = slot_ref[owner] // DEPTH

    total = jnp.zeros((1, TOK), F32)
    step = 576
    for at in range(0, D, step):
        part = hidden_ref[at : at + step, :].astype(F32)
        total = total + jnp.sum(part * part, axis=0, keepdims=True)
    factor = lax.rsqrt(total * (1.0 / D) + 1e-05)
    ones = jnp.ones((128, TOK), BF)
    for at in range(0, D, 128):
        size = min(128, D - at)
        gain = gain_ref[:, at : at + size].astype(F32)
        diagonal = jnp.where(
            iota((size, size), 0) == iota((size, size), 1), jnp.broadcast_to(gain, (size, size)), 0.0
        ).astype(BF)
        column = nn(diagonal, ones[:size])
        part = hidden_ref[at : at + size, :].astype(F32)
        normed_ref[at : at + size, :] = (part * factor * column).astype(BF)

    rep = lax.axis_index("yh") * 2 + lax.axis_index("c")
    logits = jnp.zeros((8, TOK), F32)
    for d in range(4):
        start = pl.multiple_of((rep ^ d) * 720, 720)
        logits = logits + nn(router_ref[d], normed_ref[pl.ds(start, 720), :])
    which = iota((8, TOK), 0)
    chosen = jnp.zeros((8, TOK), F32)
    for k in range(4):
        chosen = jnp.where(which == routes_ref[k : k + 1, :], 1.0, chosen)
    powered = jnp.where(chosen > 0, jnp.exp(logits), 0.0)
    weights = powered / jnp.sum(powered, axis=0, keepdims=True)
    weight = jnp.sum(jnp.where(which == mine, weights, 0.0), axis=0, keepdims=True)
    weight = jnp.transpose(jnp.broadcast_to(weight, (8, TOK)))[:, 0:1]

    earlier = (
        ((iota((TOK, TOK), 0) // 4) == (iota((TOK, TOK), 1) // 4))
        & (iota((TOK, TOK), 0) < iota((TOK, TOK), 1))
    ).astype(F32).astype(BF)
    rank = nn(chosen.astype(BF), earlier)
    turn = jnp.where(chosen > 0, rank, -1.0)
    my_turn = jnp.sum(jnp.where(which == mine, turn, 0.0), axis=0, keepdims=True)
    packed = iota((PACKED, TOK), 0)
    pack = (
        ((iota((PACKED, TOK), 1) // 4) == (packed // CAP))
        & (jnp.broadcast_to(my_turn, (PACKED, TOK)) == (packed % CAP).astype(F32))
    ).astype(F32).astype(BF)

    projected = tn(normed_ref[...], gate_up_ref[...])
    gate = projected[:, :HID]
    up = projected[:, HID:]
    activated = (weight * gate * jax.nn.sigmoid(1.702 * gate) * (up + 1.0)).astype(BF)
    activated = nn(pack, activated).astype(BF)
    for at in range(0, D, 640):
        size = min(640, D - at)
        out_ref[:, at : at + size] = nt(activated, down_ref[at : at + size, :]).astype(BF)

    own = (iota((8, TOK), 1) == iota((8, TOK), 0) + owner * 4).astype(F32).astype(BF)
    for at in range(0, D, 640):
        size = min(640, D - at)
        rows_ref[:, at : at + size] = nt(own, hidden_ref[at : at + size, :])[:4]

    pick = (iota((TOK, 128), 0) == iota((TOK, 128), 1) + plane * 32).astype(F32).astype(BF)
    turns = nn(turn.astype(BF), pick)
    per = 4 * DEPTH // 4 * CAP
    block = iota((per, 128), 0)
    parts = []
    for p in range(PLANE):
        expert = slot_ref[p * DEPTH + depth] // DEPTH
        theirs = jnp.sum(jnp.where(iota((8, 128), 0) == expert, turns, 0.0), axis=0, keepdims=True)
        parts.append(
            (
                ((iota((per, 128), 1) // 4) == (block // CAP))
                & (jnp.broadcast_to(theirs, (per, 128)) == (block % CAP).astype(F32))
            ).astype(F32)
        )
    merge_ref[...] = jnp.transpose(jnp.concatenate(parts, axis=0))[:32].astype(BF)


def expert_terms(placement, hidden, routes, gain, router, gate_up, down):
    return pl.pallas_call(
        expert_kernel,
        name="expert_terms",
        out_shape=(
            jax.ShapeDtypeStruct((PACKED, D), BF),
            jax.ShapeDtypeStruct((4, D), F32),
            jax.ShapeDtypeStruct((32, PACKED), BF),
        ),
        in_specs=[pl.BlockSpec(memory_space=SMEM)] + [pl.BlockSpec(memory_space=VMEM)] * 6,
        out_specs=(pl.BlockSpec(memory_space=VMEM),) * 3,
        scratch_shapes=[pltpu.SMEM((SLOTS,), jnp.int32), pltpu.VMEM((D, TOK), BF)],
        compiler_params=params(40),
        cost_estimate=pl.CostEstimate(flops=4 * 10**9, bytes_accessed=8 * 10**6, transcendentals=0),
    )(placement, hidden, routes, gain, router, gate_up, down)


def merge_kernel(merge_ref, got_ref, out_ref):
    for at in range(0, D, 640):
        size = min(640, D - at)
        part = nn(merge_ref[...], got_ref[:, at : at + size]).astype(BF)
        for z in range(DEPTH):
            out_ref[z, :, at : at + size] = part[4 * z : 4 * z + 4]


def merge_plane(merge, got):
    return pl.pallas_call(
        merge_kernel,
        name="merge_plane",
        out_shape=jax.ShapeDtypeStruct((DEPTH, 4, D), BF),
        in_specs=[pl.BlockSpec(memory_space=VMEM)] * 2,
        out_specs=pl.BlockSpec(memory_space=VMEM),
        compiler_params=params(16),
        cost_estimate=pl.CostEstimate(flops=10**8, bytes_accessed=10**6, transcendentals=0),
    )(merge, got)


def on_device(
    master, placement, resident_gate_up, resident_down, hidden, routes, norm_gain, router
):
    router_rows = router.T
    routers = [router_rows]
    for d in range(1, 4):
        pairs = [(r, r ^ d) for r in range(4)]
        routers.append(lax.ppermute(router_rows, REP, pairs))

    chunks = encode(placement, jnp.transpose(master, (2, 0, 1)))
    chunks = lax.all_to_all(chunks, FSDP, split_axis=0, concat_axis=0, tiled=True)
    chunks = lax.all_gather(chunks, REP, axis=0, tiled=False)

    terms, rows, merge = expert_terms(
        placement,
        hidden[0].T,
        routes[0].T,
        norm_gain[None],
        jnp.stack(routers),
        resident_gate_up[0],
        resident_down[0].T,
    )
    terms = lax.all_to_all(terms, ("x", "yl"), split_axis=0, concat_axis=0, tiled=True)
    terms = merge_plane(merge, terms)
    terms = lax.all_to_all(terms, "z", split_axis=0, concat_axis=0, tiled=True)
    decoded = (rows + jnp.sum(terms.astype(F32), axis=0)).astype(BF)
    refreshed = assemble(chunks).T
    return (refreshed[None], decoded[None])


def solution(mesh):
    cut = Mesh(mesh.devices.reshape(4, 2, 8, 2, 2), ("x", "yl", "z", "yh", "c"))
    placed = (
        P(None, REP, FSDP),
        P(),
        P(FSDP, None, None),
        P(FSDP, None, None),
        P(REP, None, None),
        P(REP, None, None),
        P(),
        P(REP, None),
    )
    return jax.shard_map(
        on_device,
        mesh=cut,
        in_specs=placed,
        out_specs=(P(FSDP, None, None), P(REP, FSDP, None)),
        check_vma=False,
    )
```

```python
import jax
import jax.numpy as jnp
from jax import lax
from jax.experimental import pallas as pl
from jax.experimental.pallas import tpu as pltpu
from jax.sharding import Mesh
from jax.sharding import PartitionSpec as P

D = 2880
SLOTS = 64
COLS = 45
HALF = 24
ROWS = 64
TOK = 256
HID = 256
CAP = 3
PLANE = 8
DEPTH = 8
PACKED = TOK // 4 * CAP

VMEM = pltpu.VMEM
SMEM = pltpu.SMEM
BF = jnp.bfloat16
F32 = jnp.float32

FSDP = ("x", "yl", "z")
REP = ("yh", "c")


def params(mib):
    return pltpu.CompilerParams(vmem_limit_bytes=mib * 2**20)


def nt(a, b):
    return lax.dot_general(a, b, (((1,), (1,)), ((), ())), preferred_element_type=F32)


def tn(a, b):
    return lax.dot_general(a, b, (((0,), (0,)), ((), ())), preferred_element_type=F32)


def nn(a, b):
    return lax.dot_general(a, b, (((1,), (0,)), ((), ())), preferred_element_type=F32)


def iota(shape, dim):
    return lax.broadcasted_iota(jnp.int32, shape, dim)


def invert(place_ref, slot_ref):
    def step(s, _):
        slot_ref[place_ref[s]] = s
        return 0

    lax.fori_loop(0, SLOTS, step, 0, unroll=8)


PAIRS = 12


def round_blocks(values, spread):
    size = jnp.abs(values)
    top = size
    for shift in (1, 2, 4, 8, 16):
        top = jnp.maximum(top, pltpu.roll(top, shift, 1))
    top = jnp.maximum(top, 6.0 * 2.0**-40)
    lead = top * (2.0**23 + 1.0)
    lead = jnp.abs(lead - lead * (1.0 - 2.0**-24))
    scale = jnp.where(top > lead * 1.5, lead * 0.5, lead * 0.25)
    s = nn(scale.astype(BF), spread)
    out = jnp.where(size >= s * 0.25, s * 0.5, 0.0)
    out = jnp.where(size >= s * 0.75, s, out)
    out = jnp.where(size >= s * 1.25, s * 1.5, out)
    out = jnp.where(size >= s * 1.75, s * 2.0, out)
    out = jnp.where(size >= s * 2.5, s * 3.0, out)
    out = jnp.where(size >= s * 3.5, s * 4.0, out)
    out = jnp.where(size >= s * 5.0, s * 6.0, out)
    return jnp.where(values < 0, -out, out)


def encode_kernel(place_ref, master_ref, out_ref, slot_ref, held_ref, raw_ref, sems):
    copies = []
    for g in range(HALF // PAIRS):
        at = g * PAIRS
        wide = min(PAIRS, COLS - HALF - at)
        for n, (start, size) in enumerate(((at, PAIRS), (HALF + at, wide))):
            part = pl.ds(start, size)
            copy = pltpu.make_async_copy(master_ref.at[part], raw_ref.at[part], sems.at[2 * g + n])
            copy.start()
            copies.append(copy)
    invert(place_ref, slot_ref)
    spread = (iota((128, 128), 0) == (iota((128, 128), 1) // 32) * 32 + 31).astype(F32).astype(BF)
    for g in range(HALF // PAIRS):
        at = g * PAIRS
        wide = min(PAIRS, COLS - HALF - at)
        copies[2 * g].wait()
        copies[2 * g + 1].wait()
        low = raw_ref[at : at + PAIRS]
        high = raw_ref[HALF + at : HALF + at + wide]
        if wide < PAIRS:
            high = jnp.concatenate([high, low[wide:]], axis=0)
        low = low.reshape(PAIRS * SLOTS, ROWS)
        high = high.reshape(PAIRS * SLOTS, ROWS)
        values = jnp.concatenate([low, high], axis=1)
        held_ref[at * SLOTS : (at + PAIRS) * SLOTS, :] = round_blocks(values, spread)

    def deal(o, _):
        out_ref[o] = held_ref[pl.ds(slot_ref[o], HALF, stride=SLOTS), :].astype(BF)
        return 0

    lax.fori_loop(0, SLOTS, deal, 0, unroll=8)


def encode(placement, master):
    return pl.pallas_call(
        encode_kernel,
        name="encode",
        out_shape=jax.ShapeDtypeStruct((SLOTS, HALF, 128), BF),
        in_specs=[pl.BlockSpec(memory_space=SMEM), pl.BlockSpec(memory_space=pl.ANY)],
        out_specs=pl.BlockSpec(memory_space=VMEM),
        scratch_shapes=[
            pltpu.SMEM((SLOTS,), jnp.int32),
            VMEM((HALF * SLOTS, 128), F32),
            VMEM((COLS, SLOTS, ROWS), F32),
            pltpu.SemaphoreType.DMA((2 * HALF // PAIRS,)),
        ],
        compiler_params=params(60),
        cost_estimate=pl.CostEstimate(flops=10**9, bytes_accessed=4 * 10**6, transcendentals=0),
    )(placement, master)


GROUP = 16


def assemble_kernel(own_ref, across_ref, core_ref, both_ref, out_ref, held_ref):
    low = iota((HALF, 128), 1) < ROWS
    half = lax.axis_index("yh")
    core = lax.axis_index("c")
    for i in range(GROUP):
        here = (own_ref[i].astype(F32), core_ref[i].astype(F32))
        there = (across_ref[i].astype(F32), both_ref[i].astype(F32))
        for h in range(2):
            mine, other = (jnp.where(half == h, a, b) for a, b in zip(here, there))
            first = jnp.where(core == 0, mine, other)
            second = jnp.where(core == 0, other, mine)
            upper = jnp.where(low, first, pltpu.roll(second, ROWS, 1))
            lower = jnp.where(low, pltpu.roll(first, ROWS, 1), second)
            lanes = slice(128 * h, 128 * h + 128)
            held_ref[COLS * i : COLS * i + HALF, lanes] = upper
            held_ref[COLS * i + HALF : COLS * (i + 1), lanes] = lower[: COLS - HALF]
    out_ref[...] = held_ref[...].astype(BF)


def assemble(own, across, core, both):
    rows = GROUP * COLS
    return pl.pallas_call(
        assemble_kernel,
        name="assemble",
        grid=(SLOTS // GROUP,),
        out_shape=jax.ShapeDtypeStruct((D, 4 * ROWS), BF),
        in_specs=[pl.BlockSpec((GROUP, HALF, 128), lambda g: (g, 0, 0))] * 4,
        out_specs=pl.BlockSpec((rows, 4 * ROWS), lambda g: (g, 0)),
        scratch_shapes=[VMEM((rows, 4 * ROWS), F32)],
        compiler_params=params(24),
        cost_estimate=pl.CostEstimate(flops=10**9, bytes_accessed=4 * 10**6, transcendentals=0),
    )(own, across, core, both)


def expert_kernel(
    place_ref,
    hidden_ref,
    routes_ref,
    gain_ref,
    router_ref,
    gate_up_ref,
    down_ref,
    out_ref,
    rows_ref,
    merge_ref,
    slot_ref,
    normed_ref,
):
    invert(place_ref, slot_ref)
    plane = lax.axis_index("x") * 2 + lax.axis_index("yl")
    depth = lax.axis_index("z")
    owner = plane * DEPTH + depth
    mine = slot_ref[owner] // DEPTH

    total = jnp.zeros((1, TOK), F32)
    step = 576
    for at in range(0, D, step):
        part = hidden_ref[at : at + step, :].astype(F32)
        total = total + jnp.sum(part * part, axis=0, keepdims=True)
    factor = lax.rsqrt(total * (1.0 / D) + 1e-05)
    ones = jnp.ones((128, TOK), BF)
    for at in range(0, D, 128):
        size = min(128, D - at)
        gain = gain_ref[:, at : at + size].astype(F32)
        diagonal = jnp.where(
            iota((size, size), 0) == iota((size, size), 1), jnp.broadcast_to(gain, (size, size)), 0.0
        ).astype(BF)
        column = nn(diagonal, ones[:size])
        part = hidden_ref[at : at + size, :].astype(F32)
        normed_ref[at : at + size, :] = (part * factor * column).astype(BF)

    rep = lax.axis_index("yh") * 2 + lax.axis_index("c")
    logits = jnp.zeros((8, TOK), F32)
    for d in range(4):
        start = pl.multiple_of((rep ^ d) * 720, 720)
        logits = logits + nn(router_ref[d], normed_ref[pl.ds(start, 720), :])
    which = iota((8, TOK), 0)
    chosen = jnp.zeros((8, TOK), F32)
    for k in range(4):
        chosen = jnp.where(which == routes_ref[k : k + 1, :], 1.0, chosen)
    powered = jnp.where(chosen > 0, jnp.exp(logits), 0.0)
    weights = powered / jnp.sum(powered, axis=0, keepdims=True)
    weight = jnp.sum(jnp.where(which == mine, weights, 0.0), axis=0, keepdims=True)
    weight = jnp.transpose(jnp.broadcast_to(weight, (8, TOK)))[:, 0:1]

    earlier = (
        ((iota((TOK, TOK), 0) // 4) == (iota((TOK, TOK), 1) // 4))
        & (iota((TOK, TOK), 0) < iota((TOK, TOK), 1))
    ).astype(F32).astype(BF)
    rank = nn(chosen.astype(BF), earlier)
    turn = jnp.where(chosen > 0, rank, -1.0)
    my_turn = jnp.sum(jnp.where(which == mine, turn, 0.0), axis=0, keepdims=True)
    packed = iota((PACKED, TOK), 0)
    pack = (
        ((iota((PACKED, TOK), 1) // 4) == (packed // CAP))
        & (jnp.broadcast_to(my_turn, (PACKED, TOK)) == (packed % CAP).astype(F32))
    ).astype(F32).astype(BF)

    projected = tn(normed_ref[...], gate_up_ref[...])
    gate = projected[:, :HID]
    up = projected[:, HID:]
    activated = (weight * gate * jax.nn.sigmoid(1.702 * gate) * (up + 1.0)).astype(BF)
    activated = nn(pack, activated).astype(BF)
    for at in range(0, D, 640):
        size = min(640, D - at)
        out_ref[:, at : at + size] = nt(activated, down_ref[at : at + size, :]).astype(BF)

    own = (iota((8, TOK), 1) == iota((8, TOK), 0) + owner * 4).astype(F32).astype(BF)
    for at in range(0, D, 640):
        size = min(640, D - at)
        rows_ref[:, at : at + size] = nt(own, hidden_ref[at : at + size, :])[:4]

    pick = (iota((TOK, 128), 0) == iota((TOK, 128), 1) + plane * 32).astype(F32).astype(BF)
    turns = nn(turn.astype(BF), pick)
    per = 4 * DEPTH // 4 * CAP
    block = iota((per, 128), 0)
    parts = []
    for p in range(PLANE):
        expert = slot_ref[p * DEPTH + depth] // DEPTH
        theirs = jnp.sum(jnp.where(iota((8, 128), 0) == expert, turns, 0.0), axis=0, keepdims=True)
        parts.append(
            (
                ((iota((per, 128), 1) // 4) == (block // CAP))
                & (jnp.broadcast_to(theirs, (per, 128)) == (block % CAP).astype(F32))
            ).astype(F32)
        )
    merge_ref[...] = jnp.transpose(jnp.concatenate(parts, axis=0))[:32].astype(BF)


def expert_terms(placement, hidden, routes, gain, router, gate_up, down):
    return pl.pallas_call(
        expert_kernel,
        name="expert_terms",
        out_shape=(
            jax.ShapeDtypeStruct((PACKED, D), BF),
            jax.ShapeDtypeStruct((4, D), F32),
            jax.ShapeDtypeStruct((32, PACKED), BF),
        ),
        in_specs=[pl.BlockSpec(memory_space=SMEM)] + [pl.BlockSpec(memory_space=VMEM)] * 6,
        out_specs=(pl.BlockSpec(memory_space=VMEM),) * 3,
        scratch_shapes=[pltpu.SMEM((SLOTS,), jnp.int32), pltpu.VMEM((D, TOK), BF)],
        compiler_params=params(40),
        cost_estimate=pl.CostEstimate(flops=4 * 10**9, bytes_accessed=8 * 10**6, transcendentals=0),
    )(placement, hidden, routes, gain, router, gate_up, down)


def merge_kernel(merge_ref, got_ref, out_ref):
    for at in range(0, D, 640):
        size = min(640, D - at)
        part = nn(merge_ref[...], got_ref[:, at : at + size]).astype(BF)
        for z in range(DEPTH):
            out_ref[z, :, at : at + size] = part[4 * z : 4 * z + 4]


def merge_plane(merge, got):
    return pl.pallas_call(
        merge_kernel,
        name="merge_plane",
        out_shape=jax.ShapeDtypeStruct((DEPTH, 4, D), BF),
        in_specs=[pl.BlockSpec(memory_space=VMEM)] * 2,
        out_specs=pl.BlockSpec(memory_space=VMEM),
        compiler_params=params(16),
        cost_estimate=pl.CostEstimate(flops=10**8, bytes_accessed=10**6, transcendentals=0),
    )(merge, got)


def on_device(
    master, placement, resident_gate_up, resident_down, hidden, routes, norm_gain, router
):
    router_rows = router.T
    routers = [router_rows]
    for d in range(1, 4):
        pairs = [(r, r ^ d) for r in range(4)]
        routers.append(lax.ppermute(router_rows, REP, pairs))

    chunks = encode(placement, jnp.transpose(master, (2, 0, 1)))
    chunks = lax.all_to_all(chunks, FSDP, split_axis=0, concat_axis=0, tiled=True)

    terms, rows, merge = expert_terms(
        placement,
        hidden[0].T,
        routes[0].T,
        norm_gain[None],
        jnp.stack(routers),
        resident_gate_up[0],
        resident_down[0].T,
    )
    chunks, terms = lax.optimization_barrier((chunks, terms))
    across = lax.ppermute(chunks, "yh", ((0, 1), (1, 0)))
    core = lax.ppermute(chunks, "c", ((0, 1), (1, 0)))
    both = lax.ppermute(across, "c", ((0, 1), (1, 0)))
    terms = lax.all_to_all(terms, ("x", "yl"), split_axis=0, concat_axis=0, tiled=True)
    terms = merge_plane(merge, terms)
    terms = lax.all_to_all(terms, "z", split_axis=0, concat_axis=0, tiled=True)
    decoded = (rows + jnp.sum(terms.astype(F32), axis=0)).astype(BF)
    refreshed = assemble(chunks, across, core, both).T
    return (refreshed[None], decoded[None])


def solution(mesh):
    cut = Mesh(mesh.devices.reshape(4, 2, 8, 2, 2), ("x", "yl", "z", "yh", "c"))
    placed = (
        P(None, REP, FSDP),
        P(),
        P(FSDP, None, None),
        P(FSDP, None, None),
        P(REP, None, None),
        P(REP, None, None),
        P(),
        P(REP, None),
    )
    return jax.shard_map(
        on_device,
        mesh=cut,
        in_specs=placed,
        out_specs=(P(FSDP, None, None), P(REP, FSDP, None)),
        check_vma=False,
    )
```

```python
import jax
import jax.numpy as jnp
from jax import lax
from jax.experimental import pallas as pl
from jax.experimental.pallas import tpu as pltpu
from jax.sharding import Mesh
from jax.sharding import PartitionSpec as P

D = 2880
SLOTS = 64
COLS = 45
HALF = 24
ROWS = 64
TOK = 256
HID = 256
CAP = 3
SIDE = 4
DEPTH = 8
INNER = 16
PIECES = 5
PIECE = D // PIECES
PACKED = TOK // 4 * CAP

VMEM = pltpu.VMEM
SMEM = pltpu.SMEM
BF = jnp.bfloat16
F32 = jnp.float32

FSDP = ("x", "yl", "z")
REP = ("yh", "c")


def params(mib):
    return pltpu.CompilerParams(vmem_limit_bytes=mib * 2**20)


def in_hbm(x):
    return pltpu.with_memory_space_constraint(x, pltpu.HBM)


def nt(a, b):
    return lax.dot_general(a, b, (((1,), (1,)), ((), ())), preferred_element_type=F32)


def tn(a, b):
    return lax.dot_general(a, b, (((0,), (0,)), ((), ())), preferred_element_type=F32)


def nn(a, b):
    return lax.dot_general(a, b, (((1,), (0,)), ((), ())), preferred_element_type=F32)


def iota(shape, dim):
    return lax.broadcasted_iota(jnp.int32, shape, dim)


def invert(place_ref, slot_ref):
    def step(s, _):
        slot_ref[place_ref[s]] = s
        return 0

    lax.fori_loop(0, SLOTS, step, 0, unroll=8)


PAIRS = 12


def round_blocks(values, spread):
    size = jnp.abs(values)
    top = size
    for shift in (1, 2, 4, 8, 16):
        top = jnp.maximum(top, pltpu.roll(top, shift, 1))
    top = jnp.maximum(top, 6.0 * 2.0**-40)
    lead = top * (2.0**23 + 1.0)
    lead = jnp.abs(lead - lead * (1.0 - 2.0**-24))
    scale = jnp.where(top > lead * 1.5, lead * 0.5, lead * 0.25)
    s = nn(scale.astype(BF), spread)
    out = jnp.where(size >= s * 0.25, s * 0.5, 0.0)
    out = jnp.where(size >= s * 0.75, s, out)
    out = jnp.where(size >= s * 1.25, s * 1.5, out)
    out = jnp.where(size >= s * 1.75, s * 2.0, out)
    out = jnp.where(size >= s * 2.5, s * 3.0, out)
    out = jnp.where(size >= s * 3.5, s * 4.0, out)
    out = jnp.where(size >= s * 5.0, s * 6.0, out)
    return jnp.where(values < 0, -out, out)


def encode_kernel(
    place_hbm, master_ref, out_ref, place_ref, slot_ref, held_ref, raw_ref, sems, place_sem
):
    place_copy = pltpu.make_async_copy(place_hbm, place_ref, place_sem)
    place_copy.start()
    copies = []
    for g in range(HALF // PAIRS):
        at = g * PAIRS
        wide = min(PAIRS, COLS - HALF - at)
        for n, (start, size) in enumerate(((at, PAIRS), (HALF + at, wide))):
            part = pl.ds(start, size)
            copy = pltpu.make_async_copy(master_ref.at[part], raw_ref.at[part], sems.at[2 * g + n])
            copy.start()
            copies.append(copy)
    spread = (iota((128, 128), 0) == (iota((128, 128), 1) // 32) * 32 + 31).astype(F32).astype(BF)
    for g in range(HALF // PAIRS):
        at = g * PAIRS
        wide = min(PAIRS, COLS - HALF - at)
        copies[2 * g].wait()
        copies[2 * g + 1].wait()
        low = raw_ref[at : at + PAIRS]
        high = raw_ref[HALF + at : HALF + at + wide]
        if wide < PAIRS:
            high = jnp.concatenate([high, low[wide:]], axis=0)
        low = low.reshape(PAIRS * SLOTS, ROWS)
        high = high.reshape(PAIRS * SLOTS, ROWS)
        values = jnp.concatenate([low, high], axis=1)
        held_ref[at * SLOTS : (at + PAIRS) * SLOTS, :] = round_blocks(values, spread)

    place_copy.wait()
    invert(place_ref, slot_ref)

    def deal(o, _):
        out_ref[o] = held_ref[pl.ds(slot_ref[o], HALF, stride=SLOTS), :].astype(BF)
        return 0

    lax.fori_loop(0, SLOTS, deal, 0, unroll=8)


def encode(placement, master):
    return pl.pallas_call(
        encode_kernel,
        name="encode",
        out_shape=jax.ShapeDtypeStruct((SLOTS, HALF, 128), BF),
        in_specs=[pl.BlockSpec(memory_space=pl.ANY)] * 2,
        out_specs=pl.BlockSpec(memory_space=VMEM),
        scratch_shapes=[
            pltpu.SMEM((SLOTS,), jnp.int32),
            pltpu.SMEM((SLOTS,), jnp.int32),
            VMEM((HALF * SLOTS, 128), F32),
            VMEM((COLS, SLOTS, ROWS), F32),
            pltpu.SemaphoreType.DMA((2 * HALF // PAIRS,)),
            pltpu.SemaphoreType.DMA(()),
        ],
        compiler_params=params(16),
        cost_estimate=pl.CostEstimate(flops=10**9, bytes_accessed=4 * 10**6, transcendentals=0),
    )(placement, master)


GROUP = 16


def assemble_kernel(own_ref, across_ref, core_ref, both_ref, out_ref, held_ref):
    low = iota((HALF, 128), 1) < ROWS
    half = lax.axis_index("yh")
    core = lax.axis_index("c")
    for i in range(GROUP):
        here = (own_ref[i].astype(F32), core_ref[i].astype(F32))
        there = (across_ref[i].astype(F32), both_ref[i].astype(F32))
        for h in range(2):
            mine, other = (jnp.where(half == h, a, b) for a, b in zip(here, there))
            first = jnp.where(core == 0, mine, other)
            second = jnp.where(core == 0, other, mine)
            upper = jnp.where(low, first, pltpu.roll(second, ROWS, 1))
            lower = jnp.where(low, pltpu.roll(first, ROWS, 1), second)
            lanes = slice(128 * h, 128 * h + 128)
            held_ref[COLS * i : COLS * i + HALF, lanes] = upper
            held_ref[COLS * i + HALF : COLS * (i + 1), lanes] = lower[: COLS - HALF]
    out_ref[...] = held_ref[...].astype(BF)


def assemble(own, across, core, both):
    rows = GROUP * COLS
    return pl.pallas_call(
        assemble_kernel,
        name="assemble",
        grid=(SLOTS // GROUP,),
        out_shape=jax.ShapeDtypeStruct((D, 4 * ROWS), BF),
        in_specs=[pl.BlockSpec((GROUP, HALF, 128), lambda g: (g, 0, 0))] * 4,
        out_specs=pl.BlockSpec((rows, 4 * ROWS), lambda g: (g, 0)),
        scratch_shapes=[VMEM((rows, 4 * ROWS), F32)],
        compiler_params=params(24),
        cost_estimate=pl.CostEstimate(flops=10**9, bytes_accessed=4 * 10**6, transcendentals=0),
    )(own, across, core, both)


def norm_kernel(
    place_ref,
    hidden_ref,
    routes_ref,
    gain_ref,
    gate_up_ref,
    normed_ref,
    projected_ref,
    pack_ref,
    rows_ref,
    merge_ref,
    slot_ref,
    weight_ref,
    sems,
):
    copies = []
    for n in range(PIECES):
        part = pl.ds(n * PIECE, PIECE)
        copy = pltpu.make_async_copy(gate_up_ref.at[part], weight_ref.at[part], sems.at[n])
        copy.start()
        copies.append(copy)
    invert(place_ref, slot_ref)
    column = lax.axis_index("x")
    inner = lax.axis_index("yl") * DEPTH + lax.axis_index("z")
    owner = column * INNER + inner
    mine = slot_ref[owner] // DEPTH

    total = jnp.zeros((1, TOK), F32)
    step = 576
    for at in range(0, D, step):
        part = hidden_ref[at : at + step, :].astype(F32)
        total = total + jnp.sum(part * part, axis=0, keepdims=True)
    factor = lax.rsqrt(total * (1.0 / D) + 1e-05)
    ones = jnp.ones((128, TOK), BF)
    for at in range(0, D, 128):
        size = min(128, D - at)
        gain = gain_ref[:, at : at + size].astype(F32)
        diagonal = jnp.where(
            iota((size, size), 0) == iota((size, size), 1), jnp.broadcast_to(gain, (size, size)), 0.0
        ).astype(BF)
        spread = nn(diagonal, ones[:size])
        part = hidden_ref[at : at + size, :].astype(F32)
        normed_ref[at : at + size, :] = (part * factor * spread).astype(BF)
    projected = jnp.zeros((TOK, 2 * HID), F32)
    for n in range(PIECES):
        copies[n].wait()
        part = slice(n * PIECE, (n + 1) * PIECE)
        projected = projected + tn(normed_ref[part, :], weight_ref[part, :])
    projected_ref[...] = projected

    which = iota((8, TOK), 0)
    chosen = choices(routes_ref)
    earlier = (
        ((iota((TOK, TOK), 0) // 4) == (iota((TOK, TOK), 1) // 4))
        & (iota((TOK, TOK), 0) < iota((TOK, TOK), 1))
    ).astype(F32).astype(BF)
    rank = nn(chosen.astype(BF), earlier)
    turn = jnp.where(chosen > 0, rank, -1.0)
    my_turn = jnp.sum(jnp.where(which == mine, turn, 0.0), axis=0, keepdims=True)
    packed = iota((PACKED, TOK), 0)
    pack_ref[...] = (
        ((iota((PACKED, TOK), 1) // 4) == (packed // CAP))
        & (jnp.broadcast_to(my_turn, (PACKED, TOK)) == (packed % CAP).astype(F32))
    ).astype(F32).astype(BF)

    own = (iota((8, TOK), 1) == iota((8, TOK), 0) + owner * 4).astype(F32).astype(BF)
    for at in range(0, D, 640):
        size = min(640, D - at)
        rows_ref[:, at : at + size] = nt(own, hidden_ref[at : at + size, :])[:4]

    local = 4 * INNER
    pick = (iota((TOK, 128), 0) == iota((TOK, 128), 1) + column * local).astype(F32).astype(BF)
    turns = nn(turn.astype(BF), pick)
    per = INNER * CAP
    block = iota((per, 128), 0)
    parts = []
    for x in range(SIDE):
        expert = slot_ref[x * INNER + inner] // DEPTH
        theirs = jnp.sum(jnp.where(iota((8, 128), 0) == expert, turns, 0.0), axis=0, keepdims=True)
        parts.append(
            (
                ((iota((per, 128), 1) // 4) == (block // CAP))
                & (jnp.broadcast_to(theirs, (per, 128)) == (block % CAP).astype(F32))
            ).astype(F32)
        )
    merge_ref[...] = jnp.transpose(jnp.concatenate(parts, axis=0))[:local].astype(BF)


def choices(routes_ref):
    which = iota((8, TOK), 0)
    chosen = jnp.zeros((8, TOK), F32)
    for k in range(4):
        chosen = jnp.where(which == routes_ref[k : k + 1, :], 1.0, chosen)
    return chosen


def norm_project(placement, hidden, routes, gain, gate_up):
    return pl.pallas_call(
        norm_kernel,
        name="norm_project",
        out_shape=(
            jax.ShapeDtypeStruct((D, TOK), BF),
            jax.ShapeDtypeStruct((TOK, 2 * HID), F32),
            jax.ShapeDtypeStruct((PACKED, TOK), BF),
            jax.ShapeDtypeStruct((4, D), F32),
            jax.ShapeDtypeStruct((4 * INNER, PACKED), BF),
        ),
        in_specs=[pl.BlockSpec(memory_space=SMEM)]
        + [pl.BlockSpec(memory_space=VMEM)] * 3
        + [pl.BlockSpec(memory_space=pl.ANY)],
        out_specs=(pl.BlockSpec(memory_space=VMEM),) * 5,
        scratch_shapes=[
            pltpu.SMEM((SLOTS,), jnp.int32),
            VMEM((D, 2 * HID), BF),
            pltpu.SemaphoreType.DMA((PIECES,)),
        ],
        compiler_params=params(32),
        cost_estimate=pl.CostEstimate(flops=3 * 10**9, bytes_accessed=8 * 10**6, transcendentals=0),
    )(placement, hidden, routes, gain, gate_up)


def terms_kernel(
    place_ref, routes_ref, router_ref, normed_ref, projected_ref, pack_ref, down_ref, out_ref, slot_ref
):
    invert(place_ref, slot_ref)
    owner = lax.axis_index("x") * INNER + lax.axis_index("yl") * DEPTH + lax.axis_index("z")
    mine = slot_ref[owner] // DEPTH

    rep = lax.axis_index("yh") * 2 + lax.axis_index("c")
    logits = jnp.zeros((8, TOK), F32)
    for d in range(4):
        start = pl.multiple_of((rep ^ d) * 720, 720)
        logits = logits + nn(router_ref[d], normed_ref[pl.ds(start, 720), :])
    which = iota((8, TOK), 0)
    chosen = choices(routes_ref)
    powered = jnp.where(chosen > 0, jnp.exp(logits), 0.0)
    weights = powered / jnp.sum(powered, axis=0, keepdims=True)
    weight = jnp.sum(jnp.where(which == mine, weights, 0.0), axis=0, keepdims=True)
    weight = jnp.transpose(jnp.broadcast_to(weight, (8, TOK)))[:, 0:1]

    gate = projected_ref[:, :HID]
    up = projected_ref[:, HID:]
    activated = (weight * gate * jax.nn.sigmoid(1.702 * gate) * (up + 1.0)).astype(BF)
    activated = nn(pack_ref[...], activated).astype(BF)
    for at in range(0, D, 640):
        size = min(640, D - at)
        out_ref[:, at : at + size] = nt(activated, down_ref[at : at + size, :]).astype(BF)


def expert_terms(placement, routes, router, normed, projected, pack, down):
    return pl.pallas_call(
        terms_kernel,
        name="expert_terms",
        out_shape=jax.ShapeDtypeStruct((PACKED, D), BF),
        in_specs=[pl.BlockSpec(memory_space=SMEM)] + [pl.BlockSpec(memory_space=VMEM)] * 6,
        out_specs=pl.BlockSpec(memory_space=VMEM),
        scratch_shapes=[pltpu.SMEM((SLOTS,), jnp.int32)],
        compiler_params=params(32),
        cost_estimate=pl.CostEstimate(flops=10**9, bytes_accessed=4 * 10**6, transcendentals=0),
    )(placement, routes, router, normed, projected, pack, down)


def merge_kernel(merge_ref, got_ref, out_ref):
    for at in range(0, D, 640):
        size = min(640, D - at)
        part = nn(merge_ref[...], got_ref[:, at : at + size]).astype(BF)
        for n in range(INNER):
            out_ref[n, :, at : at + size] = part[4 * n : 4 * n + 4]


def merge_side(merge, got):
    return pl.pallas_call(
        merge_kernel,
        name="merge_side",
        out_shape=jax.ShapeDtypeStruct((INNER, 4, D), BF),
        in_specs=[pl.BlockSpec(memory_space=VMEM)] * 2,
        out_specs=pl.BlockSpec(memory_space=VMEM),
        compiler_params=params(16),
        cost_estimate=pl.CostEstimate(flops=10**8, bytes_accessed=10**6, transcendentals=0),
    )(merge, got)


def on_device(
    master, placement, resident_gate_up, resident_down, hidden, routes, norm_gain, router
):
    router_rows = router.T
    routers = [router_rows]
    for d in range(1, 4):
        pairs = [(r, r ^ d) for r in range(4)]
        routers.append(lax.ppermute(router_rows, REP, pairs))

    chunks = encode(in_hbm(placement), in_hbm(jnp.transpose(master, (2, 0, 1))))
    chunks = lax.all_to_all(chunks, FSDP, split_axis=0, concat_axis=0, tiled=True)

    chosen = routes[0].T
    normed, projected, pack, rows, merge = norm_project(
        placement, hidden[0].T, chosen, norm_gain[None], in_hbm(resident_gate_up[0])
    )
    terms = expert_terms(
        placement, chosen, jnp.stack(routers), normed, projected, pack, resident_down[0].T
    )
    chunks, terms = lax.optimization_barrier((chunks, terms))
    terms = lax.all_to_all(terms, "x", split_axis=0, concat_axis=0, tiled=True)
    across = lax.ppermute(chunks, "yh", ((0, 1), (1, 0)))
    core = lax.ppermute(chunks, "c", ((0, 1), (1, 0)))
    terms = merge_side(merge, terms)
    across, _ = lax.optimization_barrier((across, terms))
    both = lax.ppermute(across, "c", ((0, 1), (1, 0)))
    terms = lax.all_to_all(terms, ("yl", "z"), split_axis=0, concat_axis=0, tiled=True)
    decoded = (rows + jnp.sum(terms.astype(F32), axis=0)).astype(BF)
    refreshed = assemble(chunks, across, core, both).T
    return (refreshed[None], decoded[None])


def solution(mesh):
    cut = Mesh(mesh.devices.reshape(4, 2, 8, 2, 2), ("x", "yl", "z", "yh", "c"))
    placed = (
        P(None, REP, FSDP),
        P(),
        P(FSDP, None, None),
        P(FSDP, None, None),
        P(REP, None, None),
        P(REP, None, None),
        P(),
        P(REP, None),
    )
    return jax.shard_map(
        on_device,
        mesh=cut,
        in_specs=placed,
        out_specs=(P(FSDP, None, None), P(REP, FSDP, None)),
        check_vma=False,
    )
```

```python
import jax
import jax.numpy as jnp
from jax import lax
from jax.experimental import pallas as pl
from jax.experimental.pallas import tpu as pltpu
from jax.sharding import Mesh
from jax.sharding import PartitionSpec as P

D = 2880
SLOTS = 64
COLS = 45
HALF = 24
ROWS = 64
TOK = 256
HID = 256
CAP = 3
DEPTH = 8
PIECES = 5
PIECE = D // PIECES
SUB = 8
WIDE = 1152

VMEM = pltpu.VMEM
SMEM = pltpu.SMEM
BF = jnp.bfloat16
F32 = jnp.float32

FSDP = ("x", "yl", "z")
REP = ("yh", "c")


def params(mib):
    return pltpu.CompilerParams(vmem_limit_bytes=mib * 2**20)


def in_hbm(x):
    return pltpu.with_memory_space_constraint(x, pltpu.HBM)


def nt(a, b):
    return lax.dot_general(a, b, (((1,), (1,)), ((), ())), preferred_element_type=F32)


def tn(a, b):
    return lax.dot_general(a, b, (((0,), (0,)), ((), ())), preferred_element_type=F32)


def nn(a, b):
    return lax.dot_general(a, b, (((1,), (0,)), ((), ())), preferred_element_type=F32)


def iota(shape, dim):
    return lax.broadcasted_iota(jnp.int32, shape, dim)


def invert(place_ref, slot_ref):
    def step(s, _):
        slot_ref[place_ref[s]] = s
        return 0

    lax.fori_loop(0, SLOTS, step, 0, unroll=8)


PAIRS = 12


def round_blocks(values, spread):
    size = jnp.abs(values)
    top = size
    for shift in (1, 2, 4, 8, 16):
        top = jnp.maximum(top, pltpu.roll(top, shift, 1))
    top = jnp.maximum(top, 6.0 * 2.0**-40)
    lead = top * (2.0**23 + 1.0)
    lead = jnp.abs(lead - lead * (1.0 - 2.0**-24))
    scale = jnp.where(top > lead * 1.5, lead * 0.5, lead * 0.25)
    s = nn(scale.astype(BF), spread)
    out = jnp.where(size >= s * 0.25, s * 0.5, 0.0)
    out = jnp.where(size >= s * 0.75, s, out)
    out = jnp.where(size >= s * 1.25, s * 1.5, out)
    out = jnp.where(size >= s * 1.75, s * 2.0, out)
    out = jnp.where(size >= s * 2.5, s * 3.0, out)
    out = jnp.where(size >= s * 3.5, s * 4.0, out)
    out = jnp.where(size >= s * 5.0, s * 6.0, out)
    return jnp.where(values < 0, -out, out)


def encode_kernel(
    place_hbm, master_ref, out_ref, place_ref, slot_ref, held_ref, raw_ref, sems, place_sem
):
    place_copy = pltpu.make_async_copy(place_hbm, place_ref, place_sem)
    place_copy.start()
    copies = []
    for g in range(HALF // PAIRS):
        at = g * PAIRS
        wide = min(PAIRS, COLS - HALF - at)
        for n, (start, size) in enumerate(((at, PAIRS), (HALF + at, wide))):
            part = pl.ds(start, size)
            copy = pltpu.make_async_copy(master_ref.at[part], raw_ref.at[part], sems.at[2 * g + n])
            copy.start()
            copies.append(copy)
    spread = (iota((128, 128), 0) == (iota((128, 128), 1) // 32) * 32 + 31).astype(F32).astype(BF)
    for g in range(HALF // PAIRS):
        at = g * PAIRS
        wide = min(PAIRS, COLS - HALF - at)
        copies[2 * g].wait()
        copies[2 * g + 1].wait()
        low = raw_ref[at : at + PAIRS]
        high = raw_ref[HALF + at : HALF + at + wide]
        if wide < PAIRS:
            high = jnp.concatenate([high, low[wide:]], axis=0)
        low = low.reshape(PAIRS * SLOTS, ROWS)
        high = high.reshape(PAIRS * SLOTS, ROWS)
        values = jnp.concatenate([low, high], axis=1)
        held_ref[at * SLOTS : (at + PAIRS) * SLOTS, :] = round_blocks(values, spread)

    place_copy.wait()
    invert(place_ref, slot_ref)

    def deal(o, _):
        out_ref[o] = held_ref[pl.ds(slot_ref[o], HALF, stride=SLOTS), :].astype(BF)
        return 0

    lax.fori_loop(0, SLOTS, deal, 0, unroll=8)


def encode(placement, master):
    return pl.pallas_call(
        encode_kernel,
        name="encode",
        out_shape=jax.ShapeDtypeStruct((SLOTS, HALF, 128), BF),
        in_specs=[pl.BlockSpec(memory_space=pl.ANY)] * 2,
        out_specs=pl.BlockSpec(memory_space=VMEM),
        scratch_shapes=[
            pltpu.SMEM((SLOTS,), jnp.int32),
            pltpu.SMEM((SLOTS,), jnp.int32),
            VMEM((HALF * SLOTS, 128), F32),
            VMEM((COLS, SLOTS, ROWS), F32),
            pltpu.SemaphoreType.DMA((2 * HALF // PAIRS,)),
            pltpu.SemaphoreType.DMA(()),
        ],
        compiler_params=params(16),
        cost_estimate=pl.CostEstimate(flops=10**9, bytes_accessed=4 * 10**6, transcendentals=0),
    )(placement, master)


GROUP = 16


def assemble_kernel(own_ref, across_ref, core_ref, both_ref, out_ref, held_ref):
    low = iota((HALF, 128), 1) < ROWS
    half = lax.axis_index("yh")
    core = lax.axis_index("c")
    for i in range(GROUP):
        here = (own_ref[i].astype(F32), core_ref[i].astype(F32))
        there = (across_ref[i].astype(F32), both_ref[i].astype(F32))
        for h in range(2):
            mine, other = (jnp.where(half == h, a, b) for a, b in zip(here, there))
            first = jnp.where(core == 0, mine, other)
            second = jnp.where(core == 0, other, mine)
            upper = jnp.where(low, first, pltpu.roll(second, ROWS, 1))
            lower = jnp.where(low, pltpu.roll(first, ROWS, 1), second)
            lanes = slice(128 * h, 128 * h + 128)
            held_ref[COLS * i : COLS * i + HALF, lanes] = upper
            held_ref[COLS * i + HALF : COLS * (i + 1), lanes] = lower[: COLS - HALF]
    out_ref[...] = held_ref[...].astype(BF)


def assemble(own, across, core, both):
    rows = GROUP * COLS
    return pl.pallas_call(
        assemble_kernel,
        name="assemble",
        grid=(SLOTS // GROUP,),
        out_shape=jax.ShapeDtypeStruct((D, 4 * ROWS), BF),
        in_specs=[pl.BlockSpec((GROUP, HALF, 128), lambda g: (g, 0, 0))] * 4,
        out_specs=pl.BlockSpec((rows, 4 * ROWS), lambda g: (g, 0)),
        scratch_shapes=[VMEM((rows, 4 * ROWS), F32)],
        compiler_params=params(24),
        cost_estimate=pl.CostEstimate(flops=10**9, bytes_accessed=4 * 10**6, transcendentals=0),
    )(own, across, core, both)


def choices(routes_ref):
    which = iota((8, TOK), 0)
    chosen = jnp.zeros((8, TOK), F32)
    for k in range(4):
        chosen = jnp.where(which == routes_ref[k : k + 1, :], 1.0, chosen)
    return chosen


def turns(chosen):
    earlier = (
        ((iota((TOK, TOK), 0) // 4) == (iota((TOK, TOK), 1) // 4))
        & (iota((TOK, TOK), 0) < iota((TOK, TOK), 1))
    ).astype(F32).astype(BF)
    return jnp.where(chosen > 0, nn(chosen.astype(BF), earlier), -1.0)


def row_of(table, expert):
    return jnp.sum(jnp.where(iota((8, TOK), 0) == expert, table, 0.0), axis=0, keepdims=True)


def pack_rows(my_turn, wanted, valid):
    row = iota((SLOTS * SUB, TOK), 0)
    inside = (iota((SLOTS * SUB, TOK), 1) // 4) == row // SUB
    here = jnp.broadcast_to(my_turn, (SLOTS * SUB, TOK)) == wanted(row % SUB).astype(F32)
    return (inside & here & valid(row % SUB)).astype(F32).astype(BF)


PLACES = (
    (lambda s: s, lambda s: s < 3),
    (lambda s: s - 3, lambda s: (s >= 3) & (s < 6)),
    (lambda s: (s - 6) * 2, lambda s: s >= 6),
    (lambda s: s * 0 + 1, lambda s: s == 6),
)


def expert_kernel(
    place_ref,
    hidden_hbm,
    routes_ref,
    gain_ref,
    gate_up_hbm,
    down_hbm,
    out_ref,
    normed_ref,
    rows_ref,
    slot_ref,
    hidden_ref,
    gate_up_ref,
    down_ref,
    sems,
):
    copies = []
    for m, (hbm, ref) in enumerate(
        ((hidden_hbm, hidden_ref), (gate_up_hbm, gate_up_ref), (down_hbm, down_ref))
    ):
        for n in range(PIECES):
            part = pl.ds(n * PIECE, PIECE)
            copy = pltpu.make_async_copy(hbm.at[part], ref.at[part], sems.at[m * PIECES + n])
            copy.start()
            copies.append(copy)
    down_ref[D:, :] = jnp.zeros((64, HID), BF)
    invert(place_ref, slot_ref)
    owner = (lax.axis_index("x") * 2 + lax.axis_index("yl")) * DEPTH + lax.axis_index("z")
    mine = slot_ref[owner] // DEPTH
    my_turn = row_of(turns(choices(routes_ref)), mine)

    total = jnp.zeros((1, TOK), F32)
    for n in range(PIECES):
        copies[n].wait()
        part = hidden_ref[n * PIECE : (n + 1) * PIECE, :].astype(F32)
        total = total + jnp.sum(part * part, axis=0, keepdims=True)
    factor = lax.rsqrt(total * (1.0 / D) + 1e-05)
    ones = jnp.ones((128, TOK), BF)
    for at in range(0, D, 128):
        size = min(128, D - at)
        gain = gain_ref[:, at : at + size].astype(F32)
        diagonal = jnp.where(
            iota((size, size), 0) == iota((size, size), 1), jnp.broadcast_to(gain, (size, size)), 0.0
        ).astype(BF)
        spread = nn(diagonal, ones[:size])
        part = hidden_ref[at : at + size, :].astype(F32)
        normed_ref[at : at + size, :] = (part * factor * spread).astype(BF)

    projected = jnp.zeros((TOK, 2 * HID), F32)
    for n in range(PIECES):
        copies[PIECES + n].wait()
        part = slice(n * PIECE, (n + 1) * PIECE)
        projected = projected + tn(normed_ref[part, :], gate_up_ref[part, :])
    gate = projected[:, :HID]
    up = projected[:, HID:]
    activated = (gate * jax.nn.sigmoid(1.702 * gate) * (up + 1.0)).astype(BF)
    first, second, third, fourth = (
        nn(pack_rows(my_turn, *place), activated).astype(BF) for place in PLACES
    )
    near = jnp.concatenate([first, second, third], axis=1)
    far = jnp.concatenate([first, second, fourth], axis=1)
    for n in range(PIECES):
        copies[2 * PIECES + n].wait()

    def terms(lhs, at, size, last):
        parts = [down_ref[b : b + size, :] for b in (at, WIDE + at, last)]
        return nt(lhs, jnp.concatenate(parts, axis=1))

    end = 2 * WIDE
    for at in range(0, 512, 256):
        out_ref[:, at : at + 256] = terms(near, at, 256, end + at).astype(BF)
    out_ref[:, 512:640] = jnp.where(
        iota((SLOTS * SUB, 128), 1) < 64,
        terms(near, 512, 128, end + 512),
        terms(far, 512, 128, end - 64),
    ).astype(BF)
    for at in range(640, WIDE, 256):
        out_ref[:, at : at + 256] = terms(far, at, 256, end + at - 576).astype(BF)

    own = (iota((8, TOK), 1) == iota((8, TOK), 0) + owner * 4).astype(F32).astype(BF)
    for at in range(0, D, 640):
        size = min(640, D - at)
        rows_ref[:, at : at + size] = nt(own, hidden_ref[at : at + size, :])


def expert_terms(placement, hidden, routes, gain, gate_up, down):
    whole = pl.BlockSpec(memory_space=VMEM)
    return pl.pallas_call(
        expert_kernel,
        name="expert_terms",
        out_shape=(
            jax.ShapeDtypeStruct((SLOTS * SUB, WIDE), BF),
            jax.ShapeDtypeStruct((D, TOK), BF),
            jax.ShapeDtypeStruct((8, D), F32),
        ),
        in_specs=[
            pl.BlockSpec(memory_space=SMEM),
            pl.BlockSpec(memory_space=pl.ANY),
            whole,
            whole,
            pl.BlockSpec(memory_space=pl.ANY),
            pl.BlockSpec(memory_space=pl.ANY),
        ],
        out_specs=(whole,) * 3,
        scratch_shapes=[
            pltpu.SMEM((SLOTS,), jnp.int32),
            VMEM((D, TOK), BF),
            VMEM((D, 2 * HID), BF),
            VMEM((D + 64, HID), BF),
            pltpu.SemaphoreType.DMA((3 * PIECES,)),
        ],
        compiler_params=params(32),
        cost_estimate=pl.CostEstimate(flops=3 * 10**9, bytes_accessed=8 * 10**6, transcendentals=0),
    )(placement, hidden, routes, gain, gate_up, down)


def weigh_kernel(place_ref, routes_ref, router_ref, normed_ref, out_ref, slot_ref):
    invert(place_ref, slot_ref)
    owner = (lax.axis_index("x") * 2 + lax.axis_index("yl")) * DEPTH + lax.axis_index("z")

    rep = lax.axis_index("yh") * 2 + lax.axis_index("c")
    logits = jnp.zeros((8, TOK), F32)
    for d in range(4):
        start = pl.multiple_of((rep ^ d) * 720, 720)
        logits = logits + nn(router_ref[d], normed_ref[pl.ds(start, 720), :])
    chosen = choices(routes_ref)
    powered = jnp.where(chosen > 0, jnp.exp(logits), 0.0)
    weights = powered / jnp.sum(powered, axis=0, keepdims=True)
    turn = turns(chosen)

    lanes = SLOTS * SUB
    source = iota((8, lanes), 1) // SUB
    sub = iota((8, lanes), 1) % SUB
    expert = jnp.zeros((8, lanes), jnp.int32)
    for o in range(SLOTS):
        expert = jnp.where(source == o, slot_ref[o] // DEPTH, expert)
    match = expert == iota((8, lanes), 0)
    their_turn = jnp.zeros((8, lanes), F32)
    their_weight = jnp.zeros((8, lanes), F32)
    for i in range(4):
        mine = iota((8, TOK), 1) == owner * 4 + i
        token = iota((8, lanes), 0) == i
        for table, kind in ((turn, 0), (weights, 1)):
            column = jnp.sum(jnp.where(mine, table, 0.0), axis=1, keepdims=True)
            row = jnp.sum(jnp.where(match, column, 0.0), axis=0, keepdims=True)
            row = jnp.broadcast_to(row, (8, lanes))
            if kind == 0:
                their_turn = jnp.where(token, row, their_turn)
            else:
                their_weight = jnp.where(token, row, their_weight)
    their_weight = jnp.where(iota((8, lanes), 0) < 4, their_weight, 0.0)
    for n, (wanted, valid) in enumerate(PLACES):
        here = valid(sub) & (their_turn == wanted(sub).astype(F32))
        table = jnp.where(here, their_weight, 0.0)
        upper = table.astype(BF).astype(F32)
        both = jnp.concatenate([upper, table - upper], axis=0)
        out_ref[16 * n : 16 * n + 16, :] = both.astype(BF)


def weigh(placement, routes, router, normed):
    return pl.pallas_call(
        weigh_kernel,
        name="weigh",
        out_shape=jax.ShapeDtypeStruct((64, SLOTS * SUB), BF),
        in_specs=[pl.BlockSpec(memory_space=SMEM)] + [pl.BlockSpec(memory_space=VMEM)] * 3,
        out_specs=pl.BlockSpec(memory_space=VMEM),
        scratch_shapes=[pltpu.SMEM((SLOTS,), jnp.int32)],
        compiler_params=params(16),
        cost_estimate=pl.CostEstimate(flops=10**9, bytes_accessed=2 * 10**6, transcendentals=0),
    )(placement, routes, router, normed)


def finish_kernel(table_ref, got_ref, rows_ref, out_ref):
    mixed = []
    both = nn(table_ref[...], got_ref[...])
    for n in range(4):
        mixed.append(both[16 * n : 16 * n + 8] + both[16 * n + 8 : 16 * n + 16])
    rest = mixed[2] + pltpu.roll(mixed[3], WIDE // 2, 1)
    for at, part in ((0, mixed[0]), (WIDE, mixed[1]), (2 * WIDE, rest)):
        size = min(WIDE, D - at)
        out = rows_ref[:, at : at + size] + part[:, :size]
        out_ref[:, at : at + size] = out[:4].astype(BF)


def finish(table, got, rows):
    return pl.pallas_call(
        finish_kernel,
        name="finish",
        out_shape=jax.ShapeDtypeStruct((4, D), BF),
        in_specs=[pl.BlockSpec(memory_space=VMEM)] * 3,
        out_specs=pl.BlockSpec(memory_space=VMEM),
        compiler_params=params(16),
        cost_estimate=pl.CostEstimate(flops=10**8, bytes_accessed=10**6, transcendentals=0),
    )(table, got, rows)


def on_device(
    master, placement, resident_gate_up, resident_down, hidden, routes, norm_gain, router
):
    chunks = encode(in_hbm(placement), in_hbm(jnp.transpose(master, (2, 0, 1))))
    chunks = lax.all_to_all(chunks, FSDP, split_axis=0, concat_axis=0, tiled=True)

    chosen = routes[0].T
    terms, normed, rows = expert_terms(
        placement,
        in_hbm(hidden[0].T),
        chosen,
        norm_gain[None],
        in_hbm(resident_gate_up[0]),
        in_hbm(resident_down[0].T),
    )
    chunks, terms = lax.optimization_barrier((chunks, terms))
    terms = terms.reshape(SLOTS, SUB, WIDE)
    terms = lax.all_to_all(terms, FSDP, split_axis=0, concat_axis=0, tiled=True)

    across = lax.ppermute(chunks, "yh", ((0, 1), (1, 0)))
    core = lax.ppermute(chunks, "c", ((0, 1), (1, 0)))
    both = lax.ppermute(across, "c", ((0, 1), (1, 0)))
    refreshed = assemble(chunks, across, core, both).T
    router_rows, _ = lax.optimization_barrier((router.T, chunks))
    routers = [router_rows]
    for d in range(1, 4):
        routers.append(lax.ppermute(router_rows, REP, [(r, r ^ d) for r in range(4)]))
    table = weigh(placement, chosen, jnp.stack(routers), normed)
    terms, refreshed, table = lax.optimization_barrier((terms, refreshed, table))
    decoded = finish(table, terms.reshape(SLOTS * SUB, WIDE), rows)
    return (refreshed[None], decoded[None])


def solution(mesh):
    cut = Mesh(mesh.devices.reshape(4, 2, 8, 2, 2), ("x", "yl", "z", "yh", "c"))
    placed = (
        P(None, REP, FSDP),
        P(),
        P(FSDP, None, None),
        P(FSDP, None, None),
        P(REP, None, None),
        P(REP, None, None),
        P(),
        P(REP, None),
    )
    return jax.shard_map(
        on_device,
        mesh=cut,
        in_specs=placed,
        out_specs=(P(FSDP, None, None), P(REP, FSDP, None)),
        check_vma=False,
    )
```

```python
import jax
import jax.numpy as jnp
from jax import lax
from jax.experimental import pallas as pl
from jax.experimental.pallas import tpu as pltpu
from jax.sharding import Mesh
from jax.sharding import PartitionSpec as P

D = 2880
SLOTS = 64
COLS = 45
HALF = 24
ROWS = 64
TOK = 256
HID = 256
CAP = 3
DEPTH = 8
PIECES = 5
PIECE = D // PIECES
SUB = 8
WIDE = 1152

VMEM = pltpu.VMEM
SMEM = pltpu.SMEM
BF = jnp.bfloat16
F32 = jnp.float32

FSDP = ("x", "yl", "z")
REP = ("yh", "c")


def params(mib):
    return pltpu.CompilerParams(vmem_limit_bytes=mib * 2**20)


def in_hbm(x):
    return pltpu.with_memory_space_constraint(x, pltpu.HBM)


def nt(a, b):
    return lax.dot_general(a, b, (((1,), (1,)), ((), ())), preferred_element_type=F32)


def tn(a, b):
    return lax.dot_general(a, b, (((0,), (0,)), ((), ())), preferred_element_type=F32)


def nn(a, b):
    return lax.dot_general(a, b, (((1,), (0,)), ((), ())), preferred_element_type=F32)


def iota(shape, dim):
    return lax.broadcasted_iota(jnp.int32, shape, dim)


def invert(place_ref, slot_ref):
    def step(s, _):
        slot_ref[place_ref[s]] = s
        return 0

    lax.fori_loop(0, SLOTS, step, 0, unroll=8)


PAIRS = 12


def round_blocks(values, spread):
    size = jnp.abs(values)
    top = size
    for shift in (1, 2, 4, 8, 16):
        top = jnp.maximum(top, pltpu.roll(top, shift, 1))
    top = jnp.maximum(top, 6.0 * 2.0**-40)
    lead = top * (2.0**23 + 1.0)
    lead = jnp.abs(lead - lead * (1.0 - 2.0**-24))
    scale = jnp.where(top > lead * 1.5, lead * 0.5, lead * 0.25)
    s = nn(scale.astype(BF), spread)
    out = jnp.where(size >= s * 0.25, s * 0.5, 0.0)
    out = jnp.where(size >= s * 0.75, s, out)
    out = jnp.where(size >= s * 1.25, s * 1.5, out)
    out = jnp.where(size >= s * 1.75, s * 2.0, out)
    out = jnp.where(size >= s * 2.5, s * 3.0, out)
    out = jnp.where(size >= s * 3.5, s * 4.0, out)
    out = jnp.where(size >= s * 5.0, s * 6.0, out)
    return jnp.where(values < 0, -out, out)


def encode_kernel(
    place_hbm, master_ref, out_ref, place_ref, slot_ref, held_ref, raw_ref, sems, place_sem
):
    place_copy = pltpu.make_async_copy(place_hbm, place_ref, place_sem)
    place_copy.start()
    copies = []
    for g in range(HALF // PAIRS):
        at = g * PAIRS
        wide = min(PAIRS, COLS - HALF - at)
        for n, (start, size) in enumerate(((at, PAIRS), (HALF + at, wide))):
            part = pl.ds(start, size)
            copy = pltpu.make_async_copy(master_ref.at[part], raw_ref.at[part], sems.at[2 * g + n])
            copy.start()
            copies.append(copy)
    spread = (iota((128, 128), 0) == (iota((128, 128), 1) // 32) * 32 + 31).astype(F32).astype(BF)
    for g in range(HALF // PAIRS):
        at = g * PAIRS
        wide = min(PAIRS, COLS - HALF - at)
        copies[2 * g].wait()
        copies[2 * g + 1].wait()
        low = raw_ref[at : at + PAIRS]
        high = raw_ref[HALF + at : HALF + at + wide]
        if wide < PAIRS:
            high = jnp.concatenate([high, low[wide:]], axis=0)
        low = low.reshape(PAIRS * SLOTS, ROWS)
        high = high.reshape(PAIRS * SLOTS, ROWS)
        values = jnp.concatenate([low, high], axis=1)
        held_ref[at * SLOTS : (at + PAIRS) * SLOTS, :] = round_blocks(values, spread)

    place_copy.wait()
    invert(place_ref, slot_ref)

    def deal(o, _):
        out_ref[o] = held_ref[pl.ds(slot_ref[o], HALF, stride=SLOTS), :].astype(BF)
        return 0

    lax.fori_loop(0, SLOTS, deal, 0, unroll=8)


def encode(placement, master):
    return pl.pallas_call(
        encode_kernel,
        name="encode",
        out_shape=jax.ShapeDtypeStruct((SLOTS, HALF, 128), BF),
        in_specs=[pl.BlockSpec(memory_space=pl.ANY)] * 2,
        out_specs=pl.BlockSpec(memory_space=VMEM),
        scratch_shapes=[
            pltpu.SMEM((SLOTS,), jnp.int32),
            pltpu.SMEM((SLOTS,), jnp.int32),
            VMEM((HALF * SLOTS, 128), F32),
            VMEM((COLS, SLOTS, ROWS), F32),
            pltpu.SemaphoreType.DMA((2 * HALF // PAIRS,)),
            pltpu.SemaphoreType.DMA(()),
        ],
        compiler_params=params(16),
        cost_estimate=pl.CostEstimate(flops=10**9, bytes_accessed=4 * 10**6, transcendentals=0),
    )(placement, master)


GROUP = 16


def assemble_kernel(own_ref, across_ref, core_ref, both_ref, out_ref, held_ref):
    low = iota((HALF, 128), 1) < ROWS
    half = lax.axis_index("yh")
    core = lax.axis_index("c")
    for i in range(GROUP):
        here = (own_ref[i].astype(F32), core_ref[i].astype(F32))
        there = (across_ref[i].astype(F32), both_ref[i].astype(F32))
        for h in range(2):
            mine, other = (jnp.where(half == h, a, b) for a, b in zip(here, there))
            first = jnp.where(core == 0, mine, other)
            second = jnp.where(core == 0, other, mine)
            upper = jnp.where(low, first, pltpu.roll(second, ROWS, 1))
            lower = jnp.where(low, pltpu.roll(first, ROWS, 1), second)
            lanes = slice(128 * h, 128 * h + 128)
            held_ref[COLS * i : COLS * i + HALF, lanes] = upper
            held_ref[COLS * i + HALF : COLS * (i + 1), lanes] = lower[: COLS - HALF]
    out_ref[...] = held_ref[...].astype(BF)


def assemble(own, across, core, both):
    rows = GROUP * COLS
    return pl.pallas_call(
        assemble_kernel,
        name="assemble",
        grid=(SLOTS // GROUP,),
        out_shape=jax.ShapeDtypeStruct((D, 4 * ROWS), BF),
        in_specs=[pl.BlockSpec((GROUP, HALF, 128), lambda g: (g, 0, 0))] * 4,
        out_specs=pl.BlockSpec((rows, 4 * ROWS), lambda g: (g, 0)),
        scratch_shapes=[VMEM((rows, 4 * ROWS), F32)],
        compiler_params=params(24),
        cost_estimate=pl.CostEstimate(flops=10**9, bytes_accessed=4 * 10**6, transcendentals=0),
    )(own, across, core, both)


def choices(routes_ref):
    which = iota((8, TOK), 0)
    chosen = jnp.zeros((8, TOK), F32)
    for k in range(4):
        chosen = jnp.where(which == routes_ref[k : k + 1, :], 1.0, chosen)
    return chosen


def turns(chosen):
    earlier = (
        ((iota((TOK, TOK), 0) // 4) == (iota((TOK, TOK), 1) // 4))
        & (iota((TOK, TOK), 0) < iota((TOK, TOK), 1))
    ).astype(F32).astype(BF)
    return jnp.where(chosen > 0, nn(chosen.astype(BF), earlier), -1.0)


def row_of(table, expert):
    return jnp.sum(jnp.where(iota((8, TOK), 0) == expert, table, 0.0), axis=0, keepdims=True)


def pack_rows(my_turn, wanted, valid):
    row = iota((SLOTS * SUB, TOK), 0)
    inside = (iota((SLOTS * SUB, TOK), 1) // 4) == row // SUB
    here = jnp.broadcast_to(my_turn, (SLOTS * SUB, TOK)) == wanted(row % SUB).astype(F32)
    return (inside & here & valid(row % SUB)).astype(F32).astype(BF)


PLACES = (
    (lambda s: s, lambda s: s < 3),
    (lambda s: s - 3, lambda s: (s >= 3) & (s < 6)),
    (lambda s: (s - 6) * 2, lambda s: s >= 6),
    (lambda s: s * 0 + 1, lambda s: s == 6),
)


def expert_kernel(
    place_ref,
    hidden_hbm,
    routes_ref,
    gain_ref,
    gate_up_hbm,
    down_hbm,
    out_ref,
    normed_ref,
    rows_ref,
    slot_ref,
    hidden_ref,
    gate_up_ref,
    down_ref,
    sems,
):
    copies = []
    for m, (hbm, ref) in enumerate(
        ((hidden_hbm, hidden_ref), (gate_up_hbm, gate_up_ref), (down_hbm, down_ref))
    ):
        for n in range(PIECES):
            part = pl.ds(n * PIECE, PIECE)
            copy = pltpu.make_async_copy(hbm.at[part], ref.at[part], sems.at[m * PIECES + n])
            copy.start()
            copies.append(copy)
    down_ref[D:, :] = jnp.zeros((64, HID), BF)
    invert(place_ref, slot_ref)
    owner = (lax.axis_index("x") * 2 + lax.axis_index("yl")) * DEPTH + lax.axis_index("z")
    mine = slot_ref[owner] // DEPTH
    my_turn = row_of(turns(choices(routes_ref)), mine)

    total = jnp.zeros((1, TOK), F32)
    for n in range(PIECES):
        copies[n].wait()
        part = hidden_ref[n * PIECE : (n + 1) * PIECE, :].astype(F32)
        total = total + jnp.sum(part * part, axis=0, keepdims=True)
    factor = lax.rsqrt(total * (1.0 / D) + 1e-05)
    ones = jnp.ones((128, TOK), BF)
    for at in range(0, D, 128):
        size = min(128, D - at)
        gain = gain_ref[:, at : at + size].astype(F32)
        diagonal = jnp.where(
            iota((size, size), 0) == iota((size, size), 1), jnp.broadcast_to(gain, (size, size)), 0.0
        ).astype(BF)
        spread = nn(diagonal, ones[:size])
        part = hidden_ref[at : at + size, :].astype(F32)
        normed_ref[at : at + size, :] = (part * factor * spread).astype(BF)

    projected = jnp.zeros((TOK, 2 * HID), F32)
    for n in range(PIECES):
        copies[PIECES + n].wait()
        part = slice(n * PIECE, (n + 1) * PIECE)
        projected = projected + tn(normed_ref[part, :], gate_up_ref[part, :])
    gate = projected[:, :HID]
    up = projected[:, HID:]
    activated = (gate * jax.nn.sigmoid(1.702 * gate) * (up + 1.0)).astype(BF)
    first, second, third, fourth = (
        nn(pack_rows(my_turn, *place), activated).astype(BF) for place in PLACES
    )
    near = jnp.concatenate([first, second, third], axis=1)
    far = jnp.concatenate([first, second, fourth], axis=1)
    for n in range(PIECES):
        copies[2 * PIECES + n].wait()

    def terms(lhs, at, size, last):
        parts = [down_ref[b : b + size, :] for b in (at, WIDE + at, last)]
        return nt(lhs, jnp.concatenate(parts, axis=1))

    end = 2 * WIDE
    for at in range(0, 512, 256):
        out_ref[:, at : at + 256] = terms(near, at, 256, end + at).astype(BF)
    out_ref[:, 512:640] = jnp.where(
        iota((SLOTS * SUB, 128), 1) < 64,
        terms(near, 512, 128, end + 512),
        terms(far, 512, 128, end - 64),
    ).astype(BF)
    for at in range(640, WIDE, 256):
        out_ref[:, at : at + 256] = terms(far, at, 256, end + at - 576).astype(BF)

    own = (iota((8, TOK), 1) == iota((8, TOK), 0) + owner * 4).astype(F32).astype(BF)
    for at in range(0, D, 640):
        size = min(640, D - at)
        rows_ref[:, at : at + size] = nt(own, hidden_ref[at : at + size, :])


def expert_terms(placement, hidden, routes, gain, gate_up, down):
    whole = pl.BlockSpec(memory_space=VMEM)
    return pl.pallas_call(
        expert_kernel,
        name="expert_terms",
        out_shape=(
            jax.ShapeDtypeStruct((SLOTS * SUB, WIDE), BF),
            jax.ShapeDtypeStruct((D, TOK), BF),
            jax.ShapeDtypeStruct((8, D), F32),
        ),
        in_specs=[
            pl.BlockSpec(memory_space=SMEM),
            pl.BlockSpec(memory_space=pl.ANY),
            whole,
            whole,
            pl.BlockSpec(memory_space=pl.ANY),
            pl.BlockSpec(memory_space=pl.ANY),
        ],
        out_specs=(whole,) * 3,
        scratch_shapes=[
            pltpu.SMEM((SLOTS,), jnp.int32),
            VMEM((D, TOK), BF),
            VMEM((D, 2 * HID), BF),
            VMEM((D + 64, HID), BF),
            pltpu.SemaphoreType.DMA((3 * PIECES,)),
        ],
        compiler_params=params(32),
        cost_estimate=pl.CostEstimate(flops=3 * 10**9, bytes_accessed=8 * 10**6, transcendentals=0),
    )(placement, hidden, routes, gain, gate_up, down)


def weigh_kernel(place_ref, routes_ref, router_ref, normed_ref, out_ref, slot_ref):
    invert(place_ref, slot_ref)
    owner = (lax.axis_index("x") * 2 + lax.axis_index("yl")) * DEPTH + lax.axis_index("z")

    rep = lax.axis_index("yh") * 2 + lax.axis_index("c")
    logits = jnp.zeros((8, TOK), F32)
    for d in range(4):
        start = pl.multiple_of((rep ^ d) * 720, 720)
        logits = logits + nn(router_ref[d], normed_ref[pl.ds(start, 720), :])
    chosen = choices(routes_ref)
    powered = jnp.where(chosen > 0, jnp.exp(logits), 0.0)
    weights = powered / jnp.sum(powered, axis=0, keepdims=True)
    turn = turns(chosen)

    lanes = SLOTS * SUB
    source = iota((8, lanes), 1) // SUB
    sub = iota((8, lanes), 1) % SUB
    expert = jnp.zeros((8, lanes), jnp.int32)
    for o in range(SLOTS):
        expert = jnp.where(source == o, slot_ref[o] // DEPTH, expert)
    match = expert == iota((8, lanes), 0)
    their_turn = jnp.zeros((8, lanes), F32)
    their_weight = jnp.zeros((8, lanes), F32)
    for i in range(4):
        mine = iota((8, TOK), 1) == owner * 4 + i
        token = iota((8, lanes), 0) == i
        for table, kind in ((turn, 0), (weights, 1)):
            column = jnp.sum(jnp.where(mine, table, 0.0), axis=1, keepdims=True)
            row = jnp.sum(jnp.where(match, column, 0.0), axis=0, keepdims=True)
            row = jnp.broadcast_to(row, (8, lanes))
            if kind == 0:
                their_turn = jnp.where(token, row, their_turn)
            else:
                their_weight = jnp.where(token, row, their_weight)
    their_weight = jnp.where(iota((8, lanes), 0) < 4, their_weight, 0.0)
    for n, (wanted, valid) in enumerate(PLACES):
        here = valid(sub) & (their_turn == wanted(sub).astype(F32))
        table = jnp.where(here, their_weight, 0.0)
        upper = table.astype(BF).astype(F32)
        both = jnp.concatenate([upper, table - upper], axis=0)
        out_ref[16 * n : 16 * n + 16, :] = both.astype(BF)


def weigh(placement, routes, router, normed):
    return pl.pallas_call(
        weigh_kernel,
        name="weigh",
        out_shape=jax.ShapeDtypeStruct((64, SLOTS * SUB), BF),
        in_specs=[pl.BlockSpec(memory_space=SMEM)] + [pl.BlockSpec(memory_space=VMEM)] * 3,
        out_specs=pl.BlockSpec(memory_space=VMEM),
        scratch_shapes=[pltpu.SMEM((SLOTS,), jnp.int32)],
        compiler_params=params(16),
        cost_estimate=pl.CostEstimate(flops=10**9, bytes_accessed=2 * 10**6, transcendentals=0),
    )(placement, routes, router, normed)


def finish_kernel(table_ref, got_ref, rows_ref, out_ref):
    mixed = []
    both = nn(table_ref[...], got_ref[...])
    for n in range(4):
        mixed.append(both[16 * n : 16 * n + 8] + both[16 * n + 8 : 16 * n + 16])
    rest = mixed[2] + pltpu.roll(mixed[3], WIDE // 2, 1)
    for at, part in ((0, mixed[0]), (WIDE, mixed[1]), (2 * WIDE, rest)):
        size = min(WIDE, D - at)
        out = rows_ref[:, at : at + size] + part[:, :size]
        out_ref[:, at : at + size] = out[:4].astype(BF)


def finish(table, got, rows):
    return pl.pallas_call(
        finish_kernel,
        name="finish",
        out_shape=jax.ShapeDtypeStruct((4, D), BF),
        in_specs=[pl.BlockSpec(memory_space=VMEM)] * 3,
        out_specs=pl.BlockSpec(memory_space=VMEM),
        compiler_params=params(16),
        cost_estimate=pl.CostEstimate(flops=10**8, bytes_accessed=10**6, transcendentals=0),
    )(table, got, rows)


def on_device(
    master, placement, resident_gate_up, resident_down, hidden, routes, norm_gain, router
):
    chunks = encode(in_hbm(placement), in_hbm(jnp.transpose(master, (2, 0, 1))))
    router_rows, chunks = lax.optimization_barrier((router.T, chunks))
    chunks = lax.all_to_all(chunks, FSDP, split_axis=0, concat_axis=0, tiled=True)

    chosen = routes[0].T
    terms, normed, rows = expert_terms(
        placement,
        in_hbm(hidden[0].T),
        chosen,
        norm_gain[None],
        in_hbm(resident_gate_up[0]),
        in_hbm(resident_down[0].T),
    )
    routers = [router_rows]
    for d in range(1, 4):
        routers.append(lax.ppermute(router_rows, REP, [(r, r ^ d) for r in range(4)]))
    table = weigh(placement, chosen, jnp.stack(routers), normed)
    chunks, terms, table = lax.optimization_barrier((chunks, terms, table))
    terms = terms.reshape(SLOTS, SUB, WIDE)
    terms = lax.all_to_all(terms, FSDP, split_axis=0, concat_axis=0, tiled=True)

    across = lax.ppermute(chunks, "yh", ((0, 1), (1, 0)))
    core = lax.ppermute(chunks, "c", ((0, 1), (1, 0)))
    both = lax.ppermute(across, "c", ((0, 1), (1, 0)))
    refreshed = assemble(chunks, across, core, both).T
    terms, refreshed = lax.optimization_barrier((terms, refreshed))
    decoded = finish(table, terms.reshape(SLOTS * SUB, WIDE), rows)
    return (refreshed[None], decoded[None])


def solution(mesh):
    cut = Mesh(mesh.devices.reshape(4, 2, 8, 2, 2), ("x", "yl", "z", "yh", "c"))
    placed = (
        P(None, REP, FSDP),
        P(),
        P(FSDP, None, None),
        P(FSDP, None, None),
        P(REP, None, None),
        P(REP, None, None),
        P(),
        P(REP, None),
    )
    return jax.shard_map(
        on_device,
        mesh=cut,
        in_specs=placed,
        out_specs=(P(FSDP, None, None), P(REP, FSDP, None)),
        check_vma=False,
    )
```

```python
import jax
import jax.numpy as jnp
from jax import lax
from jax.experimental import pallas as pl
from jax.experimental.pallas import tpu as pltpu
from jax.sharding import Mesh
from jax.sharding import PartitionSpec as P

D = 2880
SLOTS = 64
COLS = 45
HALF = 24
ROWS = 64
TOK = 256
HID = 256
CAP = 3
SIDE = 4
DEPTH = 8
INNER = 16
PIECES = 5
PIECE = D // PIECES
PACKED = TOK // 4 * CAP
SIDE_ROWS = PACKED // SIDE

VMEM = pltpu.VMEM
SMEM = pltpu.SMEM
BF = jnp.bfloat16
F32 = jnp.float32

FSDP = ("x", "yl", "z")
REP = ("yh", "c")


def params(mib):
    return pltpu.CompilerParams(vmem_limit_bytes=mib * 2**20)


def in_hbm(x):
    return pltpu.with_memory_space_constraint(x, pltpu.HBM)


def nt(a, b):
    return lax.dot_general(a, b, (((1,), (1,)), ((), ())), preferred_element_type=F32)


def tn(a, b):
    return lax.dot_general(a, b, (((0,), (0,)), ((), ())), preferred_element_type=F32)


def nn(a, b):
    return lax.dot_general(a, b, (((1,), (0,)), ((), ())), preferred_element_type=F32)


def iota(shape, dim):
    return lax.broadcasted_iota(jnp.int32, shape, dim)


def invert(place_ref, slot_ref):
    def step(s, _):
        slot_ref[place_ref[s]] = s
        return 0

    lax.fori_loop(0, SLOTS, step, 0, unroll=8)


PAIRS = 12


def round_blocks(values, spread):
    size = jnp.abs(values)
    top = size
    for shift in (1, 2, 4, 8, 16):
        top = jnp.maximum(top, pltpu.roll(top, shift, 1))
    top = jnp.maximum(top, 6.0 * 2.0**-40)
    lead = top * (2.0**23 + 1.0)
    lead = jnp.abs(lead - lead * (1.0 - 2.0**-24))
    scale = jnp.where(top > lead * 1.5, lead * 0.5, lead * 0.25)
    s = nn(scale.astype(BF), spread)
    out = jnp.where(size >= s * 0.25, s * 0.5, 0.0)
    out = jnp.where(size >= s * 0.75, s, out)
    out = jnp.where(size >= s * 1.25, s * 1.5, out)
    out = jnp.where(size >= s * 1.75, s * 2.0, out)
    out = jnp.where(size >= s * 2.5, s * 3.0, out)
    out = jnp.where(size >= s * 3.5, s * 4.0, out)
    out = jnp.where(size >= s * 5.0, s * 6.0, out)
    return jnp.where(values < 0, -out, out)


def encode_kernel(
    place_hbm, master_ref, out_ref, place_ref, slot_ref, held_ref, raw_ref, sems, place_sem
):
    place_copy = pltpu.make_async_copy(place_hbm, place_ref, place_sem)
    place_copy.start()
    copies = []
    for g in range(HALF // PAIRS):
        at = g * PAIRS
        wide = min(PAIRS, COLS - HALF - at)
        for n, (start, size) in enumerate(((at, PAIRS), (HALF + at, wide))):
            part = pl.ds(start, size)
            copy = pltpu.make_async_copy(master_ref.at[part], raw_ref.at[part], sems.at[2 * g + n])
            copy.start()
            copies.append(copy)
    spread = (iota((128, 128), 0) == (iota((128, 128), 1) // 32) * 32 + 31).astype(F32).astype(BF)
    for g in range(HALF // PAIRS):
        at = g * PAIRS
        wide = min(PAIRS, COLS - HALF - at)
        copies[2 * g].wait()
        copies[2 * g + 1].wait()
        low = raw_ref[at : at + PAIRS]
        high = raw_ref[HALF + at : HALF + at + wide]
        if wide < PAIRS:
            high = jnp.concatenate([high, low[wide:]], axis=0)
        low = low.reshape(PAIRS * SLOTS, ROWS)
        high = high.reshape(PAIRS * SLOTS, ROWS)
        values = jnp.concatenate([low, high], axis=1)
        held_ref[at * SLOTS : (at + PAIRS) * SLOTS, :] = round_blocks(values, spread)

    place_copy.wait()
    invert(place_ref, slot_ref)

    def deal(o, _):
        out_ref[o] = held_ref[pl.ds(slot_ref[o], HALF, stride=SLOTS), :].astype(BF)
        return 0

    lax.fori_loop(0, SLOTS, deal, 0, unroll=8)


def encode(placement, master):
    return pl.pallas_call(
        encode_kernel,
        name="encode",
        out_shape=jax.ShapeDtypeStruct((SLOTS, HALF, 128), BF),
        in_specs=[pl.BlockSpec(memory_space=pl.ANY)] * 2,
        out_specs=pl.BlockSpec(memory_space=VMEM),
        scratch_shapes=[
            pltpu.SMEM((SLOTS,), jnp.int32),
            pltpu.SMEM((SLOTS,), jnp.int32),
            VMEM((HALF * SLOTS, 128), F32),
            VMEM((COLS, SLOTS, ROWS), F32),
            pltpu.SemaphoreType.DMA((2 * HALF // PAIRS,)),
            pltpu.SemaphoreType.DMA(()),
        ],
        compiler_params=params(16),
        cost_estimate=pl.CostEstimate(flops=1, bytes_accessed=1, transcendentals=0),
    )(placement, master)


GROUP = 16


def assemble_kernel(own_ref, across_ref, core_ref, both_ref, out_ref, held_ref):
    low = iota((HALF, 128), 1) < ROWS
    half = lax.axis_index("yh")
    core = lax.axis_index("c")
    for i in range(GROUP):
        here = (own_ref[i].astype(F32), core_ref[i].astype(F32))
        there = (across_ref[i].astype(F32), both_ref[i].astype(F32))
        for h in range(2):
            mine, other = (jnp.where(half == h, a, b) for a, b in zip(here, there))
            first = jnp.where(core == 0, mine, other)
            second = jnp.where(core == 0, other, mine)
            upper = jnp.where(low, first, pltpu.roll(second, ROWS, 1))
            lower = jnp.where(low, pltpu.roll(first, ROWS, 1), second)
            lanes = slice(128 * h, 128 * h + 128)
            held_ref[COLS * i : COLS * i + HALF, lanes] = upper
            held_ref[COLS * i + HALF : COLS * (i + 1), lanes] = lower[: COLS - HALF]
    out_ref[...] = held_ref[...].astype(BF)


def assemble(own, across, core, both):
    rows = GROUP * COLS
    return pl.pallas_call(
        assemble_kernel,
        name="assemble",
        grid=(SLOTS // GROUP,),
        out_shape=jax.ShapeDtypeStruct((D, 4 * ROWS), BF),
        in_specs=[pl.BlockSpec((GROUP, HALF, 128), lambda g: (g, 0, 0))] * 4,
        out_specs=pl.BlockSpec((rows, 4 * ROWS), lambda g: (g, 0)),
        scratch_shapes=[VMEM((rows, 4 * ROWS), F32)],
        compiler_params=params(24),
        cost_estimate=pl.CostEstimate(flops=10**9, bytes_accessed=4 * 10**6, transcendentals=0),
    )(own, across, core, both)


def choices(routes_ref):
    which = iota((8, TOK), 0)
    chosen = jnp.zeros((8, TOK), F32)
    for k in range(4):
        chosen = jnp.where(which == routes_ref[k : k + 1, :], 1.0, chosen)
    return chosen


def turns(chosen):
    earlier = (
        ((iota((TOK, TOK), 0) // 4) == (iota((TOK, TOK), 1) // 4))
        & (iota((TOK, TOK), 0) < iota((TOK, TOK), 1))
    ).astype(F32).astype(BF)
    return jnp.where(chosen > 0, nn(chosen.astype(BF), earlier), -1.0)


def row_of(table, expert):
    return jnp.sum(jnp.where(iota((8, TOK), 0) == expert, table, 0.0), axis=0, keepdims=True)


def expert_kernel(
    place_ref,
    hidden_hbm,
    routes_ref,
    gain_ref,
    gate_up_hbm,
    down_hbm,
    out0_ref,
    out1_ref,
    out2_ref,
    out3_ref,
    normed_ref,
    rows_ref,
    slot_ref,
    hidden_ref,
    gate_up_ref,
    down_ref,
    sems,
):
    copies = []
    for m, (hbm, ref) in enumerate(
        ((hidden_hbm, hidden_ref), (gate_up_hbm, gate_up_ref), (down_hbm, down_ref))
    ):
        for n in range(PIECES):
            part = pl.ds(n * PIECE, PIECE)
            copy = pltpu.make_async_copy(hbm.at[part], ref.at[part], sems.at[m * PIECES + n])
            copy.start()
            copies.append(copy)
    invert(place_ref, slot_ref)
    side = lax.axis_index("x")
    owner = side * INNER + lax.axis_index("yl") * DEPTH + lax.axis_index("z")
    mine = slot_ref[owner] // DEPTH

    my_turn = row_of(turns(choices(routes_ref)), mine)
    packed = iota((PACKED, TOK), 0)
    block = ((packed // SIDE_ROWS) ^ side) * INNER + (packed % SIDE_ROWS) // CAP
    pack = (
        ((iota((PACKED, TOK), 1) // 4) == block)
        & (jnp.broadcast_to(my_turn, (PACKED, TOK)) == (packed % CAP).astype(F32))
    ).astype(F32).astype(BF)

    total = jnp.zeros((1, TOK), F32)
    for n in range(PIECES):
        copies[n].wait()
        part = hidden_ref[n * PIECE : (n + 1) * PIECE, :].astype(F32)
        total = total + jnp.sum(part * part, axis=0, keepdims=True)
    factor = lax.rsqrt(total * (1.0 / D) + 1e-05)
    ones = jnp.ones((128, TOK), BF)
    for at in range(0, D, 128):
        size = min(128, D - at)
        gain = gain_ref[:, at : at + size].astype(F32)
        diagonal = jnp.where(
            iota((size, size), 0) == iota((size, size), 1), jnp.broadcast_to(gain, (size, size)), 0.0
        ).astype(BF)
        spread = nn(diagonal, ones[:size])
        part = hidden_ref[at : at + size, :].astype(F32)
        normed_ref[at : at + size, :] = (part * factor * spread).astype(BF)

    projected = jnp.zeros((TOK, 2 * HID), F32)
    for n in range(PIECES):
        copies[PIECES + n].wait()
        part = slice(n * PIECE, (n + 1) * PIECE)
        projected = projected + tn(normed_ref[part, :], gate_up_ref[part, :])
    gate = projected[:, :HID]
    up = projected[:, HID:]
    activated = (gate * jax.nn.sigmoid(1.702 * gate) * (up + 1.0)).astype(BF)
    activated = nn(pack, activated).astype(BF)
    for n in range(PIECES):
        copies[2 * PIECES + n].wait()
    for at in range(0, D, 640):
        size = min(640, D - at)
        terms = nt(activated, down_ref[at : at + size, :]).astype(BF)
        for d, out_ref in enumerate((out0_ref, out1_ref, out2_ref, out3_ref)):
            out_ref[:, at : at + size] = terms[d * SIDE_ROWS : (d + 1) * SIDE_ROWS]

    own = (iota((8, TOK), 1) == iota((8, TOK), 0) + owner * 4).astype(F32).astype(BF)
    for at in range(0, D, 640):
        size = min(640, D - at)
        rows_ref[:, at : at + size] = nt(own, hidden_ref[at : at + size, :])[:4]


def expert_terms(placement, hidden, routes, gain, gate_up, down):
    whole = pl.BlockSpec(memory_space=VMEM)
    out = jax.ShapeDtypeStruct((SIDE_ROWS, D), BF)
    return pl.pallas_call(
        expert_kernel,
        name="expert_terms",
        out_shape=(out,) * 4
        + (jax.ShapeDtypeStruct((D, TOK), BF), jax.ShapeDtypeStruct((4, D), F32)),
        in_specs=[
            pl.BlockSpec(memory_space=SMEM),
            pl.BlockSpec(memory_space=pl.ANY),
            whole,
            whole,
            pl.BlockSpec(memory_space=pl.ANY),
            pl.BlockSpec(memory_space=pl.ANY),
        ],
        out_specs=(whole,) * 6,
        scratch_shapes=[
            pltpu.SMEM((SLOTS,), jnp.int32),
            VMEM((D, TOK), BF),
            VMEM((D, 2 * HID), BF),
            VMEM((D, HID), BF),
            pltpu.SemaphoreType.DMA((3 * PIECES,)),
        ],
        compiler_params=params(32),
        cost_estimate=pl.CostEstimate(flops=3 * 10**9, bytes_accessed=8 * 10**6, transcendentals=0),
    )(placement, hidden, routes, gain, gate_up, down)


def weigh_kernel(place_ref, routes_ref, router_ref, normed_ref, out_ref, slot_ref, held_ref):
    invert(place_ref, slot_ref)
    side = lax.axis_index("x")
    inner = lax.axis_index("yl") * DEPTH + lax.axis_index("z")

    rep = lax.axis_index("yh") * 2 + lax.axis_index("c")
    logits = jnp.zeros((8, TOK), F32)
    for d in range(4):
        start = pl.multiple_of((rep ^ d) * 720, 720)
        logits = logits + nn(router_ref[d], normed_ref[pl.ds(start, 720), :])
    chosen = choices(routes_ref)
    powered = jnp.where(chosen > 0, jnp.exp(logits), 0.0)
    weights = powered / jnp.sum(powered, axis=0, keepdims=True)
    turn = turns(chosen)

    packed = iota((SIDE_ROWS, TOK), 0)
    inside = (iota((SIDE_ROWS, TOK), 1) // 4) == side * INNER + packed // CAP
    parts = []
    for d in range(SIDE):
        expert = slot_ref[(side ^ d) * INNER + inner] // DEPTH
        here = jnp.broadcast_to(row_of(turn, expert), (SIDE_ROWS, TOK)) == (packed % CAP).astype(F32)
        weight = jnp.broadcast_to(row_of(weights, expert), (SIDE_ROWS, TOK))
        parts.append(jnp.where(inside & here, weight, 0.0))
    held_ref[...] = jnp.transpose(jnp.concatenate(parts, axis=0))
    local = 4 * INNER
    table = held_ref[pl.ds(pl.multiple_of(side * local, local), local), :]
    upper = table.astype(BF)
    out_ref[:local, :] = upper
    out_ref[local:, :] = (table - upper.astype(F32)).astype(BF)


def weigh(placement, routes, router, normed):
    return pl.pallas_call(
        weigh_kernel,
        name="weigh",
        out_shape=jax.ShapeDtypeStruct((8 * INNER, PACKED), BF),
        in_specs=[pl.BlockSpec(memory_space=SMEM)] + [pl.BlockSpec(memory_space=VMEM)] * 3,
        out_specs=pl.BlockSpec(memory_space=VMEM),
        scratch_shapes=[pltpu.SMEM((SLOTS,), jnp.int32), VMEM((TOK, PACKED), F32)],
        compiler_params=params(16),
        cost_estimate=pl.CostEstimate(flops=1, bytes_accessed=1, transcendentals=0),
    )(placement, routes, router, normed)


def merge_kernel(table_ref, got0_ref, got1_ref, got2_ref, got3_ref, out_ref):
    local = 4 * INNER
    for at in range(0, D, 640):
        size = min(640, D - at)
        got = jnp.concatenate(
            [ref[:, at : at + size] for ref in (got0_ref, got1_ref, got2_ref, got3_ref)], axis=0
        )
        both = nn(table_ref[...], got)
        part = (both[:local] + both[local:]).astype(BF)
        for n in range(INNER):
            out_ref[n, :, at : at + size] = part[4 * n : 4 * n + 4]


def merge_side(table, got):
    return pl.pallas_call(
        merge_kernel,
        name="merge_side",
        out_shape=jax.ShapeDtypeStruct((INNER, 4, D), BF),
        in_specs=[pl.BlockSpec(memory_space=VMEM)] * 5,
        out_specs=pl.BlockSpec(memory_space=VMEM),
        compiler_params=params(16),
        cost_estimate=pl.CostEstimate(flops=10**8, bytes_accessed=10**6, transcendentals=0),
    )(table, *got)


def on_device(
    master, placement, resident_gate_up, resident_down, hidden, routes, norm_gain, router
):
    chosen = routes[0].T
    *terms, normed, rows = expert_terms(
        placement,
        in_hbm(hidden[0].T),
        chosen,
        norm_gain[None],
        in_hbm(resident_gate_up[0]),
        in_hbm(resident_down[0].T),
    )
    got = [terms[0]]
    for d in range(1, SIDE):
        got.append(lax.ppermute(terms[d], "x", [(x, x ^ d) for x in range(SIDE)]))

    master, _ = lax.optimization_barrier((master, terms[0]))
    chunks = encode(in_hbm(placement), in_hbm(jnp.transpose(master, (2, 0, 1))))
    router_rows, _ = lax.optimization_barrier((router.T, chunks))
    routers = [router_rows]
    for d in range(1, 4):
        routers.append(lax.ppermute(router_rows, REP, [(r, r ^ d) for r in range(4)]))
    chunks = lax.all_to_all(chunks, FSDP, split_axis=0, concat_axis=0, tiled=True)
    table = weigh(placement, chosen, jnp.stack(routers), normed)
    terms = merge_side(table, got)
    chunks, terms = lax.optimization_barrier((chunks, terms))

    across = lax.ppermute(chunks, "yh", ((0, 1), (1, 0)))
    core = lax.ppermute(chunks, "c", ((0, 1), (1, 0)))
    both = lax.ppermute(across, "c", ((0, 1), (1, 0)))
    terms = lax.all_to_all(terms, ("yl", "z"), split_axis=0, concat_axis=0, tiled=True)
    refreshed = assemble(chunks, across, core, both).T
    terms, refreshed = lax.optimization_barrier((terms, refreshed))
    decoded = (rows + jnp.sum(terms.astype(F32), axis=0)).astype(BF)
    return (refreshed[None], decoded[None])


def solution(mesh):
    cut = Mesh(mesh.devices.reshape(4, 2, 8, 2, 2), ("x", "yl", "z", "yh", "c"))
    placed = (
        P(None, REP, FSDP),
        P(),
        P(FSDP, None, None),
        P(FSDP, None, None),
        P(REP, None, None),
        P(REP, None, None),
        P(),
        P(REP, None),
    )
    return jax.shard_map(
        on_device,
        mesh=cut,
        in_specs=placed,
        out_specs=(P(FSDP, None, None), P(REP, FSDP, None)),
        check_vma=False,
    )
```

```python
import jax
import jax.numpy as jnp
from jax import lax
from jax.experimental import pallas as pl
from jax.experimental.pallas import tpu as pltpu
from jax.sharding import Mesh
from jax.sharding import PartitionSpec as P

D = 2880
SLOTS = 64
COLS = 45
HALF = 24
ROWS = 64
TOK = 256
HID = 256
CAP = 3
SIDE = 4
DEPTH = 8
INNER = 16
PIECES = 5
PIECE = D // PIECES
PACKED = TOK // 4 * CAP
SIDE_ROWS = PACKED // SIDE

VMEM = pltpu.VMEM
SMEM = pltpu.SMEM
BF = jnp.bfloat16
F32 = jnp.float32

FSDP = ("x", "yl", "z")
REP = ("yh", "c")


def params(mib):
    return pltpu.CompilerParams(vmem_limit_bytes=mib * 2**20)


def in_hbm(x):
    return pltpu.with_memory_space_constraint(x, pltpu.HBM)


def nt(a, b):
    return lax.dot_general(a, b, (((1,), (1,)), ((), ())), preferred_element_type=F32)


def tn(a, b):
    return lax.dot_general(a, b, (((0,), (0,)), ((), ())), preferred_element_type=F32)


def nn(a, b):
    return lax.dot_general(a, b, (((1,), (0,)), ((), ())), preferred_element_type=F32)


def iota(shape, dim):
    return lax.broadcasted_iota(jnp.int32, shape, dim)


def invert(place_ref, slot_ref):
    def step(s, _):
        slot_ref[place_ref[s]] = s
        return 0

    lax.fori_loop(0, SLOTS, step, 0, unroll=8)


PAIRS = 12


def round_blocks(values, spread):
    size = jnp.abs(values)
    top = size
    for shift in (1, 2, 4, 8, 16):
        top = jnp.maximum(top, pltpu.roll(top, shift, 1))
    top = jnp.maximum(top, 6.0 * 2.0**-40)
    lead = top * (2.0**23 + 1.0)
    lead = jnp.abs(lead - lead * (1.0 - 2.0**-24))
    scale = jnp.where(top > lead * 1.5, lead * 0.5, lead * 0.25)
    s = nn(scale.astype(BF), spread)
    out = jnp.where(size >= s * 0.25, s * 0.5, 0.0)
    out = jnp.where(size >= s * 0.75, s, out)
    out = jnp.where(size >= s * 1.25, s * 1.5, out)
    out = jnp.where(size >= s * 1.75, s * 2.0, out)
    out = jnp.where(size >= s * 2.5, s * 3.0, out)
    out = jnp.where(size >= s * 3.5, s * 4.0, out)
    out = jnp.where(size >= s * 5.0, s * 6.0, out)
    return jnp.where(values < 0, -out, out)


def encode_kernel(
    place_hbm, master_ref, out_ref, place_ref, slot_ref, held_ref, raw_ref, sems, place_sem
):
    place_copy = pltpu.make_async_copy(place_hbm, place_ref, place_sem)
    place_copy.start()
    copies = []
    for g in range(HALF // PAIRS):
        at = g * PAIRS
        wide = min(PAIRS, COLS - HALF - at)
        for n, (start, size) in enumerate(((at, PAIRS), (HALF + at, wide))):
            part = pl.ds(start, size)
            copy = pltpu.make_async_copy(master_ref.at[part], raw_ref.at[part], sems.at[2 * g + n])
            copy.start()
            copies.append(copy)
    spread = (iota((128, 128), 0) == (iota((128, 128), 1) // 32) * 32 + 31).astype(F32).astype(BF)
    for g in range(HALF // PAIRS):
        at = g * PAIRS
        wide = min(PAIRS, COLS - HALF - at)
        copies[2 * g].wait()
        copies[2 * g + 1].wait()
        low = raw_ref[at : at + PAIRS]
        high = raw_ref[HALF + at : HALF + at + wide]
        if wide < PAIRS:
            high = jnp.concatenate([high, low[wide:]], axis=0)
        low = low.reshape(PAIRS * SLOTS, ROWS)
        high = high.reshape(PAIRS * SLOTS, ROWS)
        values = jnp.concatenate([low, high], axis=1)
        held_ref[at * SLOTS : (at + PAIRS) * SLOTS, :] = round_blocks(values, spread)

    place_copy.wait()
    invert(place_ref, slot_ref)

    def deal(o, _):
        out_ref[o] = held_ref[pl.ds(slot_ref[o], HALF, stride=SLOTS), :].astype(BF)
        return 0

    lax.fori_loop(0, SLOTS, deal, 0, unroll=8)


def encode(placement, master):
    return pl.pallas_call(
        encode_kernel,
        name="encode",
        out_shape=jax.ShapeDtypeStruct((SLOTS, HALF, 128), BF),
        in_specs=[pl.BlockSpec(memory_space=pl.ANY)] * 2,
        out_specs=pl.BlockSpec(memory_space=VMEM),
        scratch_shapes=[
            pltpu.SMEM((SLOTS,), jnp.int32),
            pltpu.SMEM((SLOTS,), jnp.int32),
            VMEM((HALF * SLOTS, 128), F32),
            VMEM((COLS, SLOTS, ROWS), F32),
            pltpu.SemaphoreType.DMA((2 * HALF // PAIRS,)),
            pltpu.SemaphoreType.DMA(()),
        ],
        compiler_params=params(16),
        cost_estimate=pl.CostEstimate(flops=1, bytes_accessed=1, transcendentals=0),
    )(placement, master)


GROUP = 16


def assemble_kernel(own_ref, across_ref, core_ref, both_ref, out_ref, held_ref):
    low = iota((HALF, 128), 1) < ROWS
    half = lax.axis_index("yh")
    core = lax.axis_index("c")
    for i in range(GROUP):
        here = (own_ref[i].astype(F32), core_ref[i].astype(F32))
        there = (across_ref[i].astype(F32), both_ref[i].astype(F32))
        for h in range(2):
            mine, other = (jnp.where(half == h, a, b) for a, b in zip(here, there))
            first = jnp.where(core == 0, mine, other)
            second = jnp.where(core == 0, other, mine)
            upper = jnp.where(low, first, pltpu.roll(second, ROWS, 1))
            lower = jnp.where(low, pltpu.roll(first, ROWS, 1), second)
            lanes = slice(128 * h, 128 * h + 128)
            held_ref[COLS * i : COLS * i + HALF, lanes] = upper
            held_ref[COLS * i + HALF : COLS * (i + 1), lanes] = lower[: COLS - HALF]
    out_ref[...] = held_ref[...].astype(BF)


def assemble(own, across, core, both):
    rows = GROUP * COLS
    return pl.pallas_call(
        assemble_kernel,
        name="assemble",
        grid=(SLOTS // GROUP,),
        out_shape=jax.ShapeDtypeStruct((D, 4 * ROWS), BF),
        in_specs=[pl.BlockSpec((GROUP, HALF, 128), lambda g: (g, 0, 0))] * 4,
        out_specs=pl.BlockSpec((rows, 4 * ROWS), lambda g: (g, 0)),
        scratch_shapes=[VMEM((rows, 4 * ROWS), F32)],
        compiler_params=params(24),
        cost_estimate=pl.CostEstimate(flops=10**9, bytes_accessed=4 * 10**6, transcendentals=0),
    )(own, across, core, both)


def choices(routes_ref):
    which = iota((8, TOK), 0)
    chosen = jnp.zeros((8, TOK), F32)
    for k in range(4):
        chosen = jnp.where(which == routes_ref[k : k + 1, :], 1.0, chosen)
    return chosen


def turns(chosen):
    earlier = (
        ((iota((TOK, TOK), 0) // 4) == (iota((TOK, TOK), 1) // 4))
        & (iota((TOK, TOK), 0) < iota((TOK, TOK), 1))
    ).astype(F32).astype(BF)
    return jnp.where(chosen > 0, nn(chosen.astype(BF), earlier), -1.0)


def row_of(table, expert):
    return jnp.sum(jnp.where(iota((8, TOK), 0) == expert, table, 0.0), axis=0, keepdims=True)


def expert_kernel(
    place_ref,
    hidden_ref,
    routes_ref,
    gain_ref,
    gate_up_hbm,
    down_hbm,
    out0_ref,
    out1_ref,
    out2_ref,
    out3_ref,
    normed_ref,
    rows_ref,
    slot_ref,
    gate_up_ref,
    down_ref,
    sems,
):
    copies = []
    for m, (hbm, ref) in enumerate(((gate_up_hbm, gate_up_ref), (down_hbm, down_ref))):
        for n in range(PIECES):
            part = pl.ds(n * PIECE, PIECE)
            copy = pltpu.make_async_copy(hbm.at[part], ref.at[part], sems.at[m * PIECES + n])
            copy.start()
            copies.append(copy)
    invert(place_ref, slot_ref)
    side = lax.axis_index("x")
    owner = side * INNER + lax.axis_index("yl") * DEPTH + lax.axis_index("z")
    mine = slot_ref[owner] // DEPTH

    my_turn = row_of(turns(choices(routes_ref)), mine)
    packed = iota((PACKED, TOK), 0)
    block = ((packed // SIDE_ROWS) ^ side) * INNER + (packed % SIDE_ROWS) // CAP
    pack = (
        ((iota((PACKED, TOK), 1) // 4) == block)
        & (jnp.broadcast_to(my_turn, (PACKED, TOK)) == (packed % CAP).astype(F32))
    ).astype(F32).astype(BF)

    total = jnp.zeros((1, TOK), F32)
    for n in range(PIECES):
        part = hidden_ref[n * PIECE : (n + 1) * PIECE, :].astype(F32)
        total = total + jnp.sum(part * part, axis=0, keepdims=True)
    factor = lax.rsqrt(total * (1.0 / D) + 1e-05)
    ones = jnp.ones((128, TOK), BF)
    for at in range(0, D, 128):
        size = min(128, D - at)
        gain = gain_ref[:, at : at + size].astype(F32)
        diagonal = jnp.where(
            iota((size, size), 0) == iota((size, size), 1), jnp.broadcast_to(gain, (size, size)), 0.0
        ).astype(BF)
        spread = nn(diagonal, ones[:size])
        part = hidden_ref[at : at + size, :].astype(F32)
        normed_ref[at : at + size, :] = (part * factor * spread).astype(BF)

    projected = jnp.zeros((TOK, 2 * HID), F32)
    for n in range(PIECES):
        copies[n].wait()
        part = slice(n * PIECE, (n + 1) * PIECE)
        projected = projected + tn(normed_ref[part, :], gate_up_ref[part, :])
    gate = projected[:, :HID]
    up = projected[:, HID:]
    activated = (gate * jax.nn.sigmoid(1.702 * gate) * (up + 1.0)).astype(BF)
    activated = nn(pack, activated).astype(BF)
    for n in range(PIECES):
        copies[PIECES + n].wait()
    for at in range(0, D, 640):
        size = min(640, D - at)
        terms = nt(activated, down_ref[at : at + size, :]).astype(BF)
        for d, out_ref in enumerate((out0_ref, out1_ref, out2_ref, out3_ref)):
            out_ref[:, at : at + size] = terms[d * SIDE_ROWS : (d + 1) * SIDE_ROWS]

    own = (iota((8, TOK), 1) == iota((8, TOK), 0) + owner * 4).astype(F32).astype(BF)
    for at in range(0, D, 640):
        size = min(640, D - at)
        rows_ref[:, at : at + size] = nt(own, hidden_ref[at : at + size, :])[:4]


def expert_terms(placement, hidden, routes, gain, gate_up, down):
    whole = pl.BlockSpec(memory_space=VMEM)
    out = jax.ShapeDtypeStruct((SIDE_ROWS, D), BF)
    return pl.pallas_call(
        expert_kernel,
        name="expert_terms",
        out_shape=(out,) * 4
        + (jax.ShapeDtypeStruct((D, TOK), BF), jax.ShapeDtypeStruct((4, D), F32)),
        in_specs=[
            pl.BlockSpec(memory_space=SMEM),
            whole,
            whole,
            whole,
            pl.BlockSpec(memory_space=pl.ANY),
            pl.BlockSpec(memory_space=pl.ANY),
        ],
        out_specs=(whole,) * 6,
        scratch_shapes=[
            pltpu.SMEM((SLOTS,), jnp.int32),
            VMEM((D, 2 * HID), BF),
            VMEM((D, HID), BF),
            pltpu.SemaphoreType.DMA((2 * PIECES,)),
        ],
        compiler_params=params(32),
        cost_estimate=pl.CostEstimate(flops=3 * 10**9, bytes_accessed=8 * 10**6, transcendentals=0),
    )(placement, hidden, routes, gain, gate_up, down)


def weigh_kernel(place_ref, routes_ref, router_ref, normed_ref, out_ref, slot_ref, held_ref):
    invert(place_ref, slot_ref)
    side = lax.axis_index("x")
    inner = lax.axis_index("yl") * DEPTH + lax.axis_index("z")

    rep = lax.axis_index("yh") * 2 + lax.axis_index("c")
    logits = jnp.zeros((8, TOK), F32)
    for d in range(4):
        start = pl.multiple_of((rep ^ d) * 720, 720)
        logits = logits + nn(router_ref[d], normed_ref[pl.ds(start, 720), :])
    chosen = choices(routes_ref)
    powered = jnp.where(chosen > 0, jnp.exp(logits), 0.0)
    weights = powered / jnp.sum(powered, axis=0, keepdims=True)
    turn = turns(chosen)

    packed = iota((SIDE_ROWS, TOK), 0)
    inside = (iota((SIDE_ROWS, TOK), 1) // 4) == side * INNER + packed // CAP
    parts = []
    for d in range(SIDE):
        expert = slot_ref[(side ^ d) * INNER + inner] // DEPTH
        here = jnp.broadcast_to(row_of(turn, expert), (SIDE_ROWS, TOK)) == (packed % CAP).astype(F32)
        weight = jnp.broadcast_to(row_of(weights, expert), (SIDE_ROWS, TOK))
        parts.append(jnp.where(inside & here, weight, 0.0))
    held_ref[...] = jnp.transpose(jnp.concatenate(parts, axis=0))
    local = 4 * INNER
    table = held_ref[pl.ds(pl.multiple_of(side * local, local), local), :]
    upper = table.astype(BF)
    out_ref[:local, :] = upper
    out_ref[local:, :] = (table - upper.astype(F32)).astype(BF)


def weigh(placement, routes, router, normed):
    return pl.pallas_call(
        weigh_kernel,
        name="weigh",
        out_shape=jax.ShapeDtypeStruct((8 * INNER, PACKED), BF),
        in_specs=[pl.BlockSpec(memory_space=SMEM)] + [pl.BlockSpec(memory_space=VMEM)] * 3,
        out_specs=pl.BlockSpec(memory_space=VMEM),
        scratch_shapes=[pltpu.SMEM((SLOTS,), jnp.int32), VMEM((TOK, PACKED), F32)],
        compiler_params=params(16),
        cost_estimate=pl.CostEstimate(flops=1, bytes_accessed=1, transcendentals=0),
    )(placement, routes, router, normed)


def merge_kernel(table_ref, got0_ref, got1_ref, got2_ref, got3_ref, out_ref):
    local = 4 * INNER
    for at in range(0, D, 640):
        size = min(640, D - at)
        got = jnp.concatenate(
            [ref[:, at : at + size] for ref in (got0_ref, got1_ref, got2_ref, got3_ref)], axis=0
        )
        both = nn(table_ref[...], got)
        part = (both[:local] + both[local:]).astype(BF)
        for n in range(INNER):
            out_ref[n, :, at : at + size] = part[4 * n : 4 * n + 4]


def merge_side(table, got):
    return pl.pallas_call(
        merge_kernel,
        name="merge_side",
        out_shape=jax.ShapeDtypeStruct((INNER, 4, D), BF),
        in_specs=[pl.BlockSpec(memory_space=VMEM)] * 5,
        out_specs=pl.BlockSpec(memory_space=VMEM),
        compiler_params=params(16),
        cost_estimate=pl.CostEstimate(flops=4 * 10**9, bytes_accessed=1, transcendentals=0),
    )(table, *got)


def on_device(
    master, placement, resident_gate_up, resident_down, hidden, routes, norm_gain, router
):
    chunks = encode(in_hbm(placement), in_hbm(jnp.transpose(master, (2, 0, 1))))
    chosen = routes[0].T
    norm_gain, chunks = lax.optimization_barrier((norm_gain, chunks))
    *terms, normed, rows = expert_terms(
        placement,
        hidden[0].T,
        chosen,
        norm_gain[None],
        in_hbm(resident_gate_up[0]),
        in_hbm(resident_down[0].T),
    )
    got = [terms[0]]
    chunks, *terms = lax.optimization_barrier((chunks, *terms))
    for d in range(1, SIDE):
        got.append(lax.ppermute(terms[d], "x", [(x, x ^ d) for x in range(SIDE)]))
    chunks = lax.all_to_all(chunks, FSDP, split_axis=0, concat_axis=0, tiled=True)
    router_rows, *_ = lax.optimization_barrier((router.T, *got[1:]))
    routers = [router_rows]
    for d in range(1, 4):
        routers.append(lax.ppermute(router_rows, REP, [(r, r ^ d) for r in range(4)]))
    table = weigh(placement, chosen, jnp.stack(routers), normed)
    terms = merge_side(table, got)
    chunks, terms = lax.optimization_barrier((chunks, terms))

    across = lax.ppermute(chunks, "yh", ((0, 1), (1, 0)))
    core = lax.ppermute(chunks, "c", ((0, 1), (1, 0)))
    both = lax.ppermute(across, "c", ((0, 1), (1, 0)))
    terms = lax.all_to_all(terms, ("yl", "z"), split_axis=0, concat_axis=0, tiled=True)
    refreshed = assemble(chunks, across, core, both).T
    terms, refreshed = lax.optimization_barrier((terms, refreshed))
    decoded = (rows + jnp.sum(terms.astype(F32), axis=0)).astype(BF)
    return (refreshed[None], decoded[None])


def solution(mesh):
    cut = Mesh(mesh.devices.reshape(4, 2, 8, 2, 2), ("x", "yl", "z", "yh", "c"))
    placed = (
        P(None, REP, FSDP),
        P(),
        P(FSDP, None, None),
        P(FSDP, None, None),
        P(REP, None, None),
        P(REP, None, None),
        P(),
        P(REP, None),
    )
    return jax.shard_map(
        on_device,
        mesh=cut,
        in_specs=placed,
        out_specs=(P(FSDP, None, None), P(REP, FSDP, None)),
        check_vma=False,
    )
```

```python
import jax
import jax.numpy as jnp
from jax import lax
from jax.experimental import pallas as pl
from jax.experimental.pallas import tpu as pltpu
from jax.sharding import Mesh
from jax.sharding import PartitionSpec as P

D = 2880
SLOTS = 64
COLS = 45
HALF = 24
ROWS = 64
TOK = 256
HID = 256
CAP = 3
SIDE = 4
DEPTH = 8
INNER = 16
PIECES = 5
PIECE = D // PIECES
PACKED = TOK // 4 * CAP
SIDE_ROWS = PACKED // SIDE

VMEM = pltpu.VMEM
SMEM = pltpu.SMEM
BF = jnp.bfloat16
F32 = jnp.float32

FSDP = ("x", "yl", "z")
REP = ("yh", "c")


def params(mib):
    return pltpu.CompilerParams(vmem_limit_bytes=mib * 2**20)


def in_hbm(x):
    return pltpu.with_memory_space_constraint(x, pltpu.HBM)


def nt(a, b):
    return lax.dot_general(a, b, (((1,), (1,)), ((), ())), preferred_element_type=F32)


def tn(a, b):
    return lax.dot_general(a, b, (((0,), (0,)), ((), ())), preferred_element_type=F32)


def nn(a, b):
    return lax.dot_general(a, b, (((1,), (0,)), ((), ())), preferred_element_type=F32)


def iota(shape, dim):
    return lax.broadcasted_iota(jnp.int32, shape, dim)


def invert(place_ref, slot_ref):
    def step(s, _):
        slot_ref[place_ref[s]] = s
        return 0

    lax.fori_loop(0, SLOTS, step, 0, unroll=8)


PAIRS = 12


def round_blocks(values, spread):
    size = jnp.abs(values)
    top = size
    for shift in (1, 2, 4, 8, 16):
        top = jnp.maximum(top, pltpu.roll(top, shift, 1))
    top = jnp.maximum(top, 6.0 * 2.0**-40)
    lead = top * (2.0**23 + 1.0)
    lead = jnp.abs(lead - lead * (1.0 - 2.0**-24))
    scale = jnp.where(top > lead * 1.5, lead * 0.5, lead * 0.25)
    s = nn(scale.astype(BF), spread)
    out = jnp.where(size >= s * 0.25, s * 0.5, 0.0)
    out = jnp.where(size >= s * 0.75, s, out)
    out = jnp.where(size >= s * 1.25, s * 1.5, out)
    out = jnp.where(size >= s * 1.75, s * 2.0, out)
    out = jnp.where(size >= s * 2.5, s * 3.0, out)
    out = jnp.where(size >= s * 3.5, s * 4.0, out)
    out = jnp.where(size >= s * 5.0, s * 6.0, out)
    return jnp.where(values < 0, -out, out)


def fetch(pairs, sems):
    copies = []
    for n, (source, target) in enumerate(pairs):
        copy = pltpu.make_async_copy(source, target, sems.at[n])
        copy.start()
        copies.append(copy)
    return copies


def master_parts():
    for at in range(0, HALF, PAIRS):
        yield at, PAIRS
        yield HALF + at, min(PAIRS, COLS - HALF - at)


def encode(copies, raw_ref, held_ref):
    spread = (iota((128, 128), 0) == (iota((128, 128), 1) // 32) * 32 + 31).astype(F32).astype(BF)
    for g in range(HALF // PAIRS):
        at = g * PAIRS
        wide = min(PAIRS, COLS - HALF - at)
        copies[2 * g].wait()
        copies[2 * g + 1].wait()
        low = raw_ref[at : at + PAIRS]
        high = raw_ref[HALF + at : HALF + at + wide]
        if wide < PAIRS:
            high = jnp.concatenate([high, low[wide:]], axis=0)
        low = low.reshape(PAIRS * SLOTS, ROWS)
        high = high.reshape(PAIRS * SLOTS, ROWS)
        values = jnp.concatenate([low, high], axis=1)
        held_ref[at * SLOTS : (at + PAIRS) * SLOTS, :] = round_blocks(values, spread)


GROUP = 16


def assemble_kernel(own_ref, across_ref, core_ref, both_ref, out_ref, held_ref):
    low = iota((HALF, 128), 1) < ROWS
    half = lax.axis_index("yh")
    core = lax.axis_index("c")
    for i in range(GROUP):
        here = (own_ref[i].astype(F32), core_ref[i].astype(F32))
        there = (across_ref[i].astype(F32), both_ref[i].astype(F32))
        for h in range(2):
            mine, other = (jnp.where(half == h, a, b) for a, b in zip(here, there))
            first = jnp.where(core == 0, mine, other)
            second = jnp.where(core == 0, other, mine)
            upper = jnp.where(low, first, pltpu.roll(second, ROWS, 1))
            lower = jnp.where(low, pltpu.roll(first, ROWS, 1), second)
            lanes = slice(128 * h, 128 * h + 128)
            held_ref[COLS * i : COLS * i + HALF, lanes] = upper
            held_ref[COLS * i + HALF : COLS * (i + 1), lanes] = lower[: COLS - HALF]
    out_ref[...] = held_ref[...].astype(BF)


def assemble(own, across, core, both):
    rows = GROUP * COLS
    return pl.pallas_call(
        assemble_kernel,
        name="assemble",
        grid=(SLOTS // GROUP,),
        out_shape=jax.ShapeDtypeStruct((D, 4 * ROWS), BF),
        in_specs=[pl.BlockSpec((GROUP, HALF, 128), lambda g: (g, 0, 0))] * 4,
        out_specs=pl.BlockSpec((rows, 4 * ROWS), lambda g: (g, 0)),
        scratch_shapes=[VMEM((rows, 4 * ROWS), F32)],
        compiler_params=params(24),
        cost_estimate=pl.CostEstimate(flops=10**9, bytes_accessed=4 * 10**6, transcendentals=0),
    )(own, across, core, both)


def choices(routes_ref):
    which = iota((8, TOK), 0)
    chosen = jnp.zeros((8, TOK), F32)
    for k in range(4):
        chosen = jnp.where(which == routes_ref[k : k + 1, :], 1.0, chosen)
    return chosen


def turns(chosen):
    earlier = (
        ((iota((TOK, TOK), 0) // 4) == (iota((TOK, TOK), 1) // 4))
        & (iota((TOK, TOK), 0) < iota((TOK, TOK), 1))
    ).astype(F32).astype(BF)
    return jnp.where(chosen > 0, nn(chosen.astype(BF), earlier), -1.0)


def row_of(table, expert):
    return jnp.sum(jnp.where(iota((8, TOK), 0) == expert, table, 0.0), axis=0, keepdims=True)


def prepare_kernel(
    place_hbm,
    master_hbm,
    hidden_hbm,
    routes_hbm,
    gain_hbm,
    gate_up_hbm,
    down_hbm,
    chunks_ref,
    out0_ref,
    out1_ref,
    out2_ref,
    out3_ref,
    normed_ref,
    rows_ref,
    place_ref,
    slot_ref,
    routes_ref,
    gain_ref,
    raw_ref,
    held_ref,
    hidden_ref,
    gate_up_ref,
    down_ref,
    sems,
):
    pieces = [pl.ds(n * PIECE, PIECE) for n in range(PIECES)]
    masters = [pl.ds(*part) for part in master_parts()]
    copies = fetch(
        [(master_hbm.at[part], raw_ref.at[part]) for part in masters]
        + [(place_hbm, place_ref), (routes_hbm, routes_ref), (gain_hbm, gain_ref)]
        + [(hidden_hbm.at[part], hidden_ref.at[part]) for part in pieces]
        + [(gate_up_hbm.at[part], gate_up_ref.at[part]) for part in pieces]
        + [(down_hbm.at[part], down_ref.at[part]) for part in pieces],
        sems,
    )
    encode(copies, raw_ref, held_ref)
    for copy in copies[len(masters) :]:
        copy.wait()
    invert(place_ref, slot_ref)

    def deal(o, _):
        chunks_ref[o] = held_ref[pl.ds(slot_ref[o], HALF, stride=SLOTS), :].astype(BF)
        return 0

    lax.fori_loop(0, SLOTS, deal, 0, unroll=8)

    side = lax.axis_index("x")
    owner = side * INNER + lax.axis_index("yl") * DEPTH + lax.axis_index("z")
    mine = slot_ref[owner] // DEPTH

    my_turn = row_of(turns(choices(routes_ref)), mine)
    packed = iota((PACKED, TOK), 0)
    block = ((packed // SIDE_ROWS) ^ side) * INNER + (packed % SIDE_ROWS) // CAP
    pack = (
        ((iota((PACKED, TOK), 1) // 4) == block)
        & (jnp.broadcast_to(my_turn, (PACKED, TOK)) == (packed % CAP).astype(F32))
    ).astype(F32).astype(BF)

    total = jnp.zeros((1, TOK), F32)
    for n in range(PIECES):
        part = hidden_ref[n * PIECE : (n + 1) * PIECE, :].astype(F32)
        total = total + jnp.sum(part * part, axis=0, keepdims=True)
    factor = lax.rsqrt(total * (1.0 / D) + 1e-05)
    ones = jnp.ones((128, TOK), BF)
    for at in range(0, D, 128):
        size = min(128, D - at)
        gain = gain_ref[at : at + size].astype(F32)
        diagonal = jnp.where(
            iota((size, size), 0) == iota((size, size), 1), jnp.broadcast_to(gain, (size, size)), 0.0
        ).astype(BF)
        spread = nn(diagonal, ones[:size])
        part = hidden_ref[at : at + size, :].astype(F32)
        normed_ref[at : at + size, :] = (part * factor * spread).astype(BF)

    projected = jnp.zeros((TOK, 2 * HID), F32)
    for n in range(PIECES):
        part = slice(n * PIECE, (n + 1) * PIECE)
        projected = projected + tn(normed_ref[part, :], gate_up_ref[part, :])
    gate = projected[:, :HID]
    up = projected[:, HID:]
    activated = (gate * jax.nn.sigmoid(1.702 * gate) * (up + 1.0)).astype(BF)
    activated = nn(pack, activated).astype(BF)
    for at in range(0, D, 640):
        size = min(640, D - at)
        terms = nt(activated, down_ref[at : at + size, :]).astype(BF)
        for d, out_ref in enumerate((out0_ref, out1_ref, out2_ref, out3_ref)):
            out_ref[:, at : at + size] = terms[d * SIDE_ROWS : (d + 1) * SIDE_ROWS]

    own = (iota((8, TOK), 1) == iota((8, TOK), 0) + owner * 4).astype(F32).astype(BF)
    for at in range(0, D, 640):
        size = min(640, D - at)
        rows_ref[:, at : at + size] = nt(own, hidden_ref[at : at + size, :])[:4]


def prepare(placement, master, hidden, routes, gain, gate_up, down):
    whole = pl.BlockSpec(memory_space=VMEM)
    apart = pl.BlockSpec(memory_space=pl.ANY)
    out = jax.ShapeDtypeStruct((SIDE_ROWS, D), BF)
    return pl.pallas_call(
        prepare_kernel,
        name="prepare",
        out_shape=(jax.ShapeDtypeStruct((SLOTS, HALF, 128), BF),)
        + (out,) * 4
        + (jax.ShapeDtypeStruct((D, TOK), BF), jax.ShapeDtypeStruct((4, D), F32)),
        in_specs=[apart] * 7,
        out_specs=(whole,) * 7,
        scratch_shapes=[
            pltpu.SMEM((SLOTS,), jnp.int32),
            pltpu.SMEM((SLOTS,), jnp.int32),
            VMEM((4, TOK), jnp.int32),
            VMEM((D,), BF),
            VMEM((COLS, SLOTS, ROWS), F32),
            VMEM((HALF * SLOTS, 128), F32),
            VMEM((D, TOK), BF),
            VMEM((D, 2 * HID), BF),
            VMEM((D, HID), BF),
            pltpu.SemaphoreType.DMA((2 * HALF // PAIRS + 3 + 3 * PIECES,)),
        ],
        compiler_params=params(32),
        cost_estimate=pl.CostEstimate(flops=8 * 10**9, bytes_accessed=10**7, transcendentals=0),
    )(
        *map(in_hbm, (placement, master, hidden, routes, gain, gate_up, down))
    )


def weigh_kernel(
    place_ref, routes_ref, near_ref, far_ref, normed_ref, out_ref, slot_ref, held_ref
):
    invert(place_ref, slot_ref)
    side = lax.axis_index("x")
    inner = lax.axis_index("yl") * DEPTH + lax.axis_index("z")

    rep = lax.axis_index("yh") * 2 + lax.axis_index("c")
    logits = jnp.zeros((8, TOK), F32)
    for d in range(4):
        start = pl.multiple_of((rep ^ d) * 720, 720)
        router = (near_ref if d < 2 else far_ref)[d % 2]
        logits = logits + nn(router, normed_ref[pl.ds(start, 720), :])
    chosen = choices(routes_ref)
    powered = jnp.where(chosen > 0, jnp.exp(logits), 0.0)
    weights = powered / jnp.sum(powered, axis=0, keepdims=True)
    turn = turns(chosen)

    packed = iota((SIDE_ROWS, TOK), 0)
    inside = (iota((SIDE_ROWS, TOK), 1) // 4) == side * INNER + packed // CAP
    parts = []
    for d in range(SIDE):
        expert = slot_ref[(side ^ d) * INNER + inner] // DEPTH
        here = jnp.broadcast_to(row_of(turn, expert), (SIDE_ROWS, TOK)) == (packed % CAP).astype(F32)
        weight = jnp.broadcast_to(row_of(weights, expert), (SIDE_ROWS, TOK))
        parts.append(jnp.where(inside & here, weight, 0.0))
    held_ref[...] = jnp.transpose(jnp.concatenate(parts, axis=0))
    local = 4 * INNER
    table = held_ref[pl.ds(pl.multiple_of(side * local, local), local), :]
    upper = table.astype(BF)
    out_ref[:local, :] = upper
    out_ref[local:, :] = (table - upper.astype(F32)).astype(BF)


def weigh(placement, routes, near, far, normed):
    return pl.pallas_call(
        weigh_kernel,
        name="weigh",
        out_shape=jax.ShapeDtypeStruct((8 * INNER, PACKED), BF),
        in_specs=[pl.BlockSpec(memory_space=SMEM)] + [pl.BlockSpec(memory_space=VMEM)] * 4,
        out_specs=pl.BlockSpec(memory_space=VMEM),
        scratch_shapes=[pltpu.SMEM((SLOTS,), jnp.int32), VMEM((TOK, PACKED), F32)],
        compiler_params=params(16),
        cost_estimate=pl.CostEstimate(flops=1, bytes_accessed=1, transcendentals=0),
    )(placement, routes, near, far, normed)


def merge_kernel(table_ref, got0_ref, got1_ref, got2_ref, got3_ref, out_ref):
    local = 4 * INNER
    for at in range(0, D, 640):
        size = min(640, D - at)
        got = jnp.concatenate(
            [ref[:, at : at + size] for ref in (got0_ref, got1_ref, got2_ref, got3_ref)], axis=0
        )
        both = nn(table_ref[...], got)
        part = (both[:local] + both[local:]).astype(BF)
        for n in range(INNER):
            out_ref[n, :, at : at + size] = part[4 * n : 4 * n + 4]


def merge_side(table, got):
    return pl.pallas_call(
        merge_kernel,
        name="merge_side",
        out_shape=jax.ShapeDtypeStruct((INNER, 4, D), BF),
        in_specs=[pl.BlockSpec(memory_space=VMEM)] * 5,
        out_specs=pl.BlockSpec(memory_space=VMEM),
        compiler_params=params(16),
        cost_estimate=pl.CostEstimate(flops=4 * 10**9, bytes_accessed=1, transcendentals=0),
    )(table, *got)


def finish_kernel(got_ref, rows_ref, out_ref):
    total = rows_ref[...]
    for n in range(INNER):
        total = total + got_ref[n].astype(F32)
    out_ref[...] = total.astype(BF)


def finish(got, rows):
    whole = pl.BlockSpec(memory_space=VMEM)
    return pl.pallas_call(
        finish_kernel,
        name="finish",
        out_shape=jax.ShapeDtypeStruct((4, D), BF),
        in_specs=[whole] * 2,
        out_specs=whole,
        compiler_params=params(16),
        cost_estimate=pl.CostEstimate(flops=10**6, bytes_accessed=10**6, transcendentals=0),
    )(got, rows)


def on_device(
    master, placement, resident_gate_up, resident_down, hidden, routes, norm_gain, router
):
    swap = ((0, 1), (1, 0))
    router_rows = router.T
    router_core = lax.ppermute(router_rows, "c", swap)
    chosen = routes[0].T
    chunks, *terms, normed, rows = prepare(
        placement,
        jnp.transpose(master, (2, 0, 1)),
        hidden[0].T,
        chosen,
        norm_gain,
        resident_gate_up[0],
        resident_down[0].T,
    )
    chunks, router_core, *terms = lax.optimization_barrier((chunks, router_core, *terms))
    got = [in_hbm(terms[0])]
    for d in range(1, SIDE):
        got.append(lax.ppermute(terms[d], "x", [(x, x ^ d) for x in range(SIDE)]))
    chunks = lax.all_to_all(chunks, FSDP, split_axis=0, concat_axis=0, tiled=True)

    router_core, *_ = lax.optimization_barrier((router_core, *got[1:]))
    near = jnp.stack([router_rows, router_core])
    far = lax.ppermute(near, "yh", swap)
    table = weigh(placement, chosen, near, far, normed)
    terms = merge_side(table, got)
    chunks, terms = lax.optimization_barrier((chunks, terms))

    core = lax.ppermute(chunks, "c", swap)
    across = lax.ppermute(chunks, "yh", swap)
    both = lax.ppermute(across, "c", swap)
    terms = lax.all_to_all(terms, ("yl", "z"), split_axis=0, concat_axis=0, tiled=True)
    refreshed = assemble(chunks, across, core, both).T
    terms, refreshed = lax.optimization_barrier((terms, refreshed))
    decoded = finish(terms, rows)
    return (refreshed[None], decoded[None])


def solution(mesh):
    cut = Mesh(mesh.devices.reshape(4, 2, 8, 2, 2), ("x", "yl", "z", "yh", "c"))
    placed = (
        P(None, REP, FSDP),
        P(),
        P(FSDP, None, None),
        P(FSDP, None, None),
        P(REP, None, None),
        P(REP, None, None),
        P(),
        P(REP, None),
    )
    return jax.shard_map(
        on_device,
        mesh=cut,
        in_specs=placed,
        out_specs=(P(FSDP, None, None), P(REP, FSDP, None)),
        check_vma=False,
    )
```

```python
import jax
import jax.numpy as jnp
from jax import lax
from jax.experimental import pallas as pl
from jax.experimental.pallas import tpu as pltpu
from jax.sharding import Mesh
from jax.sharding import PartitionSpec as P

D = 2880
SLOTS = 64
COLS = 45
HALF = 24
ROWS = 64
TOK = 256
HID = 256
CAP = 3
SIDE = 4
DEPTH = 8
INNER = 16
PIECES = 5
PIECE = D // PIECES
PACKED = TOK // 4 * CAP
SIDE_ROWS = PACKED // SIDE

VMEM = pltpu.VMEM
SMEM = pltpu.SMEM
BF = jnp.bfloat16
F32 = jnp.float32

FSDP = ("x", "yl", "z")
REP = ("yh", "c")


def params(mib):
    return pltpu.CompilerParams(vmem_limit_bytes=mib * 2**20)


def in_hbm(x):
    return pltpu.with_memory_space_constraint(x, pltpu.HBM)


def nt(a, b):
    return lax.dot_general(a, b, (((1,), (1,)), ((), ())), preferred_element_type=F32)


def tn(a, b):
    return lax.dot_general(a, b, (((0,), (0,)), ((), ())), preferred_element_type=F32)


def nn(a, b):
    return lax.dot_general(a, b, (((1,), (0,)), ((), ())), preferred_element_type=F32)


def iota(shape, dim):
    return lax.broadcasted_iota(jnp.int32, shape, dim)


def invert(place_ref, slot_ref):
    def step(s, _):
        slot_ref[place_ref[s]] = s
        return 0

    lax.fori_loop(0, SLOTS, step, 0, unroll=8)


PAIRS = 12


def round_blocks(values, spread):
    size = jnp.abs(values)
    top = size
    for shift in (1, 2, 4, 8, 16):
        top = jnp.maximum(top, pltpu.roll(top, shift, 1))
    top = jnp.maximum(top, 6.0 * 2.0**-40)
    lead = top * (2.0**23 + 1.0)
    lead = jnp.abs(lead - lead * (1.0 - 2.0**-24))
    scale = jnp.where(top > lead * 1.5, lead * 0.5, lead * 0.25)
    s = nn(scale.astype(BF), spread)
    out = jnp.where(size >= s * 0.25, s * 0.5, 0.0)
    out = jnp.where(size >= s * 0.75, s, out)
    out = jnp.where(size >= s * 1.25, s * 1.5, out)
    out = jnp.where(size >= s * 1.75, s * 2.0, out)
    out = jnp.where(size >= s * 2.5, s * 3.0, out)
    out = jnp.where(size >= s * 3.5, s * 4.0, out)
    out = jnp.where(size >= s * 5.0, s * 6.0, out)
    return jnp.where(values < 0, -out, out)


def fetch(pairs, sems):
    copies = []
    for n, (source, target) in enumerate(pairs):
        copy = pltpu.make_async_copy(source, target, sems.at[n])
        copy.start()
        copies.append(copy)
    return copies


def master_parts():
    for at in range(0, HALF, PAIRS):
        yield at, PAIRS
        yield HALF + at, min(PAIRS, COLS - HALF - at)


def encode(copies, raw_ref, held_ref):
    spread = (iota((128, 128), 0) == (iota((128, 128), 1) // 32) * 32 + 31).astype(F32).astype(BF)
    for g in range(HALF // PAIRS):
        at = g * PAIRS
        wide = min(PAIRS, COLS - HALF - at)
        copies[2 * g].wait()
        copies[2 * g + 1].wait()
        low = raw_ref[at : at + PAIRS]
        high = raw_ref[HALF + at : HALF + at + wide]
        if wide < PAIRS:
            high = jnp.concatenate([high, low[wide:]], axis=0)
        low = low.reshape(PAIRS * SLOTS, ROWS)
        high = high.reshape(PAIRS * SLOTS, ROWS)
        values = jnp.concatenate([low, high], axis=1)
        held_ref[at * SLOTS : (at + PAIRS) * SLOTS, :] = round_blocks(values, spread)


GROUP = 16


def assemble_kernel(own_ref, across_ref, core_ref, both_ref, out_hbm, held_ref, out_ref, sems):
    low = iota((HALF, 128), 1) < ROWS
    half = lax.axis_index("yh")
    core = lax.axis_index("c")
    rows = GROUP * COLS
    copies = []
    for g in range(SLOTS // GROUP):
        for i in range(GROUP):
            n = g * GROUP + i
            here = (own_ref[n].astype(F32), core_ref[n].astype(F32))
            there = (across_ref[n].astype(F32), both_ref[n].astype(F32))
            for h in range(2):
                mine, other = (jnp.where(half == h, a, b) for a, b in zip(here, there))
                first = jnp.where(core == 0, mine, other)
                second = jnp.where(core == 0, other, mine)
                upper = jnp.where(low, first, pltpu.roll(second, ROWS, 1))
                lower = jnp.where(low, pltpu.roll(first, ROWS, 1), second)
                lanes = slice(128 * h, 128 * h + 128)
                held_ref[COLS * i : COLS * i + HALF, lanes] = upper
                held_ref[COLS * i + HALF : COLS * (i + 1), lanes] = lower[: COLS - HALF]
        part = pl.ds(g * rows, rows)
        out_ref[part, :] = held_ref[...].astype(BF)
        copy = pltpu.make_async_copy(out_ref.at[part], out_hbm.at[part], sems.at[g])
        copy.start()
        copies.append(copy)
    for copy in copies:
        copy.wait()


def assemble(own, across, core, both):
    rows = GROUP * COLS
    return pl.pallas_call(
        assemble_kernel,
        name="assemble",
        out_shape=jax.ShapeDtypeStruct((D, 4 * ROWS), BF),
        in_specs=[pl.BlockSpec(memory_space=VMEM)] * 4,
        out_specs=pl.BlockSpec(memory_space=pl.ANY),
        scratch_shapes=[
            VMEM((rows, 4 * ROWS), F32),
            VMEM((D, 4 * ROWS), BF),
            pltpu.SemaphoreType.DMA((SLOTS // GROUP,)),
        ],
        compiler_params=params(24),
        cost_estimate=pl.CostEstimate(flops=10**9, bytes_accessed=4 * 10**6, transcendentals=0),
    )(own, across, core, both)


def choices(routes_ref):
    which = iota((8, TOK), 0)
    chosen = jnp.zeros((8, TOK), F32)
    for k in range(4):
        chosen = jnp.where(which == routes_ref[k : k + 1, :], 1.0, chosen)
    return chosen


def turns(chosen):
    earlier = (
        ((iota((TOK, TOK), 0) // 4) == (iota((TOK, TOK), 1) // 4))
        & (iota((TOK, TOK), 0) < iota((TOK, TOK), 1))
    ).astype(F32).astype(BF)
    return jnp.where(chosen > 0, nn(chosen.astype(BF), earlier), -1.0)


def row_of(table, expert):
    return jnp.sum(jnp.where(iota((8, TOK), 0) == expert, table, 0.0), axis=0, keepdims=True)


def prepare_kernel(
    place_hbm,
    master_hbm,
    hidden_hbm,
    routes_hbm,
    gain_hbm,
    gate_up_hbm,
    down_hbm,
    chunks_ref,
    out0_ref,
    out1_ref,
    out2_ref,
    out3_ref,
    normed_ref,
    rows_ref,
    place_ref,
    slot_ref,
    routes_ref,
    gain_ref,
    raw_ref,
    held_ref,
    hidden_ref,
    gate_up_ref,
    down_ref,
    sems,
):
    pieces = [pl.ds(n * PIECE, PIECE) for n in range(PIECES)]
    masters = [pl.ds(*part) for part in master_parts()]
    copies = fetch(
        [(master_hbm.at[part], raw_ref.at[part]) for part in masters]
        + [(place_hbm, place_ref), (routes_hbm, routes_ref), (gain_hbm, gain_ref)]
        + [(hidden_hbm.at[part], hidden_ref.at[part]) for part in pieces]
        + [(gate_up_hbm.at[part], gate_up_ref.at[part]) for part in pieces]
        + [(down_hbm.at[part], down_ref.at[part]) for part in pieces],
        sems,
    )
    encode(copies, raw_ref, held_ref)
    for copy in copies[len(masters) :]:
        copy.wait()
    invert(place_ref, slot_ref)

    def deal(o, _):
        chunks_ref[o] = held_ref[pl.ds(slot_ref[o], HALF, stride=SLOTS), :].astype(BF)
        return 0

    lax.fori_loop(0, SLOTS, deal, 0, unroll=8)

    side = lax.axis_index("x")
    owner = side * INNER + lax.axis_index("yl") * DEPTH + lax.axis_index("z")
    mine = slot_ref[owner] // DEPTH

    my_turn = row_of(turns(choices(routes_ref)), mine)
    packed = iota((PACKED, TOK), 0)
    block = ((packed // SIDE_ROWS) ^ side) * INNER + (packed % SIDE_ROWS) // CAP
    pack = (
        ((iota((PACKED, TOK), 1) // 4) == block)
        & (jnp.broadcast_to(my_turn, (PACKED, TOK)) == (packed % CAP).astype(F32))
    ).astype(F32).astype(BF)

    total = jnp.zeros((1, TOK), F32)
    for n in range(PIECES):
        part = hidden_ref[n * PIECE : (n + 1) * PIECE, :].astype(F32)
        total = total + jnp.sum(part * part, axis=0, keepdims=True)
    factor = lax.rsqrt(total * (1.0 / D) + 1e-05)
    ones = jnp.ones((128, TOK), BF)
    for at in range(0, D, 128):
        size = min(128, D - at)
        gain = gain_ref[at : at + size].astype(F32)
        diagonal = jnp.where(
            iota((size, size), 0) == iota((size, size), 1), jnp.broadcast_to(gain, (size, size)), 0.0
        ).astype(BF)
        spread = nn(diagonal, ones[:size])
        part = hidden_ref[at : at + size, :].astype(F32)
        normed_ref[at : at + size, :] = (part * factor * spread).astype(BF)

    projected = jnp.zeros((TOK, 2 * HID), F32)
    for n in range(PIECES):
        part = slice(n * PIECE, (n + 1) * PIECE)
        projected = projected + tn(normed_ref[part, :], gate_up_ref[part, :])
    gate = projected[:, :HID]
    up = projected[:, HID:]
    activated = (gate * jax.nn.sigmoid(1.702 * gate) * (up + 1.0)).astype(BF)
    activated = nn(pack, activated).astype(BF)
    for at in range(0, D, 640):
        size = min(640, D - at)
        terms = nt(activated, down_ref[at : at + size, :]).astype(BF)
        for d, out_ref in enumerate((out0_ref, out1_ref, out2_ref, out3_ref)):
            out_ref[:, at : at + size] = terms[d * SIDE_ROWS : (d + 1) * SIDE_ROWS]

    own = (iota((8, TOK), 1) == iota((8, TOK), 0) + owner * 4).astype(F32).astype(BF)
    for at in range(0, D, 640):
        size = min(640, D - at)
        rows_ref[:, at : at + size] = nt(own, hidden_ref[at : at + size, :])[:4]


def prepare(placement, master, hidden, routes, gain, gate_up, down):
    whole = pl.BlockSpec(memory_space=VMEM)
    apart = pl.BlockSpec(memory_space=pl.ANY)
    out = jax.ShapeDtypeStruct((SIDE_ROWS, D), BF)
    return pl.pallas_call(
        prepare_kernel,
        name="prepare",
        out_shape=(jax.ShapeDtypeStruct((SLOTS, HALF, 128), BF),)
        + (out,) * 4
        + (jax.ShapeDtypeStruct((D, TOK), BF), jax.ShapeDtypeStruct((4, D), F32)),
        in_specs=[apart] * 7,
        out_specs=(whole,) * 7,
        scratch_shapes=[
            pltpu.SMEM((SLOTS,), jnp.int32),
            pltpu.SMEM((SLOTS,), jnp.int32),
            VMEM((4, TOK), jnp.int32),
            VMEM((D,), BF),
            VMEM((COLS, SLOTS, ROWS), F32),
            VMEM((HALF * SLOTS, 128), F32),
            VMEM((D, TOK), BF),
            VMEM((D, 2 * HID), BF),
            VMEM((D, HID), BF),
            pltpu.SemaphoreType.DMA((2 * HALF // PAIRS + 3 + 3 * PIECES,)),
        ],
        compiler_params=params(32),
        cost_estimate=pl.CostEstimate(flops=8 * 10**9, bytes_accessed=10**7, transcendentals=0),
    )(
        *map(in_hbm, (placement, master, hidden, routes, gain, gate_up, down))
    )


def weigh_kernel(
    place_ref, routes_ref, near_ref, far_ref, normed_ref, out_ref, slot_ref, held_ref
):
    invert(place_ref, slot_ref)
    side = lax.axis_index("x")
    inner = lax.axis_index("yl") * DEPTH + lax.axis_index("z")

    rep = lax.axis_index("yh") * 2 + lax.axis_index("c")
    logits = jnp.zeros((8, TOK), F32)
    for d in range(4):
        start = pl.multiple_of((rep ^ d) * 720, 720)
        router = (near_ref if d < 2 else far_ref)[d % 2]
        logits = logits + nn(router, normed_ref[pl.ds(start, 720), :])
    chosen = choices(routes_ref)
    powered = jnp.where(chosen > 0, jnp.exp(logits), 0.0)
    weights = powered / jnp.sum(powered, axis=0, keepdims=True)
    turn = turns(chosen)

    packed = iota((SIDE_ROWS, TOK), 0)
    inside = (iota((SIDE_ROWS, TOK), 1) // 4) == side * INNER + packed // CAP
    parts = []
    for d in range(SIDE):
        expert = slot_ref[(side ^ d) * INNER + inner] // DEPTH
        here = jnp.broadcast_to(row_of(turn, expert), (SIDE_ROWS, TOK)) == (packed % CAP).astype(F32)
        weight = jnp.broadcast_to(row_of(weights, expert), (SIDE_ROWS, TOK))
        parts.append(jnp.where(inside & here, weight, 0.0))
    held_ref[...] = jnp.transpose(jnp.concatenate(parts, axis=0))
    local = 4 * INNER
    table = held_ref[pl.ds(pl.multiple_of(side * local, local), local), :]
    upper = table.astype(BF)
    out_ref[:local, :] = upper
    out_ref[local:, :] = (table - upper.astype(F32)).astype(BF)


def weigh(placement, routes, near, far, normed):
    return pl.pallas_call(
        weigh_kernel,
        name="weigh",
        out_shape=jax.ShapeDtypeStruct((8 * INNER, PACKED), BF),
        in_specs=[pl.BlockSpec(memory_space=SMEM)] + [pl.BlockSpec(memory_space=VMEM)] * 4,
        out_specs=pl.BlockSpec(memory_space=VMEM),
        scratch_shapes=[pltpu.SMEM((SLOTS,), jnp.int32), VMEM((TOK, PACKED), F32)],
        compiler_params=params(16),
        cost_estimate=pl.CostEstimate(flops=1, bytes_accessed=1, transcendentals=0),
    )(placement, routes, near, far, normed)


def merge_kernel(table_ref, got0_ref, got1_ref, got2_ref, got3_ref, out_ref):
    local = 4 * INNER
    for at in range(0, D, 640):
        size = min(640, D - at)
        got = jnp.concatenate(
            [ref[:, at : at + size] for ref in (got0_ref, got1_ref, got2_ref, got3_ref)], axis=0
        )
        both = nn(table_ref[...], got)
        part = (both[:local] + both[local:]).astype(BF)
        for n in range(INNER):
            out_ref[n, :, at : at + size] = part[4 * n : 4 * n + 4]


def merge_side(table, got):
    return pl.pallas_call(
        merge_kernel,
        name="merge_side",
        out_shape=jax.ShapeDtypeStruct((INNER, 4, D), BF),
        in_specs=[pl.BlockSpec(memory_space=VMEM)] * 5,
        out_specs=pl.BlockSpec(memory_space=VMEM),
        compiler_params=params(16),
        cost_estimate=pl.CostEstimate(flops=4 * 10**9, bytes_accessed=1, transcendentals=0),
    )(table, *got)


def finish_kernel(got_ref, rows_ref, out_ref):
    total = rows_ref[...]
    for n in range(INNER):
        total = total + got_ref[n].astype(F32)
    out_ref[...] = total.astype(BF)


def finish(got, rows):
    whole = pl.BlockSpec(memory_space=VMEM)
    return pl.pallas_call(
        finish_kernel,
        name="finish",
        out_shape=jax.ShapeDtypeStruct((4, D), BF),
        in_specs=[whole] * 2,
        out_specs=whole,
        compiler_params=params(16),
        cost_estimate=pl.CostEstimate(flops=10**6, bytes_accessed=10**6, transcendentals=0),
    )(got, rows)


def on_device(
    master, placement, resident_gate_up, resident_down, hidden, routes, norm_gain, router
):
    swap = ((0, 1), (1, 0))
    router_rows = router.T
    router_core = lax.ppermute(router_rows, "c", swap)
    chosen = routes[0].T
    chunks, *terms, normed, rows = prepare(
        placement,
        jnp.transpose(master, (2, 0, 1)),
        hidden[0].T,
        chosen,
        norm_gain,
        resident_gate_up[0],
        resident_down[0].T,
    )
    chunks, router_core, *terms[1:] = lax.optimization_barrier((chunks, router_core, *terms[1:]))
    got = [terms[0]]
    for d in range(1, SIDE):
        got.append(lax.ppermute(terms[d], "x", [(x, x ^ d) for x in range(SIDE)]))
    chunks = lax.all_to_all(chunks, FSDP, split_axis=0, concat_axis=0, tiled=True)

    router_core, _ = lax.optimization_barrier((router_core, got[2]))
    near = jnp.stack([router_rows, router_core])
    far = lax.ppermute(near, "yh", swap)
    table = weigh(placement, chosen, near, far, normed)
    terms = merge_side(table, got)
    chunks, terms = lax.optimization_barrier((chunks, terms))

    core = lax.ppermute(chunks, "c", swap)
    across = lax.ppermute(chunks, "yh", swap)
    both = lax.ppermute(across, "c", swap)
    terms = lax.all_to_all(terms, ("yl", "z"), split_axis=0, concat_axis=0, tiled=True)
    refreshed = assemble(chunks, across, core, both).T
    terms, refreshed = lax.optimization_barrier((terms, refreshed))
    decoded = finish(terms, rows)
    return (refreshed[None], decoded[None])


def solution(mesh):
    cut = Mesh(mesh.devices.reshape(4, 2, 8, 2, 2), ("x", "yl", "z", "yh", "c"))
    placed = (
        P(None, REP, FSDP),
        P(),
        P(FSDP, None, None),
        P(FSDP, None, None),
        P(REP, None, None),
        P(REP, None, None),
        P(),
        P(REP, None),
    )
    return jax.shard_map(
        on_device,
        mesh=cut,
        in_specs=placed,
        out_specs=(P(FSDP, None, None), P(REP, FSDP, None)),
        check_vma=False,
    )
```

```python
import jax
import jax.numpy as jnp
from jax import lax
from jax.experimental import pallas as pl
from jax.experimental.pallas import tpu as pltpu
from jax.sharding import Mesh
from jax.sharding import PartitionSpec as P

D = 2880
SLOTS = 64
COLS = 45
HALF = 24
ROWS = 64
TOK = 256
HID = 256
CAP = 3
SIDE = 4
DEPTH = 8
INNER = 16
PIECES = 5
PIECE = D // PIECES
PACKED = TOK // 4 * CAP
SIDE_ROWS = PACKED // SIDE

VMEM = pltpu.VMEM
SMEM = pltpu.SMEM
BF = jnp.bfloat16
F32 = jnp.float32

FSDP = ("x", "yl", "z")
REP = ("yh", "c")


def params(mib):
    return pltpu.CompilerParams(vmem_limit_bytes=mib * 2**20)


def in_hbm(x):
    return pltpu.with_memory_space_constraint(x, pltpu.HBM)


def nt(a, b):
    return lax.dot_general(a, b, (((1,), (1,)), ((), ())), preferred_element_type=F32)


def tn(a, b):
    return lax.dot_general(a, b, (((0,), (0,)), ((), ())), preferred_element_type=F32)


def nn(a, b):
    return lax.dot_general(a, b, (((1,), (0,)), ((), ())), preferred_element_type=F32)


def iota(shape, dim):
    return lax.broadcasted_iota(jnp.int32, shape, dim)


def invert(place_ref, slot_ref):
    def step(s, _):
        slot_ref[place_ref[s]] = s
        return 0

    lax.fori_loop(0, SLOTS, step, 0, unroll=8)


PAIRS = 12
STRIDE = 72


def round_blocks(values, spread):
    size = jnp.abs(values)
    top = size
    for shift in (1, 2, 4, 8, 16):
        top = jnp.maximum(top, pltpu.roll(top, shift, 1))
    top = jnp.maximum(top, 6.0 * 2.0**-40)
    lead = top * (2.0**23 + 1.0)
    lead = jnp.abs(lead - lead * (1.0 - 2.0**-24))
    scale = jnp.where(top > lead * 1.5, lead * 0.5, lead * 0.25)
    s = nn(scale.astype(BF), spread)
    out = jnp.where(size >= s * 0.25, s * 0.5, 0.0)
    out = jnp.where(size >= s * 0.75, s, out)
    out = jnp.where(size >= s * 1.25, s * 1.5, out)
    out = jnp.where(size >= s * 1.75, s * 2.0, out)
    out = jnp.where(size >= s * 2.5, s * 3.0, out)
    out = jnp.where(size >= s * 3.5, s * 4.0, out)
    out = jnp.where(size >= s * 5.0, s * 6.0, out)
    return jnp.where(values < 0, -out, out)


def fetch(pairs, sems):
    copies = []
    for n, (source, target) in enumerate(pairs):
        copy = pltpu.make_async_copy(source, target, sems.at[n])
        copy.start()
        copies.append(copy)
    return copies


def master_parts():
    for at in range(0, HALF, PAIRS):
        yield at, PAIRS
        yield HALF + at, min(PAIRS, COLS - HALF - at)


def encode(copies, raw_ref, held_ref):
    spread = (iota((128, 128), 0) == (iota((128, 128), 1) // 32) * 32 + 31).astype(F32).astype(BF)
    for g in range(HALF // PAIRS):
        at = g * PAIRS
        wide = min(PAIRS, COLS - HALF - at)
        copies[2 * g].wait()
        copies[2 * g + 1].wait()
        low = raw_ref[at : at + PAIRS]
        high = raw_ref[HALF + at : HALF + at + wide]
        if wide < PAIRS:
            high = jnp.concatenate([high, low[wide:]], axis=0)
        low = low.reshape(PAIRS * SLOTS, ROWS)
        high = high.reshape(PAIRS * SLOTS, ROWS)
        values = jnp.concatenate([low, high], axis=1)
        decoded = round_blocks(values, spread)
        for k in range(PAIRS):
            start = (at + k) * STRIDE
            held_ref[start : start + SLOTS, :] = decoded[k * SLOTS : (k + 1) * SLOTS]


GROUP = 16


def assemble_kernel(own_ref, across_ref, core_ref, both_ref, out_hbm, held_ref, out_ref, sems):
    low = iota((HALF, 128), 1) < ROWS
    half = lax.axis_index("yh")
    core = lax.axis_index("c")
    rows = GROUP * COLS
    copies = []
    for g in range(SLOTS // GROUP):
        for i in range(GROUP):
            n = g * GROUP + i
            here = (own_ref[n].astype(F32), core_ref[n].astype(F32))
            there = (across_ref[n].astype(F32), both_ref[n].astype(F32))
            for h in range(2):
                mine, other = (jnp.where(half == h, a, b) for a, b in zip(here, there))
                first = jnp.where(core == 0, mine, other)
                second = jnp.where(core == 0, other, mine)
                upper = jnp.where(low, first, pltpu.roll(second, ROWS, 1))
                lower = jnp.where(low, pltpu.roll(first, ROWS, 1), second)
                lanes = slice(128 * h, 128 * h + 128)
                held_ref[COLS * i : COLS * i + HALF, lanes] = upper
                held_ref[COLS * i + HALF : COLS * (i + 1), lanes] = lower[: COLS - HALF]
        part = pl.ds(g * rows, rows)
        out_ref[part, :] = held_ref[...].astype(BF)
        copy = pltpu.make_async_copy(out_ref.at[part], out_hbm.at[part], sems.at[g])
        copy.start()
        copies.append(copy)
    for copy in copies:
        copy.wait()


def assemble(own, across, core, both):
    rows = GROUP * COLS
    return pl.pallas_call(
        assemble_kernel,
        name="assemble",
        out_shape=jax.ShapeDtypeStruct((D, 4 * ROWS), BF),
        in_specs=[pl.BlockSpec(memory_space=VMEM)] * 4,
        out_specs=pl.BlockSpec(memory_space=pl.ANY),
        scratch_shapes=[
            VMEM((rows, 4 * ROWS), F32),
            VMEM((D, 4 * ROWS), BF),
            pltpu.SemaphoreType.DMA((SLOTS // GROUP,)),
        ],
        compiler_params=params(24),
        cost_estimate=pl.CostEstimate(flops=10**9, bytes_accessed=4 * 10**6, transcendentals=0),
    )(own, across, core, both)


def choices(routes_ref):
    which = iota((8, TOK), 0)
    chosen = jnp.zeros((8, TOK), F32)
    for k in range(4):
        chosen = jnp.where(which == routes_ref[k : k + 1, :], 1.0, chosen)
    return chosen


def turns(chosen):
    earlier = (
        ((iota((TOK, TOK), 0) // 4) == (iota((TOK, TOK), 1) // 4))
        & (iota((TOK, TOK), 0) < iota((TOK, TOK), 1))
    ).astype(F32).astype(BF)
    return jnp.where(chosen > 0, nn(chosen.astype(BF), earlier), -1.0)


def row_of(table, expert):
    return jnp.sum(jnp.where(iota((8, TOK), 0) == expert, table, 0.0), axis=0, keepdims=True)


def norm_into(normed_ref, hidden_ref, gain_ref):
    total = jnp.zeros((1, TOK), F32)
    for n in range(PIECES):
        part = hidden_ref[n * PIECE : (n + 1) * PIECE, :].astype(F32)
        total = total + jnp.sum(part * part, axis=0, keepdims=True)
    factor = lax.rsqrt(total * (1.0 / D) + 1e-05)
    for at in range(0, D, 128):
        size = min(128, D - at)
        gain = gain_ref[at : at + size].astype(F32)
        spread = jnp.transpose(jnp.broadcast_to(gain, (128, size)))
        spread = jnp.concatenate([spread, spread], axis=1)
        part = hidden_ref[at : at + size, :].astype(F32)
        normed_ref[at : at + size, :] = (part * factor * spread).astype(BF)


def prepare_kernel(
    place_hbm,
    master_hbm,
    hidden_hbm,
    routes_hbm,
    gain_hbm,
    gate_up_hbm,
    down_hbm,
    chunks_ref,
    out0_ref,
    out1_ref,
    out2_ref,
    out3_ref,
    place_ref,
    slot_ref,
    routes_ref,
    gain_ref,
    raw_ref,
    held_ref,
    hidden_ref,
    gate_up_ref,
    down_ref,
    normed_ref,
    sems,
):
    pieces = [pl.ds(n * PIECE, PIECE) for n in range(PIECES)]
    masters = [pl.ds(*part) for part in master_parts()]
    copies = fetch(
        [(master_hbm.at[part], raw_ref.at[part]) for part in masters]
        + [(place_hbm, place_ref), (routes_hbm, routes_ref), (gain_hbm, gain_ref)]
        + [(hidden_hbm.at[part], hidden_ref.at[part]) for part in pieces]
        + [(gate_up_hbm.at[part], gate_up_ref.at[part]) for part in pieces]
        + [(down_hbm.at[part], down_ref.at[part]) for part in pieces],
        sems,
    )
    encode(copies, raw_ref, held_ref)
    for copy in copies[len(masters) :]:
        copy.wait()
    invert(place_ref, slot_ref)

    def deal(o, _):
        chunks_ref[o] = held_ref[pl.ds(slot_ref[o], HALF, stride=STRIDE), :].astype(BF)
        return 0

    lax.fori_loop(0, SLOTS, deal, 0, unroll=8)

    side = lax.axis_index("x")
    owner = side * INNER + lax.axis_index("yl") * DEPTH + lax.axis_index("z")
    mine = slot_ref[owner] // DEPTH

    my_turn = row_of(turns(choices(routes_ref)), mine)
    packed = iota((PACKED, TOK), 0)
    block = ((packed // SIDE_ROWS) ^ side) * INNER + (packed % SIDE_ROWS) // CAP
    pack = (
        ((iota((PACKED, TOK), 1) // 4) == block)
        & (jnp.broadcast_to(my_turn, (PACKED, TOK)) == (packed % CAP).astype(F32))
    ).astype(F32).astype(BF)

    norm_into(normed_ref, hidden_ref, gain_ref)
    projected = jnp.zeros((TOK, 2 * HID), F32)
    for n in range(PIECES):
        part = slice(n * PIECE, (n + 1) * PIECE)
        projected = projected + tn(normed_ref[part, :], gate_up_ref[part, :])
    gate = projected[:, :HID]
    up = projected[:, HID:]
    activated = (gate * jax.nn.sigmoid(1.702 * gate) * (up + 1.0)).astype(BF)
    activated = nn(pack, activated).astype(BF)
    for at in range(0, D, 640):
        size = min(640, D - at)
        terms = nt(activated, down_ref[at : at + size, :]).astype(BF)
        for d, out_ref in enumerate((out0_ref, out1_ref, out2_ref, out3_ref)):
            out_ref[:, at : at + size] = terms[d * SIDE_ROWS : (d + 1) * SIDE_ROWS]


def prepare(placement, master, hidden, routes, gain, gate_up, down):
    whole = pl.BlockSpec(memory_space=VMEM)
    apart = pl.BlockSpec(memory_space=pl.ANY)
    out = jax.ShapeDtypeStruct((SIDE_ROWS, D), BF)
    return pl.pallas_call(
        prepare_kernel,
        name="prepare",
        out_shape=(jax.ShapeDtypeStruct((SLOTS, HALF, 128), BF),)
        + (out,) * 4,
        in_specs=[apart] * 7,
        out_specs=(whole,) * 5,
        scratch_shapes=[
            pltpu.SMEM((SLOTS,), jnp.int32),
            pltpu.SMEM((SLOTS,), jnp.int32),
            VMEM((4, TOK), jnp.int32),
            VMEM((D,), BF),
            VMEM((COLS, SLOTS, ROWS), F32),
            VMEM((HALF * STRIDE, 128), F32),
            VMEM((D, TOK), BF),
            VMEM((D, 2 * HID), BF),
            VMEM((D, HID), BF),
            VMEM((D, TOK), BF),
            pltpu.SemaphoreType.DMA((2 * HALF // PAIRS + 3 + 3 * PIECES,)),
        ],
        compiler_params=params(32),
        cost_estimate=pl.CostEstimate(flops=8 * 10**9, bytes_accessed=10**7, transcendentals=0),
    )(
        *map(in_hbm, (placement, master, hidden, routes, gain, gate_up, down))
    )


def weigh_kernel(
    place_ref,
    routes_ref,
    near_ref,
    far_ref,
    hidden_ref,
    gain_ref,
    out_ref,
    rows_ref,
    slot_ref,
    held_ref,
    normed_ref,
):
    invert(place_ref, slot_ref)
    side = lax.axis_index("x")
    inner = lax.axis_index("yl") * DEPTH + lax.axis_index("z")

    owner = side * INNER + inner
    own = (iota((8, TOK), 1) == iota((8, TOK), 0) + owner * 4).astype(F32).astype(BF)
    for at in range(0, D, 640):
        size = min(640, D - at)
        rows_ref[:, at : at + size] = nt(own, hidden_ref[at : at + size, :])[:4]

    norm_into(normed_ref, hidden_ref, gain_ref)
    rep = lax.axis_index("yh") * 2 + lax.axis_index("c")
    logits = jnp.zeros((8, TOK), F32)
    for d in range(4):
        start = pl.multiple_of((rep ^ d) * 720, 720)
        router = (near_ref if d < 2 else far_ref)[d % 2]
        logits = logits + nn(router, normed_ref[pl.ds(start, 720), :])
    chosen = choices(routes_ref)
    powered = jnp.where(chosen > 0, jnp.exp(logits), 0.0)
    weights = powered / jnp.sum(powered, axis=0, keepdims=True)
    turn = turns(chosen)

    packed = iota((SIDE_ROWS, TOK), 0)
    inside = (iota((SIDE_ROWS, TOK), 1) // 4) == side * INNER + packed // CAP
    parts = []
    for d in range(SIDE):
        expert = slot_ref[(side ^ d) * INNER + inner] // DEPTH
        here = jnp.broadcast_to(row_of(turn, expert), (SIDE_ROWS, TOK)) == (packed % CAP).astype(F32)
        weight = jnp.broadcast_to(row_of(weights, expert), (SIDE_ROWS, TOK))
        parts.append(jnp.where(inside & here, weight, 0.0))
    held_ref[...] = jnp.transpose(jnp.concatenate(parts, axis=0))
    local = 4 * INNER
    table = held_ref[pl.ds(pl.multiple_of(side * local, local), local), :]
    upper = table.astype(BF)
    out_ref[:local, :] = upper
    out_ref[local:, :] = (table - upper.astype(F32)).astype(BF)


def weigh(placement, routes, near, far, hidden, gain):
    return pl.pallas_call(
        weigh_kernel,
        name="weigh",
        out_shape=(
            jax.ShapeDtypeStruct((8 * INNER, PACKED), BF),
            jax.ShapeDtypeStruct((4, D), F32),
        ),
        in_specs=[pl.BlockSpec(memory_space=SMEM)] + [pl.BlockSpec(memory_space=VMEM)] * 5,
        out_specs=(pl.BlockSpec(memory_space=VMEM),) * 2,
        scratch_shapes=[
            pltpu.SMEM((SLOTS,), jnp.int32),
            VMEM((TOK, PACKED), F32),
            VMEM((D, TOK), BF),
        ],
        compiler_params=params(16),
        cost_estimate=pl.CostEstimate(flops=1, bytes_accessed=1, transcendentals=0),
    )(placement, routes, near, far, hidden, gain)


def merge_kernel(table_ref, got0_ref, got1_ref, got2_ref, got3_ref, out_ref):
    local = 4 * INNER
    for at in range(0, D, 640):
        size = min(640, D - at)
        got = jnp.concatenate(
            [ref[:, at : at + size] for ref in (got0_ref, got1_ref, got2_ref, got3_ref)], axis=0
        )
        both = nn(table_ref[...], got)
        part = (both[:local] + both[local:]).astype(BF)
        for n in range(INNER):
            out_ref[n, :, at : at + size] = part[4 * n : 4 * n + 4]


def merge_side(table, got):
    return pl.pallas_call(
        merge_kernel,
        name="merge_side",
        out_shape=jax.ShapeDtypeStruct((INNER, 4, D), BF),
        in_specs=[pl.BlockSpec(memory_space=VMEM)] * 5,
        out_specs=pl.BlockSpec(memory_space=VMEM),
        compiler_params=params(16),
        cost_estimate=pl.CostEstimate(flops=4 * 10**9, bytes_accessed=1, transcendentals=0),
    )(table, *got)


def finish_kernel(got_ref, rows_ref, out_ref):
    total = rows_ref[...]
    for n in range(INNER):
        total = total + got_ref[n].astype(F32)
    out_ref[...] = total.astype(BF)


def finish(got, rows):
    whole = pl.BlockSpec(memory_space=VMEM)
    return pl.pallas_call(
        finish_kernel,
        name="finish",
        out_shape=jax.ShapeDtypeStruct((4, D), BF),
        in_specs=[whole] * 2,
        out_specs=whole,
        compiler_params=params(16),
        cost_estimate=pl.CostEstimate(flops=10**6, bytes_accessed=10**6, transcendentals=0),
    )(got, rows)


def on_device(
    master, placement, resident_gate_up, resident_down, hidden, routes, norm_gain, router
):
    swap = ((0, 1), (1, 0))
    router_rows = router.T
    router_core = lax.ppermute(router_rows, "c", swap)
    chosen = routes[0].T
    chunks, *terms = prepare(
        placement,
        jnp.transpose(master, (2, 0, 1)),
        hidden[0].T,
        chosen,
        norm_gain,
        resident_gate_up[0],
        resident_down[0].T,
    )
    chunks, router_core, *terms[1:] = lax.optimization_barrier((chunks, router_core, *terms[1:]))
    got = [terms[0]]
    for d in range(1, SIDE):
        got.append(lax.ppermute(terms[d], "x", [(x, x ^ d) for x in range(SIDE)]))
    chunks = lax.all_to_all(chunks, FSDP, split_axis=0, concat_axis=0, tiled=True)

    router_core, _ = lax.optimization_barrier((router_core, got[2]))
    near = jnp.stack([router_rows, router_core])
    far = lax.ppermute(near, "yh", swap)
    table, rows = weigh(placement, chosen, near, far, hidden[0].T, norm_gain)
    terms = merge_side(table, got)
    chunks, terms = lax.optimization_barrier((chunks, terms))

    core = lax.ppermute(chunks, "c", swap)
    across = lax.ppermute(chunks, "yh", swap)
    both = lax.ppermute(across, "c", swap)
    terms = lax.all_to_all(terms, ("yl", "z"), split_axis=0, concat_axis=0, tiled=True)
    refreshed = assemble(chunks, across, core, both).T
    terms, refreshed = lax.optimization_barrier((terms, refreshed))
    decoded = finish(terms, rows)
    return (refreshed[None], decoded[None])


def solution(mesh):
    cut = Mesh(mesh.devices.reshape(4, 2, 8, 2, 2), ("x", "yl", "z", "yh", "c"))
    placed = (
        P(None, REP, FSDP),
        P(),
        P(FSDP, None, None),
        P(FSDP, None, None),
        P(REP, None, None),
        P(REP, None, None),
        P(),
        P(REP, None),
    )
    return jax.shard_map(
        on_device,
        mesh=cut,
        in_specs=placed,
        out_specs=(P(FSDP, None, None), P(REP, FSDP, None)),
        check_vma=False,
    )
```

```python
import jax
import jax.numpy as jnp
from jax import lax
from jax.experimental import pallas as pl
from jax.experimental.pallas import tpu as pltpu
from jax.sharding import Mesh
from jax.sharding import PartitionSpec as P

D = 2880
SLOTS = 64
COLS = 45
HALF = 24
ROWS = 64
TOK = 256
HID = 256
CAP = 3
SIDE = 4
DEPTH = 8
INNER = 16
PIECES = 5
PIECE = D // PIECES
PACKED = TOK // 4 * CAP
SIDE_ROWS = PACKED // SIDE

VMEM = pltpu.VMEM
SMEM = pltpu.SMEM
BF = jnp.bfloat16
F32 = jnp.float32

FSDP = ("x", "yl", "z")
REP = ("yh", "c")


def params(mib):
    return pltpu.CompilerParams(vmem_limit_bytes=mib * 2**20)


def in_hbm(x):
    return pltpu.with_memory_space_constraint(x, pltpu.HBM)


def nt(a, b):
    return lax.dot_general(a, b, (((1,), (1,)), ((), ())), preferred_element_type=F32)


def tn(a, b):
    return lax.dot_general(a, b, (((0,), (0,)), ((), ())), preferred_element_type=F32)


def nn(a, b):
    return lax.dot_general(a, b, (((1,), (0,)), ((), ())), preferred_element_type=F32)


def iota(shape, dim):
    return lax.broadcasted_iota(jnp.int32, shape, dim)


def invert(place_ref, slot_ref):
    def step(s, _):
        slot_ref[place_ref[s]] = s
        return 0

    lax.fori_loop(0, SLOTS, step, 0, unroll=8)


PAIRS = 12
STRIDE = 72


def round_blocks(values, spread):
    size = jnp.abs(values)
    top = size
    for shift in (1, 2, 4, 8, 16):
        top = jnp.maximum(top, pltpu.roll(top, shift, 1))
    top = jnp.maximum(top, 6.0 * 2.0**-40)
    lead = top * (2.0**23 + 1.0)
    lead = jnp.abs(lead - lead * (1.0 - 2.0**-24))
    scale = jnp.where(top > lead * 1.5, lead * 0.5, lead * 0.25)
    s = nn(scale.astype(BF), spread)
    out = jnp.where(size >= s * 0.25, s * 0.5, 0.0)
    out = jnp.where(size >= s * 0.75, s, out)
    out = jnp.where(size >= s * 1.25, s * 1.5, out)
    out = jnp.where(size >= s * 1.75, s * 2.0, out)
    out = jnp.where(size >= s * 2.5, s * 3.0, out)
    out = jnp.where(size >= s * 3.5, s * 4.0, out)
    out = jnp.where(size >= s * 5.0, s * 6.0, out)
    return jnp.where(values < 0, -out, out)


def fetch(pairs, sems):
    copies = []
    for n, (source, target) in enumerate(pairs):
        copy = pltpu.make_async_copy(source, target, sems.at[n])
        copy.start()
        copies.append(copy)
    return copies


def master_parts():
    for at in range(0, HALF, PAIRS):
        yield at, PAIRS
        yield HALF + at, min(PAIRS, COLS - HALF - at)


def encode(copies, raw_ref, held_ref):
    spread = (iota((128, 128), 0) == (iota((128, 128), 1) // 32) * 32 + 31).astype(F32).astype(BF)
    for g in range(HALF // PAIRS):
        at = g * PAIRS
        wide = min(PAIRS, COLS - HALF - at)
        copies[2 * g].wait()
        copies[2 * g + 1].wait()
        low = raw_ref[at : at + PAIRS]
        high = raw_ref[HALF + at : HALF + at + wide]
        if wide < PAIRS:
            high = jnp.concatenate([high, low[wide:]], axis=0)
        low = low.reshape(PAIRS * SLOTS, ROWS)
        high = high.reshape(PAIRS * SLOTS, ROWS)
        values = jnp.concatenate([low, high], axis=1)
        decoded = round_blocks(values, spread)
        for k in range(PAIRS):
            start = (at + k) * STRIDE
            held_ref[start : start + SLOTS, :] = decoded[k * SLOTS : (k + 1) * SLOTS]


GROUP = 16


def assemble_kernel(own_ref, across_ref, core_ref, both_ref, out_hbm, held_ref, out_ref, sems):
    low = iota((HALF, 128), 1) < ROWS
    half = lax.axis_index("yh")
    core = lax.axis_index("c")
    rows = GROUP * COLS
    copies = []
    for g in range(SLOTS // GROUP):
        for i in range(GROUP):
            n = g * GROUP + i
            here = (own_ref[n].astype(F32), core_ref[n].astype(F32))
            there = (across_ref[n].astype(F32), both_ref[n].astype(F32))
            for h in range(2):
                mine, other = (jnp.where(half == h, a, b) for a, b in zip(here, there))
                first = jnp.where(core == 0, mine, other)
                second = jnp.where(core == 0, other, mine)
                upper = jnp.where(low, first, pltpu.roll(second, ROWS, 1))
                lower = jnp.where(low, pltpu.roll(first, ROWS, 1), second)
                lanes = slice(128 * h, 128 * h + 128)
                held_ref[COLS * i : COLS * i + HALF, lanes] = upper
                held_ref[COLS * i + HALF : COLS * (i + 1), lanes] = lower[: COLS - HALF]
        part = pl.ds(g * rows, rows)
        out_ref[part, :] = held_ref[...].astype(BF)
        copy = pltpu.make_async_copy(out_ref.at[part], out_hbm.at[part], sems.at[g])
        copy.start()
        copies.append(copy)
    for copy in copies:
        copy.wait()


def assemble(own, across, core, both):
    rows = GROUP * COLS
    return pl.pallas_call(
        assemble_kernel,
        name="assemble",
        out_shape=jax.ShapeDtypeStruct((D, 4 * ROWS), BF),
        in_specs=[pl.BlockSpec(memory_space=VMEM)] * 4,
        out_specs=pl.BlockSpec(memory_space=pl.ANY),
        scratch_shapes=[
            VMEM((rows, 4 * ROWS), F32),
            VMEM((D, 4 * ROWS), BF),
            pltpu.SemaphoreType.DMA((SLOTS // GROUP,)),
        ],
        compiler_params=params(24),
        cost_estimate=pl.CostEstimate(flops=10**9, bytes_accessed=4 * 10**6, transcendentals=0),
    )(own, across, core, both)


def choices(routes_ref):
    which = iota((8, TOK), 0)
    chosen = jnp.zeros((8, TOK), F32)
    for k in range(4):
        chosen = jnp.where(which == routes_ref[k : k + 1, :], 1.0, chosen)
    return chosen


def turns(chosen):
    earlier = (
        ((iota((TOK, TOK), 0) // 4) == (iota((TOK, TOK), 1) // 4))
        & (iota((TOK, TOK), 0) < iota((TOK, TOK), 1))
    ).astype(F32).astype(BF)
    return jnp.where(chosen > 0, nn(chosen.astype(BF), earlier), -1.0)


def row_of(table, expert):
    return jnp.sum(jnp.where(iota((8, TOK), 0) == expert, table, 0.0), axis=0, keepdims=True)


def norm_into(normed_ref, hidden_ref, gain_ref):
    total = jnp.zeros((1, TOK), F32)
    for n in range(PIECES):
        part = hidden_ref[n * PIECE : (n + 1) * PIECE, :].astype(F32)
        total = total + jnp.sum(part * part, axis=0, keepdims=True)
    factor = lax.rsqrt(total * (1.0 / D) + 1e-05)
    for at in range(0, D, 128):
        size = min(128, D - at)
        gain = gain_ref[at : at + size].astype(F32)
        spread = jnp.transpose(jnp.broadcast_to(gain, (128, size)))
        spread = jnp.concatenate([spread, spread], axis=1)
        part = hidden_ref[at : at + size, :].astype(F32)
        normed_ref[at : at + size, :] = (part * factor * spread).astype(BF)


def prepare_kernel(
    place_hbm,
    master_hbm,
    hidden_hbm,
    routes_hbm,
    gain_hbm,
    gate_up_hbm,
    down_hbm,
    chunks_ref,
    out0_ref,
    out1_ref,
    out2_ref,
    out3_ref,
    place_ref,
    slot_ref,
    routes_ref,
    gain_ref,
    raw_ref,
    held_ref,
    hidden_ref,
    gate_up_ref,
    down_ref,
    normed_ref,
    sems,
):
    pieces = [pl.ds(n * PIECE, PIECE) for n in range(PIECES)]
    masters = [pl.ds(*part) for part in master_parts()]
    copies = fetch(
        [(master_hbm.at[part], raw_ref.at[part]) for part in masters]
        + [(place_hbm, place_ref), (routes_hbm, routes_ref), (gain_hbm, gain_ref)]
        + [(hidden_hbm.at[part], hidden_ref.at[part]) for part in pieces]
        + [(gate_up_hbm.at[part], gate_up_ref.at[part]) for part in pieces]
        + [(down_hbm.at[part], down_ref.at[part]) for part in pieces],
        sems,
    )
    encode(copies, raw_ref, held_ref)
    for copy in copies[len(masters) :]:
        copy.wait()
    invert(place_ref, slot_ref)

    def deal(o, _):
        chunks_ref[o] = held_ref[pl.ds(slot_ref[o], HALF, stride=STRIDE), :].astype(BF)
        return 0

    lax.fori_loop(0, SLOTS, deal, 0, unroll=64)

    side = lax.axis_index("x")
    owner = side * INNER + lax.axis_index("yl") * DEPTH + lax.axis_index("z")
    mine = slot_ref[owner] // DEPTH

    my_turn = row_of(turns(choices(routes_ref)), mine)
    packed = iota((PACKED, TOK), 0)
    block = ((packed // SIDE_ROWS) ^ side) * INNER + (packed % SIDE_ROWS) // CAP
    pack = (
        ((iota((PACKED, TOK), 1) // 4) == block)
        & (jnp.broadcast_to(my_turn, (PACKED, TOK)) == (packed % CAP).astype(F32))
    ).astype(F32).astype(BF)

    norm_into(normed_ref, hidden_ref, gain_ref)
    projected = jnp.zeros((TOK, 2 * HID), F32)
    for n in range(PIECES):
        part = slice(n * PIECE, (n + 1) * PIECE)
        projected = projected + tn(normed_ref[part, :], gate_up_ref[part, :])
    gate = projected[:, :HID]
    up = projected[:, HID:]
    activated = (gate * jax.nn.sigmoid(1.702 * gate) * (up + 1.0)).astype(BF)
    activated = nn(pack, activated).astype(BF)
    for at in range(0, D, 640):
        size = min(640, D - at)
        terms = nt(activated, down_ref[at : at + size, :]).astype(BF)
        for d, out_ref in enumerate((out0_ref, out1_ref, out2_ref, out3_ref)):
            out_ref[:, at : at + size] = terms[d * SIDE_ROWS : (d + 1) * SIDE_ROWS]


def prepare(placement, master, hidden, routes, gain, gate_up, down):
    whole = pl.BlockSpec(memory_space=VMEM)
    apart = pl.BlockSpec(memory_space=pl.ANY)
    out = jax.ShapeDtypeStruct((SIDE_ROWS, D), BF)
    return pl.pallas_call(
        prepare_kernel,
        name="prepare",
        out_shape=(jax.ShapeDtypeStruct((SLOTS, HALF, 128), BF),)
        + (out,) * 4,
        in_specs=[apart] * 7,
        out_specs=(whole,) * 5,
        scratch_shapes=[
            pltpu.SMEM((SLOTS,), jnp.int32),
            pltpu.SMEM((SLOTS,), jnp.int32),
            VMEM((4, TOK), jnp.int32),
            VMEM((D,), BF),
            VMEM((COLS, SLOTS, ROWS), F32),
            VMEM((HALF * STRIDE, 128), F32),
            VMEM((D, TOK), BF),
            VMEM((D, 2 * HID), BF),
            VMEM((D, HID), BF),
            VMEM((D, TOK), BF),
            pltpu.SemaphoreType.DMA((2 * HALF // PAIRS + 3 + 3 * PIECES,)),
        ],
        compiler_params=params(32),
        cost_estimate=pl.CostEstimate(flops=8 * 10**9, bytes_accessed=10**7, transcendentals=0),
    )(
        *map(in_hbm, (placement, master, hidden, routes, gain, gate_up, down))
    )


def weigh_kernel(
    place_ref,
    routes_ref,
    near_ref,
    far_ref,
    hidden_ref,
    gain_ref,
    out_ref,
    rows_ref,
    slot_ref,
    held_ref,
    normed_ref,
):
    invert(place_ref, slot_ref)
    side = lax.axis_index("x")
    inner = lax.axis_index("yl") * DEPTH + lax.axis_index("z")

    owner = side * INNER + inner
    own = (iota((8, TOK), 1) == iota((8, TOK), 0) + owner * 4).astype(F32).astype(BF)
    for at in range(0, D, 640):
        size = min(640, D - at)
        rows_ref[:, at : at + size] = nt(own, hidden_ref[at : at + size, :])[:4]

    norm_into(normed_ref, hidden_ref, gain_ref)
    rep = lax.axis_index("yh") * 2 + lax.axis_index("c")
    logits = jnp.zeros((8, TOK), F32)
    for d in range(4):
        start = pl.multiple_of((rep ^ d) * 720, 720)
        router = (near_ref if d < 2 else far_ref)[d % 2]
        logits = logits + nn(router, normed_ref[pl.ds(start, 720), :])
    chosen = choices(routes_ref)
    powered = jnp.where(chosen > 0, jnp.exp(logits), 0.0)
    weights = powered / jnp.sum(powered, axis=0, keepdims=True)
    turn = turns(chosen)

    packed = iota((SIDE_ROWS, TOK), 0)
    inside = (iota((SIDE_ROWS, TOK), 1) // 4) == side * INNER + packed // CAP
    parts = []
    for d in range(SIDE):
        expert = slot_ref[(side ^ d) * INNER + inner] // DEPTH
        here = jnp.broadcast_to(row_of(turn, expert), (SIDE_ROWS, TOK)) == (packed % CAP).astype(F32)
        weight = jnp.broadcast_to(row_of(weights, expert), (SIDE_ROWS, TOK))
        parts.append(jnp.where(inside & here, weight, 0.0))
    held_ref[...] = jnp.transpose(jnp.concatenate(parts, axis=0))
    local = 4 * INNER
    table = held_ref[pl.ds(pl.multiple_of(side * local, local), local), :]
    upper = table.astype(BF)
    out_ref[:local, :] = upper
    out_ref[local:, :] = (table - upper.astype(F32)).astype(BF)


def weigh(placement, routes, near, far, hidden, gain):
    return pl.pallas_call(
        weigh_kernel,
        name="weigh",
        out_shape=(
            jax.ShapeDtypeStruct((8 * INNER, PACKED), BF),
            jax.ShapeDtypeStruct((4, D), F32),
        ),
        in_specs=[pl.BlockSpec(memory_space=SMEM)] + [pl.BlockSpec(memory_space=VMEM)] * 5,
        out_specs=(pl.BlockSpec(memory_space=VMEM),) * 2,
        scratch_shapes=[
            pltpu.SMEM((SLOTS,), jnp.int32),
            VMEM((TOK, PACKED), F32),
            VMEM((D, TOK), BF),
        ],
        compiler_params=params(16),
        cost_estimate=pl.CostEstimate(flops=1, bytes_accessed=1, transcendentals=0),
    )(placement, routes, near, far, hidden, gain)


def merge_kernel(table_ref, got0_ref, got1_ref, got2_ref, got3_ref, out_ref):
    local = 4 * INNER
    for at in range(0, D, 640):
        size = min(640, D - at)
        got = jnp.concatenate(
            [ref[:, at : at + size] for ref in (got0_ref, got1_ref, got2_ref, got3_ref)], axis=0
        )
        both = nn(table_ref[...], got)
        part = (both[:local] + both[local:]).astype(BF)
        for n in range(INNER):
            out_ref[n, :, at : at + size] = part[4 * n : 4 * n + 4]


def merge_side(table, got):
    return pl.pallas_call(
        merge_kernel,
        name="merge_side",
        out_shape=jax.ShapeDtypeStruct((INNER, 4, D), BF),
        in_specs=[pl.BlockSpec(memory_space=VMEM)] * 5,
        out_specs=pl.BlockSpec(memory_space=VMEM),
        compiler_params=params(16),
        cost_estimate=pl.CostEstimate(flops=4 * 10**9, bytes_accessed=1, transcendentals=0),
    )(table, *got)


def finish_kernel(got_ref, rows_ref, out_ref):
    total = rows_ref[...]
    for n in range(INNER):
        total = total + got_ref[n].astype(F32)
    out_ref[...] = total.astype(BF)


def finish(got, rows):
    whole = pl.BlockSpec(memory_space=VMEM)
    return pl.pallas_call(
        finish_kernel,
        name="finish",
        out_shape=jax.ShapeDtypeStruct((4, D), BF),
        in_specs=[whole] * 2,
        out_specs=whole,
        compiler_params=params(16),
        cost_estimate=pl.CostEstimate(flops=10**6, bytes_accessed=10**6, transcendentals=0),
    )(got, rows)


def on_device(
    master, placement, resident_gate_up, resident_down, hidden, routes, norm_gain, router
):
    swap = ((0, 1), (1, 0))
    router_rows = router.T
    router_core = lax.ppermute(router_rows, "c", swap)
    chosen = routes[0].T
    chunks, *terms = prepare(
        placement,
        jnp.transpose(master, (2, 0, 1)),
        hidden[0].T,
        chosen,
        norm_gain,
        resident_gate_up[0],
        resident_down[0].T,
    )
    chunks, router_core, *terms[1:] = lax.optimization_barrier((chunks, router_core, *terms[1:]))
    got = [terms[0]]
    for d in range(1, SIDE):
        got.append(lax.ppermute(terms[d], "x", [(x, x ^ d) for x in range(SIDE)]))
    chunks = lax.all_to_all(chunks, FSDP, split_axis=0, concat_axis=0, tiled=True)

    router_core, _ = lax.optimization_barrier((router_core, got[2]))
    near = jnp.stack([router_rows, router_core])
    far = lax.ppermute(near, "yh", swap)
    table, rows = weigh(placement, chosen, near, far, hidden[0].T, norm_gain)
    terms = merge_side(table, got)
    chunks, terms = lax.optimization_barrier((chunks, terms))

    core = lax.ppermute(chunks, "c", swap)
    across = lax.ppermute(chunks, "yh", swap)
    both = lax.ppermute(across, "c", swap)
    terms = lax.all_to_all(terms, ("yl", "z"), split_axis=0, concat_axis=0, tiled=True)
    refreshed = assemble(chunks, across, core, both).T
    terms, refreshed = lax.optimization_barrier((terms, refreshed))
    decoded = finish(terms, rows)
    return (refreshed[None], decoded[None])


def solution(mesh):
    cut = Mesh(mesh.devices.reshape(4, 2, 8, 2, 2), ("x", "yl", "z", "yh", "c"))
    placed = (
        P(None, REP, FSDP),
        P(),
        P(FSDP, None, None),
        P(FSDP, None, None),
        P(REP, None, None),
        P(REP, None, None),
        P(),
        P(REP, None),
    )
    return jax.shard_map(
        on_device,
        mesh=cut,
        in_specs=placed,
        out_specs=(P(FSDP, None, None), P(REP, FSDP, None)),
        check_vma=False,
    )
```
